256 devices in a mesh: dom: 64 (over x_lo, z, y), vec: 4 (over x_hi, core).
Axes of the slice: x: 4 (x_hi: 2, x_lo: 2; x = x_hi * 2 + x_lo), y: 4, z: 8, core: 2. Of those that a mesh axis runs over, the one named last changes fastest.
Arguments:
- vectors: float32 [4, 32, 2048, 1024], P(None, 'vec', 'dom'), may hold values from -6 to 6
- hoppings: float32 [2, 3, 2048, 1024], P(None, None, 'dom'), may hold values from 0.5 to 1.5
- potential: float32 [4, 2048, 1024], P(None, 'dom'), may hold values from -1 to 1
- stacking: int32 [2048, 1024], P('dom'), may hold values from 0 to 7
- interlayer: float32 [2, 8], replicated, may hold values from 0.2 to 1
- filling: float32 [1], replicated, may hold values from 0.3 to 0.7
Outputs:
- new_potential: float32 [4, 2048, 1024], P(None, 'dom')
The draws below stay inside these ranges and needn't reach their ends.
All inputs are finite; a program needn't handle non-finite values.
Results may differ from the reference program's by a relative error of at most 0.0003.
Values sent between devices are 32-bit elements; how exact they have to be, the bound alone decides.
No kernel may reach another device: no remote copies, remote signals or barrier semaphores. Data moves between devices by JAX's collectives and lax.ppermute only.
A program may use at most 128 MiB of HBM per device.

```python
import math
import jax
import jax.numpy as jnp
from jax import lax

LY = 1024
CHEB = 4
BISECT = 16
NCLS = 8
NV = 32
NX = 2048


def place_ends(drawn, own_key, smallest, high):
    place = [jax.random.randint(jax.random.fold_in(own_key, axis), (), 0, length) for axis, length in enumerate(drawn.shape)]
    longest = drawn.shape.index(max(drawn.shape))
    next_to = place[:longest] + [(place[longest] + 1) % drawn.shape[longest]] + place[longest + 1:]
    return drawn.at[tuple(place)].set(smallest).at[tuple(next_to)].set(high)


def levels(own_key, dims, pieces, least, largest):
    gain, own = 1.0, jax.random.fold_in(own_key, 6)
    for dim, shards_of in pieces:
        steps = jnp.exp(jax.random.uniform(jax.random.fold_in(own, dim), (shards_of,), jnp.float32, least / len(pieces), largest / len(pieces)))
        gain = gain * jnp.repeat(steps, dims[dim] // shards_of).reshape([-1 if axis == dim else 1 for axis in range(len(dims))])
    return gain


def normal_values(key, extent, width, most, pieces=(), kind=jnp.bfloat16):
    factor_of = levels(key, extent, pieces, -0.22, 0.18) if pieces else 1.0
    result = jax.random.normal(key, extent, jnp.float32) * width * factor_of
    return jnp.minimum(jnp.maximum(result, -most), most).astype(kind)


def setup_inputs(seed: int = 0) -> dict:
    splits = jax.random.split(jax.random.key(seed), 7)
    return {
        "vectors": normal_values(splits[0], (4, NV, NX, LY), 1.0, 6.0, ((1, 4), (2, 64)), jnp.float32),
        "hoppings": jnp.clip(1.0 + 0.1 * jax.random.normal(splits[1], (2, 3, NX, LY), jnp.float32), 0.5, 1.5),
        "potential": jnp.clip(jax.random.uniform(splits[2], (4, NX, LY), jnp.float32, -1.0, 1.0) * levels(splits[2], (4, NX, LY), ((1, 64),), -0.4, 0.0), -1.0, 1.0),
        "stacking": place_ends(jax.random.randint(splits[3], (NX, LY), 0, NCLS), jax.random.fold_in(splits[3], 1), 0, NCLS - 1).astype(jnp.int32),
        "interlayer": jnp.clip(jax.random.uniform(splits[4], (2, NCLS), jnp.float32, 0.2, 1.0), 0.2, 1.0),
        "filling": jnp.clip(jax.random.uniform(splits[5], (1,), jnp.float32, 0.3, 0.7), 0.3, 0.7),
    }


def jackson(count):
    angle = math.pi / (count + 1)
    return [((count - m + 1) * math.cos(angle * m) + math.sin(angle * m) / math.tan(angle)) / (count + 1) for m in range(count)]


def weights_at(energy, count):
    gains = jnp.array(jackson(count), dtype=jnp.float32)
    theta = jnp.arccos(energy)
    orders = jnp.arange(count).astype(jnp.float32)
    first = 1.0 - theta / math.pi
    rest = -2.0 * jnp.sin(orders * theta) / (math.pi * jnp.maximum(orders, 1.0))
    return jnp.where(orders == 0.0, first, rest) * gains


def couplings(stacking, interlayer):
    coup_aa = jnp.zeros(stacking.shape, jnp.float32)
    coup_ab = jnp.zeros(stacking.shape, jnp.float32)
    for klass in range(NCLS):
        hit = stacking == klass
        coup_aa = coup_aa + jnp.where(hit, interlayer[0, klass], 0.0)
        coup_ab = coup_ab + jnp.where(hit, interlayer[1, klass], 0.0)
    return coup_aa, coup_ab


def apply_ham(field, hoppings, coup_aa, coup_ab, potential):
    outs = []
    for layer in range(2):
        a_site = field[2 * layer]
        b_site = field[2 * layer + 1]
        t_zero, t_one, t_two = hoppings[layer, 0], hoppings[layer, 1], hoppings[layer, 2]
        h_a = -(t_zero * b_site + t_one * jnp.roll(b_site, 1, axis=1) + t_two * jnp.roll(b_site, 1, axis=0))
        h_b = -(t_zero * a_site + jnp.roll(t_one * a_site, -1, axis=1) + jnp.roll(t_two * a_site, -1, axis=0))
        outs.append((h_a, h_b))
    h_a1 = outs[0][0] + coup_aa * field[2] + coup_ab * field[3]
    h_a2 = outs[1][0] + coup_aa * field[0]
    h_b2 = outs[1][1] + coup_ab * field[0]
    total = jnp.stack([h_a1, outs[0][1], h_a2, h_b2]) + potential * field
    return total / 8.0


def reference(vectors, hoppings, potential, stacking, interlayer, filling):
    coup_aa, coup_ab = couplings(stacking, interlayer)
    start = jnp.zeros((CHEB + 1,) + potential.shape, jnp.float32)

    def one_vector(index, acc):
        rvec = lax.dynamic_index_in_dim(vectors, index, 1, keepdims=False)
        prev = rvec
        cur = apply_ham(rvec, hoppings, coup_aa, coup_ab, potential)
        terms = [rvec * rvec, rvec * cur]
        for step in range(CHEB - 1):
            nxt = 2.0 * apply_ham(cur, hoppings, coup_aa, coup_ab, potential) - prev
            prev, cur = cur, nxt
            terms.append(rvec * cur)
        return acc + jnp.stack(terms)

    summed = lax.fori_loop(0, NV, one_vector, start)
    moments = summed / float(NV)
    totals = jnp.sum(moments, axis=(1, 2, 3))
    count_m = CHEB + 1
    target = filling[0] * float(4 * NX * LY)

    def bisect(step, carry):
        low, high = carry
        mid = 0.5 * (low + high)
        count = jnp.sum(weights_at(mid, count_m) * totals)
        below = count < target
        return (jnp.where(below, mid, low), jnp.where(below, high, mid))

    low, high = lax.fori_loop(0, BISECT, bisect, (jnp.array(-1.0, jnp.float32), jnp.array(1.0, jnp.float32)))
    chem = 0.5 * (low + high)
    coeff = weights_at(chem, count_m)
    density = coeff[0] * moments[0]
    for order in range(1, count_m):
        density = density + coeff[order] * moments[order]
    charge = jnp.sum(density - 0.5, axis=0)
    near = jnp.roll(charge, 1, axis=0) + jnp.roll(charge, -1, axis=0) + jnp.roll(charge, 1, axis=1) + jnp.roll(charge, -1, axis=1)
    return 3.0 * (density - 0.5) + 0.5 * charge + 0.25 * near
```

```python
import functools
import math

import jax
import jax.numpy as jnp
from jax import lax
from jax.experimental import pallas as pl
from jax.experimental.pallas import tpu as pltpu
from jax.sharding import PartitionSpec as P

CHEB = 4
BISECT = 16
LANES = 128
SUB = 8
REC = 48
COEF = 32
F32 = jnp.float32
VMEM_LIMIT = 44 * 1024 * 1024


def jackson(count):
    angle = math.pi / (count + 1)
    return [
        ((count - m + 1) * math.cos(angle * m) + math.sin(angle * m) / math.tan(angle))
        / (count + 1)
        for m in range(count)
    ]


def lane_is(where, shape=(SUB, LANES)):
    return lax.broadcasted_iota(jnp.int32, shape, 1) == where


def from_left(here, left):
    return jnp.where(lane_is(0, here.shape), left, here)


def from_right(here, right):
    return jnp.where(lane_is(LANES - 1, here.shape), right, here)


def roll_left(x):
    return pltpu.roll(x, LANES - 1, 1)


def roll_right(x):
    return pltpu.roll(x, 1, 1)


def pick(classes, table):
    values = list(table)
    bit = 1
    while len(values) > 1:
        hit = (classes & bit) != 0
        values = [jnp.where(hit, values[i + 1], values[i]) for i in range(0, len(values), 2)]
        bit *= 2
    return values[0]


def hop_apply(a, b, a_right, b_left, a_down, b_up, coef, t2_down):
    pot = coef[8:12]
    aa, ab = coef[12:14]
    out = []
    for layer in range(2):
        t0, t1, t2, t1r = coef[4 * layer : 4 * layer + 4]
        h_a = t0 * b[layer] + t1 * b_left[layer] + t2 * b_up[layer] + pot[2 * layer] * a[layer]
        h_b = (
            t0 * a[layer]
            + t1r * a_right[layer]
            + t2_down[layer] * a_down[layer]
            + pot[2 * layer + 1] * b[layer]
        )
        out.append([h_a, h_b])
    out[0][0] = out[0][0] + aa * a[1] + ab * b[1]
    out[1][0] = out[1][0] + aa * a[0]
    out[1][1] = out[1][1] + ab * a[0]
    return [out[0][0], out[0][1], out[1][0], out[1][1]]


def pack_kernel(rows, chunks, idx, inter, vec, hop, pot, stk, long_out, short_out, extra,
                v8, h8, p8, s8, rec, sems):
    copies = []
    n = 0
    for band in range(2):
        at = pl.ds(band * (rows - SUB), SUB)
        for c in range(chunks):
            lanes = pl.ds(c * LANES, LANES)
            for src, dst in (
                (hop.at[:, at, lanes], h8.at[band, c]),
                (pot.at[:, at, lanes], p8.at[band, c]),
                (stk.at[at, lanes], s8.at[band, c]),
                (vec.at[:, at, lanes], v8.at[band, c]),
            ):
                copies.append(pltpu.make_async_copy(src, dst, sems.at[n]))
                n += 1
    for copy in copies:
        copy.start()
    for copy in copies:
        copy.wait()
    nf = vec.shape[0]
    flat = v8.reshape(2, chunks, nf * SUB, LANES)
    odd = idx[0]
    outs = []
    for band in range(2):
        for c in range(chunks):
            first = 0 if band == 0 else SUB - 4
            for r in range(4):
                for s in range(nf // SUB):
                    rec[band, c, pl.ds(r * REC + s * SUB, SUB), :] = flat[
                        band, c, pl.ds(s * SUB * SUB + first + r, SUB, stride=SUB), :
                    ]
            after = (c + 1) % chunks
            coef = []
            for layer in range(2):
                for k in range(3):
                    coef.append(h8[band, c, 3 * layer + k] * -0.25)
                    if k == 1:
                        here = h8[band, c, 3 * layer + 1]
                        there = h8[band, after, 3 * layer + 1]
                        shifted = from_right(roll_left(here), roll_left(there)) * -0.25
                coef.append(shifted)
            for s in range(4):
                coef.append(p8[band, c, s] * 0.25)
            classes = s8[band, c]
            for w in range(2):
                table = [inter[w, k] * 0.25 for k in range(inter.shape[1])]
                coef.append(pick(classes, table))
            for k, value in enumerate(coef):
                rec[band, c, pl.ds(COEF + k, 4, stride=REC), :] = value[first : first + 4]
            zero = jnp.zeros((4, LANES), F32)
            for k in range(len(coef), REC - COEF):
                rec[band, c, pl.ds(COEF + k, 4, stride=REC), :] = zero
        message = rec.at[band, :, pl.ds(band * REC, 3 * REC)]
        spare = rec.at[band, :, pl.ds((1 - band) * 3 * REC, REC)]
        away = pltpu.make_async_copy(spare, extra.at[band], sems.at[n])
        away.start()
        outs.append(away)
        n += 1

        @pl.when(odd == band)
        def _():
            pltpu.make_async_copy(message, long_out, sems.at[n]).start()

        @pl.when(odd != band)
        def _():
            pltpu.make_async_copy(message, short_out, sems.at[n]).start()

        outs.append(pltpu.make_async_copy(message, long_out, sems.at[n]))
        n += 1
    for copy in outs:
        copy.wait()


def pack(idx, inter, vec, hop, pot, stk):
    fields, rows, width = vec.shape
    chunks = width // LANES
    any_ = pl.BlockSpec(memory_space=pl.ANY)
    smem = pl.BlockSpec(memory_space=pltpu.SMEM)
    message = jax.ShapeDtypeStruct((chunks, 3 * REC, LANES), F32)
    n_in = 2 * chunks * 4
    return pl.pallas_call(
        functools.partial(pack_kernel, rows, chunks),
        out_shape=[message, message, jax.ShapeDtypeStruct((2, chunks, REC, LANES), F32)],
        in_specs=[smem, smem, any_, any_, any_, any_],
        out_specs=[any_, any_, any_],
        scratch_shapes=[
            pltpu.VMEM((2, chunks, fields, SUB, LANES), F32),
            pltpu.VMEM((2, chunks, 6, SUB, LANES), F32),
            pltpu.VMEM((2, chunks, 4, SUB, LANES), F32),
            pltpu.VMEM((2, chunks, SUB, LANES), jnp.int32),
            pltpu.VMEM((2, chunks, 4 * REC, LANES), F32),
            pltpu.SemaphoreType.DMA((n_in + 4,)),
        ],
        compiler_params=pltpu.CompilerParams(vmem_limit_bytes=VMEM_LIMIT),
        cost_estimate=pl.CostEstimate(flops=1_000_000, bytes_accessed=4_000_000, transcendentals=0),
        name="pack",
    )(idx, inter, vec, hop, pot, stk)


PAD = 8


def interior_kernel(rows, chunks, nvec, group, idx, inter, vec, hop, pot, stk, keep, send, tot,
                    x, t1, t2, hp, pt, st, ww, mom, sems):
    halves = nvec // group
    copies = []
    n = 0
    for c in range(chunks):
        lanes = pl.ds(c * LANES, LANES)
        for src, dst in (
            (hop.at[:, :, :, lanes], hp.at[:, 0:3, c, pl.ds(0, rows)]),
            (pot.at[:, :, lanes], pt.at[:, c]),
            (stk.at[:, lanes], st.at[c]),
        ):
            copies.append(pltpu.make_async_copy(src, dst, sems.at[n]))
            n += 1
    late = []
    for q in range(halves):
        part = []
        for c in range(chunks):
            lanes = pl.ds(c * LANES, LANES)
            part.append(
                pltpu.make_async_copy(
                    vec.at[:, pl.ds(q * group, group), :, lanes],
                    x.at[:, pl.ds(q * group, group), c, pl.ds(PAD, rows)],
                    sems.at[n],
                )
            )
            n += 1
        late.append(part)
    for copy in copies + [copy for part in late for copy in part]:
        copy.start()
    for copy in copies:
        copy.wait()

    groups = rows // SUB

    def prepare(g, carry):
        at = pl.ds(pl.multiple_of(g * SUB, SUB), SUB)
        for layer in range(2):
            rolled = {}
            for c in range(chunks):
                rolled[c] = roll_left(hp[layer, 1, c, at, :])
            for c in range(chunks):
                hp[layer, 3, c, at, :] = (
                    from_right(rolled[c], rolled[(c + 1) % chunks]) * -0.25
                )
            for k in range(3):
                for c in range(chunks):
                    hp[layer, k, c, at, :] = hp[layer, k, c, at, :] * -0.25
        for c in range(chunks):
            for s in range(4):
                pt[s, c, at, :] = pt[s, c, at, :] * 0.25
            classes = st[c, at, :]
            for w in range(2):
                table = [inter[w, k] * 0.25 for k in range(inter.shape[1])]
                ww[w, c, at, :] = pick(classes, table)
        return carry

    lax.fori_loop(0, groups, prepare, 0)

    def sweep(order, q, source, before, target):
        def load(ref, s, v, c, at):
            return ref[s, v, c, at, :]

        def body(g, carry):
            base = pl.multiple_of(g * SUB, SUB)
            mid = pl.ds(base + PAD, SUB)
            up = pl.ds(base + PAD - 1, SUB)
            down = pl.ds(base + PAD + 1, SUB)
            plain = pl.ds(base, SUB)
            plain_down = pl.ds(base + 1, SUB)
            vs = range(group)
            src, off = source

            def rolled(site, c, fn):
                return [fn(load(src, site, v + off, c, mid)) for v in vs]

            b_prev = [rolled(2 * l + 1, chunks - 1, roll_right) for l in range(2)]
            a_here = [rolled(2 * l, 0, roll_left) for l in range(2)]
            for c in range(chunks):
                nxt = (c + 1) % chunks
                a_next = [rolled(2 * l, nxt, roll_left) for l in range(2)]
                b_here = [rolled(2 * l + 1, c, roll_right) for l in range(2)]
                coef = []
                for layer in range(2):
                    for k in range(4):
                        coef.append(hp[layer, k, c, plain, :])
                for s in range(4):
                    coef.append(pt[s, c, plain, :])
                for w in range(2):
                    coef.append(ww[w, c, plain, :])
                t2_down = [hp[layer, 2, c, plain_down, :] for layer in range(2)]
                sums = [None] * 4
                squares = [None] * 4
                for v in vs:
                    a = [load(src, 2 * l, v + off, c, mid) for l in range(2)]
                    b = [load(src, 2 * l + 1, v + off, c, mid) for l in range(2)]
                    a_down = [load(src, 2 * l, v + off, c, down) for l in range(2)]
                    b_up = [load(src, 2 * l + 1, v + off, c, up) for l in range(2)]
                    a_right = [from_right(a_here[l][v], a_next[l][v]) for l in range(2)]
                    b_left = [from_left(b_here[l][v], b_prev[l][v]) for l in range(2)]
                    new = hop_apply(a, b, a_right, b_left, a_down, b_up, coef, t2_down)
                    for s in range(4):
                        if order == 1:
                            value = new[s] * 0.5
                        else:
                            ref, shift = before
                            value = new[s] - load(ref, s, v + shift, c, mid)
                        if target is not None:
                            target[s, v, c, mid, :] = value
                        first = load(x, s, v + q * group, c, mid)
                        term = first * value
                        sums[s] = term if sums[s] is None else sums[s] + term
                        if order == 1:
                            sq = first * first
                            squares[s] = sq if squares[s] is None else squares[s] + sq
                for s in range(4):
                    if q > 0:
                        sums[s] = sums[s] + mom[order, s, c, plain, :]
                    mom[order, s, c, plain, :] = sums[s]
                    if order == 1:
                        if q > 0:
                            squares[s] = squares[s] + mom[0, s, c, plain, :]
                        mom[0, s, c, plain, :] = squares[s]
                a_here = a_next
                b_prev = b_here
            return carry

        lax.fori_loop(0, groups, body, 0)

    for q in range(halves):
        for copy in late[q]:
            copy.wait()
        start = (x, q * group)
        sweep(1, q, start, None, t1)
        sweep(2, q, (t1, 0), start, t2)
        sweep(3, q, (t2, 0), (t1, 0), t1)
        sweep(4, q, (t1, 0), (t2, 0), None)

    half = rows // 2
    core = idx[1]
    kept = pltpu.make_async_copy(
        mom.at[:, :, :, pl.ds(pl.multiple_of(core * half, SUB), half)], keep, sems.at[n]
    )
    sent = pltpu.make_async_copy(
        mom.at[:, :, :, pl.ds(pl.multiple_of((1 - core) * half, SUB), half)], send, sems.at[n + 1]
    )
    kept.start()
    sent.start()

    def add_up(g, carry):
        base = pl.multiple_of(g * SUB, SUB)
        row = lax.broadcasted_iota(jnp.int32, (SUB, LANES), 0) + base
        inside = (row >= 2) & (row < rows - 2)
        result = []
        for m in range(CHEB + 1):
            acc = None
            for s in range(4):
                for c in range(chunks):
                    value = mom[m, s, c, pl.ds(base, SUB), :]
                    acc = value if acc is None else acc + value
            result.append(carry[m] + jnp.where(inside, acc, 0.0))
        return tuple(result)

    sums = lax.fori_loop(
        0, groups, add_up, tuple(jnp.zeros((SUB, LANES), F32) for _ in range(CHEB + 1))
    )
    for m in range(CHEB + 1):
        tot[m] = sums[m]
    kept.wait()
    sent.wait()


def interior(idx, inter, vec, hop, pot, stk):
    _, nvec, rows, width = vec.shape
    chunks = width // LANES
    group = 4
    any_ = pl.BlockSpec(memory_space=pl.ANY)
    smem = pl.BlockSpec(memory_space=pltpu.SMEM)
    half = jax.ShapeDtypeStruct((CHEB + 1, 4, chunks, rows // 2, LANES), F32)
    n = chunks * (3 + nvec // group) + 2
    return pl.pallas_call(
        functools.partial(interior_kernel, rows, chunks, nvec, group),
        out_shape=[half, half, jax.ShapeDtypeStruct((CHEB + 1, SUB, LANES), F32)],
        in_specs=[smem, smem, any_, any_, any_, any_],
        out_specs=[any_, any_, pl.BlockSpec(memory_space=pltpu.VMEM)],
        scratch_shapes=[
            pltpu.VMEM((4, nvec, chunks, rows + 2 * PAD, LANES), F32),
            pltpu.VMEM((4, group, chunks, rows + 2 * PAD, LANES), F32),
            pltpu.VMEM((4, group, chunks, rows + 2 * PAD, LANES), F32),
            pltpu.VMEM((2, 4, chunks, rows + SUB, LANES), F32),
            pltpu.VMEM((4, chunks, rows, LANES), F32),
            pltpu.VMEM((chunks, rows, LANES), jnp.int32),
            pltpu.VMEM((2, chunks, rows, LANES), F32),
            pltpu.VMEM((CHEB + 1, 4, chunks, rows, LANES), F32),
            pltpu.SemaphoreType.DMA((n,)),
        ],
        compiler_params=pltpu.CompilerParams(vmem_limit_bytes=VMEM_LIMIT),
        cost_estimate=pl.CostEstimate(
            flops=60_000_000, bytes_accessed=9_000_000, transcendentals=0
        ),
        name="interior",
    )(idx, inter, vec, hop, pot, stk)


WIN = 7


def edges_kernel(chunks, parts, idx, own_long, own_short, got_long, got_short, extra, part, keep,
                 send, tot, w, t1, t2, res, sems):
    odd, core = idx[0], idx[1]
    three = 3 * REC

    def both(refs, when, dst, sem):
        @pl.when(when)
        def _():
            pltpu.make_async_copy(refs[0], dst, sem).start()

        @pl.when(jnp.logical_not(when))
        def _():
            pltpu.make_async_copy(refs[1], dst, sem).start()

        return pltpu.make_async_copy(refs[0], dst, sem)

    even = odd == 0
    guard = REC
    copies = [
        both((got_long, got_short), even, w.at[0, :, pl.ds(guard, three)], sems.at[0]),
        both((own_long, own_short), even, w.at[0, :, pl.ds(guard + three, three)], sems.at[1]),
        both((own_short, own_long), even, w.at[1, :, pl.ds(guard + REC, three)], sems.at[2]),
        both((got_short, got_long), even, w.at[1, :, pl.ds(guard + REC + three, three)], sems.at[3]),
    ]
    for band, place in ((0, 6), (1, 0)):
        copy = pltpu.make_async_copy(
            extra.at[band], w.at[band, :, pl.ds(guard + place * REC, REC)], sems.at[4 + band]
        )
        copy.start()
        copies.append(copy)
    for copy in copies:
        copy.wait()

    def sweep(order, first, last):
        def body(j, carry):
            band = lax.rem(j, 2)
            i = first + lax.div(j, 2)
            rec0 = guard + i * REC

            def here(ref, site, c, shift=0):
                if ref is w:
                    at = pl.multiple_of(rec0 + shift * REC + site * SUB, SUB)
                else:
                    at = pl.multiple_of((i + 1 + shift) * 32 + site * SUB, SUB)
                return ref[band, c, pl.ds(at, SUB), :]

            def coef_at(k, c, shift=0):
                at = rec0 + shift * REC + COEF + k
                return jnp.broadcast_to(w[band, c, pl.ds(at, 1), :], (SUB, LANES))

            source, before, target = {
                1: (w, None, t1),
                2: (t1, w, t2),
                3: (t2, t1, t1),
                4: (t1, t2, None),
            }[order]
            centre = order == 4
            b_prev = [roll_right(here(source, 2 * l + 1, chunks - 1)) for l in range(2)]
            a_here = [roll_left(here(source, 2 * l, 0)) for l in range(2)]
            for c in range(chunks):
                nxt = (c + 1) % chunks
                a_next = [roll_left(here(source, 2 * l, nxt)) for l in range(2)]
                b_here = [roll_right(here(source, 2 * l + 1, c)) for l in range(2)]
                coef = [coef_at(k, c) for k in range(14)]
                t2_down = [coef_at(4 * l + 2, c, 1) for l in range(2)]
                a = [here(source, 2 * l, c) for l in range(2)]
                b = [here(source, 2 * l + 1, c) for l in range(2)]
                a_down = [here(source, 2 * l, c, 1) for l in range(2)]
                b_up = [here(source, 2 * l + 1, c, -1) for l in range(2)]
                a_right = [from_right(a_here[l], a_next[l]) for l in range(2)]
                b_left = [from_left(b_here[l], b_prev[l]) for l in range(2)]
                new = hop_apply(a, b, a_right, b_left, a_down, b_up, coef, t2_down)
                for s in range(4):
                    if order == 1:
                        value = new[s] * 0.5
                    else:
                        value = new[s] - here(before, s, c)
                    if target is not None:
                        at = pl.multiple_of((i + 1) * 32 + s * SUB, SUB)
                        target[band, c, pl.ds(at, SUB), :] = value
                    new[s] = value
                if centre:
                    moments(band, i, c, 4, new, here)
                a_here = a_next
                b_prev = b_here
            return carry

        lax.fori_loop(0, 2 * (last - first + 1), body, 0)

    def moments(band, i, c, order, values, here):
        for s in range(4):
            first = here(w, s, c)
            term = jnp.sum(first * values[s], axis=0, keepdims=True)
            res[band, i - 2, c, pl.ds(order * 4 + s, 1), :] = term

    def collect(order, ref):
        def body(j, carry):
            band = lax.rem(j, 2)
            i = 2 + lax.div(j, 2)

            def here(source, site, c):
                at = pl.multiple_of(guard + i * REC + site * SUB, SUB)
                return source[band, c, pl.ds(at, SUB), :]

            for c in range(chunks):
                values = []
                for s in range(4):
                    if ref is w:
                        values.append(here(w, s, c))
                    else:
                        at = pl.multiple_of((i + 1) * 32 + s * SUB, SUB)
                        values.append(ref[band, c, pl.ds(at, SUB), :])
                moments(band, i, c, order, values, here)
            return carry

        lax.fori_loop(0, 6, body, 0)

    collect(0, w)
    sweep(1, 0, 6)
    collect(1, t1)
    sweep(2, 1, 5)
    collect(2, t2)
    sweep(3, 1, 5)
    collect(3, t1)
    sweep(4, 2, 4)
    out = [
        pltpu.make_async_copy(res.at[core], keep, sems.at[6]),
        pltpu.make_async_copy(res.at[1 - core], send, sems.at[7]),
    ]
    for copy in out:
        copy.start()
    lane = lax.broadcasted_iota(jnp.int32, (SUB, LANES), 1)
    row = jnp.zeros((SUB, LANES), F32)
    for m in range(CHEB + 1):
        acc = part[m]
        inner = None
        for band in range(2):
            for r in ((1, 2), (0, 1))[band]:
                for c in range(chunks):
                    value = res[band, r, c, pl.ds(4 * m, 4), :]
                    inner = value if inner is None else inner + value
        total = jnp.sum(acc) + jnp.sum(inner)
        row = jnp.where(lane == m, total, row)
    for k in range(parts // SUB):
        tot[pl.ds(k * SUB, SUB), :] = row
    for copy in out:
        copy.wait()


def edges(idx, own_long, own_short, got_long, got_short, extra, part, parts):
    chunks = own_long.shape[0]
    any_ = pl.BlockSpec(memory_space=pl.ANY)
    smem = pl.BlockSpec(memory_space=pltpu.SMEM)
    vmem = pl.BlockSpec(memory_space=pltpu.VMEM)
    edge = jax.ShapeDtypeStruct((3, chunks, 24, LANES), F32)
    return pl.pallas_call(
        functools.partial(edges_kernel, chunks, parts),
        out_shape=[edge, edge, jax.ShapeDtypeStruct((parts, LANES), F32)],
        in_specs=[smem, any_, any_, any_, any_, any_, vmem],
        out_specs=[any_, any_, vmem],
        scratch_shapes=[
            pltpu.VMEM((2, chunks, (WIN + 2) * REC, LANES), F32),
            pltpu.VMEM((2, chunks, (WIN + 2) * 32, LANES), F32),
            pltpu.VMEM((2, chunks, (WIN + 2) * 32, LANES), F32),
            pltpu.VMEM((2, 3, chunks, 24, LANES), F32),
            pltpu.SemaphoreType.DMA((8,)),
        ],
        compiler_params=pltpu.CompilerParams(vmem_limit_bytes=VMEM_LIMIT),
        cost_estimate=pl.CostEstimate(
            flops=20_000_000, bytes_accessed=4_000_000, transcendentals=0
        ),
        name="edges",
    )(idx, own_long, own_short, got_long, got_short, extra, part)


ACOS = (
    1.5707963050,
    -0.2145988016,
    0.0889789874,
    -0.0501743046,
    0.0308918810,
    -0.0170881256,
    0.0066700901,
    -0.0012624911,
)


def arccos(e):
    size = jnp.abs(e)
    poly = jnp.full_like(size, ACOS[-1])
    for value in ACOS[-2::-1]:
        poly = poly * size + value
    angle = jnp.sqrt(1.0 - size) * poly
    return jnp.where(e < 0.0, math.pi - angle, angle)


def weights_of(e):
    gain = jackson(CHEB + 1)
    sine = jnp.sqrt((1.0 - e) * (1.0 + e))
    square = e * e
    sines = [sine, 2.0 * e * sine, (4.0 * square - 1.0) * sine, 4.0 * e * (2.0 * square - 1.0) * sine]
    out = [gain[0] * (1.0 - arccos(e) / math.pi)]
    for m in range(1, CHEB + 1):
        out.append(sines[m - 1] * (-2.0 * gain[m] / (math.pi * m)))
    return out


def density_kernel(chunks, half, scale, sites, idx, filling, sums, mine, other, my_edge, other_edge,
                   out):
    core = idx[1]
    added = jnp.sum(sums[...], axis=0, keepdims=True) * scale
    lane = lax.broadcasted_iota(jnp.int32, (1, LANES), 1)
    totals = [jnp.sum(jnp.where(lane == m, added, 0.0)) for m in range(CHEB + 1)]
    target = filling[0] * sites

    point = (
        lax.broadcasted_iota(jnp.int32, (SUB, LANES), 0) * LANES
        + lax.broadcasted_iota(jnp.int32, (SUB, LANES), 1)
        + 1
    )
    ways = 2 ** (BISECT // 2)
    valid = point < ways
    low = jnp.float32(-1.0)
    step = 2.0
    for _ in range(2):
        step = step / ways
        mids = jnp.where(valid, low + point.astype(F32) * step, 0.0)
        count = None
        for value, total in zip(weights_of(mids), totals):
            term = value * total
            count = term if count is None else count + term
        below = jnp.sum(jnp.where(valid & (count < target), 1.0, 0.0))
        low = low + below * step
    chem = jnp.full((SUB, LANES), low + 0.5 * step, F32)
    weights = [value * scale for value in weights_of(chem)]

    for c in range(chunks):
        for s in range(4):
            for g in range(half // SUB):
                at = pl.ds(g * SUB, SUB)
                acc = None
                for m in range(CHEB + 1):
                    term = weights[m] * (mine[m, s, c, at, :] + other[m, s, c, at, :])
                    acc = term if acc is None else acc + term
                out[c, pl.ds(s * half + g * SUB, SUB), :] = acc
        rows = []
        for r in range(3):
            acc = None
            for m in range(CHEB + 1):
                at = pl.ds(4 * m, 4)
                term = weights[m][0:4] * (my_edge[r, c, at, :] + other_edge[r, c, at, :])
                acc = term if acc is None else acc + term
            rows.append(acc)
        halo = jnp.where(core == 0, rows[0], rows[2])
        out[c, pl.ds(4 * half, SUB), :] = jnp.broadcast_to(
            jnp.sum(halo, axis=0, keepdims=True), (SUB, LANES)
        )

        @pl.when(core == 0)
        def _():
            for s in range(4):
                out[c, pl.ds(s * half, 1), :] = rows[1][s : s + 1]
                out[c, pl.ds(s * half + 1, 1), :] = rows[2][s : s + 1]

        @pl.when(core != 0)
        def _():
            for s in range(4):
                out[c, pl.ds(s * half + half - 2, 1), :] = rows[0][s : s + 1]
                out[c, pl.ds(s * half + half - 1, 1), :] = rows[1][s : s + 1]


def density(idx, filling, sums, mine, other, my_edge, other_edge, vectors, sites):
    _, _, chunks, half, _ = mine.shape
    smem = pl.BlockSpec(memory_space=pltpu.SMEM)
    vmem = pl.BlockSpec(memory_space=pltpu.VMEM)
    return pl.pallas_call(
        functools.partial(density_kernel, chunks, half, 1.0 / vectors, float(sites)),
        out_shape=jax.ShapeDtypeStruct((chunks, 4 * half + SUB, LANES), F32),
        in_specs=[smem, smem, vmem, vmem, vmem, vmem, vmem],
        out_specs=vmem,
        compiler_params=pltpu.CompilerParams(vmem_limit_bytes=VMEM_LIMIT),
        cost_estimate=pl.CostEstimate(flops=2_000_000, bytes_accessed=4_000_000, transcendentals=0),
        name="density",
    )(idx, filling, sums, mine, other, my_edge, other_edge)


def potential_kernel(chunks, half, idx, mine, other, out, charge):
    first = idx[1] == 0
    guard = SUB

    def rows_of(ref, c):
        total = None
        for s in range(4):
            value = ref[c, pl.ds(s * half, half), :]
            total = value if total is None else total + value
        return total - 2.0

    for c in range(chunks):
        m, o = rows_of(mine, c), rows_of(other, c)
        charge[c, pl.ds(guard, half), :] = jnp.where(first, m, o)
        charge[c, pl.ds(guard + half, half), :] = jnp.where(first, o, m)
        m, o = (ref[c, pl.ds(4 * half, 1), :] - 2.0 for ref in (mine, other))
        charge[c, pl.ds(guard - 1, 1), :] = jnp.where(first, m, o)
        charge[c, pl.ds(guard + 2 * half, 1), :] = jnp.where(first, o, m)
    for g in range(2 * half // SUB):
        at = pl.ds(guard + g * SUB, SUB)
        for c in range(chunks):
            here = charge[c, at, :]
            left = from_left(roll_right(here), roll_right(charge[(c - 1) % chunks, at, :]))
            right = from_right(roll_left(here), roll_left(charge[(c + 1) % chunks, at, :]))
            near = (
                charge[c, pl.ds(guard + g * SUB - 1, SUB), :]
                + charge[c, pl.ds(guard + g * SUB + 1, SUB), :]
                + left
                + right
            )
            base = 0.5 * here + 0.25 * near
            in_first = g * SUB < half
            row = g * SUB - (0 if in_first else half)
            for s in range(4):
                rows = pl.ds(s * half + row, SUB)
                a, b = mine[c, rows, :], other[c, rows, :]
                dens = jnp.where(first, a, b) if in_first else jnp.where(first, b, a)
                out[s, pl.ds(g * SUB, SUB), pl.ds(c * LANES, LANES)] = 3.0 * (dens - 0.5) + base


def new_potential(idx, mine, other):
    chunks, height, _ = mine.shape
    half = (height - SUB) // 4
    smem = pl.BlockSpec(memory_space=pltpu.SMEM)
    vmem = pl.BlockSpec(memory_space=pltpu.VMEM)
    return pl.pallas_call(
        functools.partial(potential_kernel, chunks, half),
        out_shape=jax.ShapeDtypeStruct((4, 2 * half, chunks * LANES), F32),
        in_specs=[smem, vmem, vmem],
        out_specs=vmem,
        scratch_shapes=[pltpu.VMEM((chunks, 2 * half + 2 * SUB, LANES), F32)],
        compiler_params=pltpu.CompilerParams(vmem_limit_bytes=VMEM_LIMIT),
        cost_estimate=pl.CostEstimate(flops=1_000_000, bytes_accessed=2_000_000, transcendentals=0),
        name="new_potential",
    )(idx, mine, other)


def per_device(vectors, hoppings, potential, stacking, interlayer, filling):
    strips, ranks = lax.axis_size("dom"), lax.axis_size("vec")
    _, nvec, rows, width = vectors.shape
    dom, vec = lax.axis_index("dom"), lax.axis_index("vec")
    idx = jnp.stack([dom % 2, vec % 2]).astype(jnp.int32)
    long_way = [(i, (i - 1 if i % 2 == 0 else i + 1) % strips) for i in range(strips)]
    short_way = [(i, i ^ 1) for i in range(strips)]
    sibling = [(i, i ^ 1) for i in range(ranks)]
    across = [(i, i ^ 2) for i in range(ranks)]

    own_long, own_short, extra = pack(
        idx,
        interlayer,
        vectors.reshape(4 * nvec, rows, width),
        hoppings.reshape(6, rows, width),
        potential,
        stacking,
    )
    got_long = lax.ppermute(own_long, "dom", long_way)
    got_short = lax.ppermute(own_short, "dom", short_way)
    mine, yours, part = interior(idx, interlayer, vectors, hoppings, potential, stacking)
    my_edge, your_edge, totals = edges(
        idx, own_long, own_short, got_long, got_short, extra, part, strips * ranks
    )
    other = lax.ppermute(yours, "vec", sibling)
    other_edge = lax.ppermute(your_edge, "vec", sibling)
    sums = lax.all_to_all(totals, ("dom", "vec"), 0, 0, tiled=True)
    sites = 4 * rows * width * strips
    chip = density(
        idx, filling, sums, mine, other, my_edge, other_edge, nvec * ranks, sites
    )
    whole = chip + lax.ppermute(chip, "vec", across)
    return new_potential(idx, whole, lax.ppermute(whole, "vec", sibling))


def solution(mesh):
    placed = (
        P(None, "vec", "dom", None),
        P(None, None, "dom", None),
        P(None, "dom", None),
        P("dom", None),
        P(),
        P(),
    )
    return jax.shard_map(
        per_device, mesh=mesh, in_specs=placed, out_specs=P(None, "dom", None), check_vma=False
    )
```

```python
import functools
import math

import jax
import jax.numpy as jnp
from jax import lax
from jax.experimental import pallas as pl
from jax.experimental.pallas import tpu as pltpu
from jax.sharding import PartitionSpec as P

CHEB = 4
BISECT = 16
LANES = 128
SUB = 8
REC = 48
COEF = 32
F32 = jnp.float32
VMEM_LIMIT = 44 * 1024 * 1024
VMEM_WIDE = 64 * 1024 * 1024 - 256 * 1024


def jackson(count):
    angle = math.pi / (count + 1)
    return [
        ((count - m + 1) * math.cos(angle * m) + math.sin(angle * m) / math.tan(angle))
        / (count + 1)
        for m in range(count)
    ]


def lane_is(where, shape=(SUB, LANES)):
    return lax.broadcasted_iota(jnp.int32, shape, 1) == where


def from_left(here, left):
    return jnp.where(lane_is(0, here.shape), left, here)


def from_right(here, right):
    return jnp.where(lane_is(LANES - 1, here.shape), right, here)


def roll_left(x):
    return pltpu.roll(x, LANES - 1, 1)


def roll_right(x):
    return pltpu.roll(x, 1, 1)


def pick(classes, table):
    values = list(table)
    bit = 1
    while len(values) > 1:
        hit = (classes & bit) != 0
        values = [jnp.where(hit, values[i + 1], values[i]) for i in range(0, len(values), 2)]
        bit *= 2
    return values[0]


def hop_apply(a, b, a_right, b_left, a_down, b_up, coef, t2_down):
    pot = coef[8:12]
    aa, ab = coef[12:14]
    out = []
    for layer in range(2):
        t0, t1, t2, t1r = coef[4 * layer : 4 * layer + 4]
        h_a = t0 * b[layer] + t1 * b_left[layer] + t2 * b_up[layer] + pot[2 * layer] * a[layer]
        h_b = (
            t0 * a[layer]
            + t1r * a_right[layer]
            + t2_down[layer] * a_down[layer]
            + pot[2 * layer + 1] * b[layer]
        )
        out.append([h_a, h_b])
    out[0][0] = out[0][0] + aa * a[1] + ab * b[1]
    out[1][0] = out[1][0] + aa * a[0]
    out[1][1] = out[1][1] + ab * a[0]
    return [out[0][0], out[0][1], out[1][0], out[1][1]]


def pack_kernel(rows, chunks, idx, inter, vec, hop, pot, stk, long_out, short_out, extra,
                v8, h8, p8, s8, rec, sems):
    copies = []
    n = 0
    for band in range(2):
        at = pl.ds(band * (rows - SUB), SUB)
        for c in range(chunks):
            lanes = pl.ds(c * LANES, LANES)
            for src, dst in (
                (hop.at[:, at, lanes], h8.at[band, c]),
                (pot.at[:, at, lanes], p8.at[band, c]),
                (stk.at[at, lanes], s8.at[band, c]),
                (vec.at[:, at, lanes], v8.at[band, c]),
            ):
                copies.append(pltpu.make_async_copy(src, dst, sems.at[n]))
                n += 1
    for copy in copies:
        copy.start()
    nf = vec.shape[0]
    flat = v8.reshape(2, chunks, nf * SUB, LANES)
    odd = idx[0]
    outs = []
    for band in range(2):
        for copy in copies[4 * chunks * band : 4 * chunks * (band + 1)]:
            copy.wait()
        for c in range(chunks):
            first = 0 if band == 0 else SUB - 4
            for r in range(4):
                for s in range(nf // SUB):
                    rec[band, c, pl.ds(r * REC + s * SUB, SUB), :] = flat[
                        band, c, pl.ds(s * SUB * SUB + first + r, SUB, stride=SUB), :
                    ]
            after = (c + 1) % chunks
            coef = []
            for layer in range(2):
                for k in range(3):
                    coef.append(h8[band, c, 3 * layer + k] * -0.25)
                    if k == 1:
                        here = h8[band, c, 3 * layer + 1]
                        there = h8[band, after, 3 * layer + 1]
                        shifted = from_right(roll_left(here), roll_left(there)) * -0.25
                coef.append(shifted)
            for s in range(4):
                coef.append(p8[band, c, s] * 0.25)
            classes = s8[band, c]
            for w in range(2):
                table = [inter[w, k] * 0.25 for k in range(inter.shape[1])]
                coef.append(pick(classes, table))
            for k, value in enumerate(coef):
                rec[band, c, pl.ds(COEF + k, 4, stride=REC), :] = value[first : first + 4]
            zero = jnp.zeros((4, LANES), F32)
            for k in range(len(coef), REC - COEF):
                rec[band, c, pl.ds(COEF + k, 4, stride=REC), :] = zero
        message = rec.at[band, :, pl.ds(band * REC, 3 * REC)]
        spare = rec.at[band, :, pl.ds((1 - band) * 3 * REC, REC)]
        away = pltpu.make_async_copy(spare, extra.at[band], sems.at[n])
        away.start()
        outs.append(away)
        n += 1

        @pl.when(odd == band)
        def _():
            pltpu.make_async_copy(message, long_out, sems.at[n]).start()

        @pl.when(odd != band)
        def _():
            pltpu.make_async_copy(message, short_out, sems.at[n]).start()

        outs.append(pltpu.make_async_copy(message, long_out, sems.at[n]))
        n += 1
    for copy in outs:
        copy.wait()


def pack(idx, inter, vec, hop, pot, stk):
    fields, rows, width = vec.shape
    chunks = width // LANES
    any_ = pl.BlockSpec(memory_space=pl.ANY)
    smem = pl.BlockSpec(memory_space=pltpu.SMEM)
    message = jax.ShapeDtypeStruct((chunks, 3 * REC, LANES), F32)
    n_in = 2 * chunks * 4
    return pl.pallas_call(
        functools.partial(pack_kernel, rows, chunks),
        out_shape=[message, message, jax.ShapeDtypeStruct((2, chunks, REC, LANES), F32)],
        in_specs=[smem, smem, any_, any_, any_, any_],
        out_specs=[any_, any_, any_],
        scratch_shapes=[
            pltpu.VMEM((2, chunks, fields, SUB, LANES), F32),
            pltpu.VMEM((2, chunks, 6, SUB, LANES), F32),
            pltpu.VMEM((2, chunks, 4, SUB, LANES), F32),
            pltpu.VMEM((2, chunks, SUB, LANES), jnp.int32),
            pltpu.VMEM((2, chunks, 4 * REC, LANES), F32),
            pltpu.SemaphoreType.DMA((n_in + 4,)),
        ],
        compiler_params=pltpu.CompilerParams(vmem_limit_bytes=VMEM_WIDE),
        cost_estimate=pl.CostEstimate(flops=1_000_000, bytes_accessed=4_000_000, transcendentals=0),
        name="pack",
    )(idx, inter, vec, hop, pot, stk)


PAD = 8


def interior_kernel(rows, chunks, nvec, group, idx, inter, vec, hop, pot, stk, after, keep, send,
                    tot, x, t1, t2, hp, pt, st, ww, mom, dots, sems):
    del after
    halves = nvec // group
    copies = []
    n = 0
    for c in range(chunks):
        lanes = pl.ds(c * LANES, LANES)
        for src, dst in (
            (hop.at[:, :, :, lanes], hp.at[:, 0:3, c, pl.ds(0, rows)]),
            (pot.at[:, :, lanes], pt.at[:, c]),
            (stk.at[:, lanes], st.at[c]),
        ):
            copies.append(pltpu.make_async_copy(src, dst, sems.at[n]))
            n += 1
    late = []
    for q in range(halves):
        part = []
        for c in range(chunks):
            lanes = pl.ds(c * LANES, LANES)
            part.append(
                pltpu.make_async_copy(
                    vec.at[:, pl.ds(q * group, group), :, lanes],
                    x.at[:, pl.ds(q * group, group), c, pl.ds(PAD, rows)],
                    sems.at[n],
                )
            )
            n += 1
        late.append(part)
    for copy in copies + [copy for part in late for copy in part]:
        copy.start()
    for copy in copies:
        copy.wait()

    groups = rows // SUB

    def prepare(g, carry):
        at = pl.ds(pl.multiple_of(g * SUB, SUB), SUB)
        for layer in range(2):
            rolled = {}
            for c in range(chunks):
                rolled[c] = roll_left(hp[layer, 1, c, at, :])
            for c in range(chunks):
                hp[layer, 3, c, at, :] = (
                    from_right(rolled[c], rolled[(c + 1) % chunks]) * -0.25
                )
            for k in range(3):
                for c in range(chunks):
                    hp[layer, k, c, at, :] = hp[layer, k, c, at, :] * -0.25
        for c in range(chunks):
            for s in range(4):
                pt[s, c, at, :] = pt[s, c, at, :] * 0.25
            classes = st[c, at, :]
            for w in range(2):
                table = [inter[w, k] * 0.25 for k in range(inter.shape[1])]
                ww[w, c, at, :] = pick(classes, table)
        return carry

    lax.fori_loop(0, groups, prepare, 0)

    def sweep(order, q, source, before, target):
        def load(ref, s, v, c, at):
            return ref[s, v, c, at, :]

        def body(g, carry):
            base = pl.multiple_of(g * SUB, SUB)
            mid = pl.ds(base + PAD, SUB)
            up = pl.ds(base + PAD - 1, SUB)
            down = pl.ds(base + PAD + 1, SUB)
            plain = pl.ds(base, SUB)
            plain_down = pl.ds(base + 1, SUB)
            vs = range(group)
            src, off = source

            def rolled(site, c, fn):
                return [fn(load(src, site, v + off, c, mid)) for v in vs]

            products = [None] * 2
            b_prev = [rolled(2 * l + 1, chunks - 1, roll_right) for l in range(2)]
            a_here = [rolled(2 * l, 0, roll_left) for l in range(2)]
            for c in range(chunks):
                nxt = (c + 1) % chunks
                a_next = [rolled(2 * l, nxt, roll_left) for l in range(2)]
                b_here = [rolled(2 * l + 1, c, roll_right) for l in range(2)]
                coef = []
                for layer in range(2):
                    for k in range(4):
                        coef.append(hp[layer, k, c, plain, :])
                for s in range(4):
                    coef.append(pt[s, c, plain, :])
                for w in range(2):
                    coef.append(ww[w, c, plain, :])
                t2_down = [hp[layer, 2, c, plain_down, :] for layer in range(2)]
                sums = [None] * 4
                squares = [None] * 4
                for v in vs:
                    a = [load(src, 2 * l, v + off, c, mid) for l in range(2)]
                    b = [load(src, 2 * l + 1, v + off, c, mid) for l in range(2)]
                    a_down = [load(src, 2 * l, v + off, c, down) for l in range(2)]
                    b_up = [load(src, 2 * l + 1, v + off, c, up) for l in range(2)]
                    a_right = [from_right(a_here[l][v], a_next[l][v]) for l in range(2)]
                    b_left = [from_left(b_here[l][v], b_prev[l][v]) for l in range(2)]
                    new = hop_apply(a, b, a_right, b_left, a_down, b_up, coef, t2_down)
                    for s in range(4):
                        if order == 1:
                            value = new[s] * 0.5
                        else:
                            ref, shift = before
                            value = new[s] - load(ref, s, v + shift, c, mid)
                        if target is not None:
                            target[s, v, c, mid, :] = value
                        first = load(x, s, v + q * group, c, mid)
                        term = first * value
                        sums[s] = term if sums[s] is None else sums[s] + term
                        if order == 2:
                            prior = load(src, s, v + off, c, mid)
                            for k, pair in enumerate((prior * value, value * value)):
                                products[k] = pair if products[k] is None else products[k] + pair
                        if order == 1:
                            sq = first * first
                            squares[s] = sq if squares[s] is None else squares[s] + sq
                for s in range(4):
                    if q > 0:
                        sums[s] = sums[s] + mom[order, s, c, plain, :]
                    mom[order, s, c, plain, :] = sums[s]
                    if order == 1:
                        if q > 0:
                            squares[s] = squares[s] + mom[0, s, c, plain, :]
                        mom[0, s, c, plain, :] = squares[s]
                a_here = a_next
                b_prev = b_here
            if order == 2:
                row = lax.broadcasted_iota(jnp.int32, (SUB, LANES), 0) + base
                inside = (row >= 2) & (row < rows - 2)
                for k in range(2):
                    dots[k] = dots[k] + jnp.where(inside, products[k], 0.0)
            return carry

        lax.fori_loop(0, groups, body, 0)

    dots[...] = jnp.zeros_like(dots)
    for q in range(halves):
        for copy in late[q]:
            copy.wait()
        start = (x, q * group)
        sweep(1, q, start, None, t1)
        sweep(2, q, (t1, 0), start, t2)
        sweep(3, q, (t2, 0), (t1, 0), t1)
        sweep(4, q, (t1, 0), (t2, 0), None)

    half = rows // 2
    core = idx[1]
    kept = pltpu.make_async_copy(
        mom.at[:, :, :, pl.ds(pl.multiple_of(core * half, SUB), half)], keep, sems.at[n]
    )
    sent = pltpu.make_async_copy(
        mom.at[:, :, :, pl.ds(pl.multiple_of((1 - core) * half, SUB), half)], send, sems.at[n + 1]
    )
    kept.start()
    sent.start()

    def add_up(g, carry):
        base = pl.multiple_of(g * SUB, SUB)
        row = lax.broadcasted_iota(jnp.int32, (SUB, LANES), 0) + base
        inside = (row >= 2) & (row < rows - 2)
        result = []
        for m in range(3):
            acc = None
            for s in range(4):
                for c in range(chunks):
                    value = mom[m, s, c, pl.ds(base, SUB), :]
                    acc = value if acc is None else acc + value
            result.append(carry[m] + jnp.where(inside, acc, 0.0))
        return tuple(result)

    sums = lax.fori_loop(0, groups, add_up, tuple(jnp.zeros((SUB, LANES), F32) for _ in range(3)))
    for m in range(3):
        tot[m] = sums[m]
    for k in range(2):
        tot[3 + k] = dots[k]
    kept.wait()
    sent.wait()


def interior(idx, inter, vec, hop, pot, stk, after):
    _, nvec, rows, width = vec.shape
    chunks = width // LANES
    group = 4
    any_ = pl.BlockSpec(memory_space=pl.ANY)
    smem = pl.BlockSpec(memory_space=pltpu.SMEM)
    half = jax.ShapeDtypeStruct((CHEB + 1, 4, chunks, rows // 2, LANES), F32)
    n = chunks * (3 + nvec // group) + 2
    return pl.pallas_call(
        functools.partial(interior_kernel, rows, chunks, nvec, group),
        out_shape=[half, half, jax.ShapeDtypeStruct((CHEB + 1, SUB, LANES), F32)],
        in_specs=[smem, smem, any_, any_, any_, any_, any_],
        out_specs=[any_, any_, pl.BlockSpec(memory_space=pltpu.VMEM)],
        scratch_shapes=[
            pltpu.VMEM((4, nvec, chunks, rows + 2 * PAD, LANES), F32),
            pltpu.VMEM((4, group, chunks, rows + 2 * PAD, LANES), F32),
            pltpu.VMEM((4, group, chunks, rows + 2 * PAD, LANES), F32),
            pltpu.VMEM((2, 4, chunks, rows + SUB, LANES), F32),
            pltpu.VMEM((4, chunks, rows, LANES), F32),
            pltpu.VMEM((chunks, rows, LANES), jnp.int32),
            pltpu.VMEM((2, chunks, rows, LANES), F32),
            pltpu.VMEM((CHEB + 1, 4, chunks, rows, LANES), F32),
            pltpu.VMEM((2, SUB, LANES), F32),
            pltpu.SemaphoreType.DMA((n,)),
        ],
        compiler_params=pltpu.CompilerParams(vmem_limit_bytes=VMEM_WIDE),
        cost_estimate=pl.CostEstimate(
            flops=60_000_000, bytes_accessed=9_000_000, transcendentals=0
        ),
        name="interior",
    )(idx, inter, vec, hop, pot, stk, after)


WIN = 7
GUARD = REC


def gather_window(odd, refs, w, sems):
    own_long, own_short, got_long, got_short, extra = refs
    three = 3 * REC
    even = odd == 0

    def both(first, second, dst, sem):
        @pl.when(even)
        def _():
            pltpu.make_async_copy(first, dst, sem).start()

        @pl.when(jnp.logical_not(even))
        def _():
            pltpu.make_async_copy(second, dst, sem).start()

        return pltpu.make_async_copy(first, dst, sem)

    copies = [
        both(got_long, got_short, w.at[0, :, pl.ds(GUARD, three)], sems.at[0]),
        both(own_long, own_short, w.at[0, :, pl.ds(GUARD + three, three)], sems.at[1]),
        both(own_short, own_long, w.at[1, :, pl.ds(GUARD + REC, three)], sems.at[2]),
        both(got_short, got_long, w.at[1, :, pl.ds(GUARD + REC + three, three)], sems.at[3]),
    ]
    for band, place in ((0, 6), (1, 0)):
        copy = pltpu.make_async_copy(
            extra.at[band], w.at[band, :, pl.ds(GUARD + place * REC, REC)], sems.at[4 + band]
        )
        copy.start()
        copies.append(copy)
    for copy in copies:
        copy.wait()


def window_slice(ref, is_w, band, c, i, site):
    start = GUARD + i * REC + site * SUB if is_w else (i + 1) * 32 + site * SUB
    return ref[band, c, pl.ds(pl.multiple_of(start, SUB), SUB), :]


def window_step(chunks, order, w, source, before, band, i, emit):
    from_w = order == 1

    def here(site, c, shift=0):
        return window_slice(source, from_w, band, c, i + shift, site)

    def coef_at(k, c, shift=0):
        at = GUARD + (i + shift) * REC + COEF + k
        return jnp.broadcast_to(w[band, c, pl.ds(at, 1), :], (SUB, LANES))

    b_prev = [roll_right(here(2 * l + 1, chunks - 1)) for l in range(2)]
    a_here = [roll_left(here(2 * l, 0)) for l in range(2)]
    for c in range(chunks):
        nxt = (c + 1) % chunks
        a_next = [roll_left(here(2 * l, nxt)) for l in range(2)]
        b_here = [roll_right(here(2 * l + 1, c)) for l in range(2)]
        coef = [coef_at(k, c) for k in range(14)]
        t2_down = [coef_at(4 * l + 2, c, 1) for l in range(2)]
        a = [here(2 * l, c) for l in range(2)]
        b = [here(2 * l + 1, c) for l in range(2)]
        a_down = [here(2 * l, c, 1) for l in range(2)]
        b_up = [here(2 * l + 1, c, -1) for l in range(2)]
        a_right = [from_right(a_here[l], a_next[l]) for l in range(2)]
        b_left = [from_left(b_here[l], b_prev[l]) for l in range(2)]
        new = hop_apply(a, b, a_right, b_left, a_down, b_up, coef, t2_down)
        for s in range(4):
            if order == 1:
                new[s] = new[s] * 0.5
            else:
                new[s] = new[s] - window_slice(before, order == 2, band, c, i, s)
        emit(c, new)
        a_here = a_next
        b_prev = b_here


def store_row(target, band, i):
    def emit(c, values):
        for s in range(4):
            at = pl.multiple_of((i + 1) * 32 + s * SUB, SUB)
            target[band, c, pl.ds(at, SUB), :] = values[s]

    return emit


def totals_kernel(chunks, parts, idx, own_long, own_short, got_long, got_short, extra, part, tot,
                  w, t1, dots, sems):
    gather_window(idx[0], (own_long, own_short, got_long, got_short, extra), w, sems)

    def first(j, carry):
        for band in range(2):
            i = 2 - band + j
            window_step(chunks, 1, w, w, None, band, i, store_row(t1, band, i))
        return carry

    lax.fori_loop(0, 4, first, 0)
    dots[...] = part[...]

    def second(j, carry):
        for band in range(2):
            i = 3 - band + j
            sums = [None] * 5

            def emit(c, values):
                for s in range(4):
                    zero = window_slice(w, True, band, c, i, s)
                    one = window_slice(t1, False, band, c, i, s)
                    two = values[s]
                    terms = (zero * zero, zero * one, zero * two, one * two, two * two)
                    for k, term in enumerate(terms):
                        sums[k] = term if sums[k] is None else sums[k] + term

            window_step(chunks, 2, w, t1, w, band, i, emit)
            for k in range(5):
                dots[k] = dots[k] + sums[k]
        return carry

    lax.fori_loop(0, 2, second, 0)
    lane = lax.broadcasted_iota(jnp.int32, (SUB, LANES), 1)
    row = jnp.zeros((SUB, LANES), F32)
    for m in range(5):
        row = jnp.where(lane == m, jnp.sum(dots[m]), row)
    for k in range(parts // SUB):
        tot[pl.ds(k * SUB, SUB), :] = row


def totals_of(idx, records, part, parts):
    chunks = records[0].shape[0]
    any_ = pl.BlockSpec(memory_space=pl.ANY)
    smem = pl.BlockSpec(memory_space=pltpu.SMEM)
    vmem = pl.BlockSpec(memory_space=pltpu.VMEM)
    return pl.pallas_call(
        functools.partial(totals_kernel, chunks, parts),
        out_shape=jax.ShapeDtypeStruct((parts, LANES), F32),
        in_specs=[smem, any_, any_, any_, any_, any_, vmem],
        out_specs=vmem,
        scratch_shapes=[
            pltpu.VMEM((2, chunks, (WIN + 2) * REC, LANES), F32),
            pltpu.VMEM((2, chunks, (WIN + 2) * 32, LANES), F32),
            pltpu.VMEM((5, SUB, LANES), F32),
            pltpu.SemaphoreType.DMA((6,)),
        ],
        compiler_params=pltpu.CompilerParams(vmem_limit_bytes=VMEM_WIDE),
        cost_estimate=pl.CostEstimate(flops=8_000_000, bytes_accessed=4_000_000, transcendentals=0),
        name="totals",
    )(idx, *records, part)


def edges_kernel(chunks, idx, own_long, own_short, got_long, got_short, extra, after, out, w, t1,
                 t2, res, sems):
    del after
    gather_window(idx[0], (own_long, own_short, got_long, got_short, extra), w, sems)

    def moments(band, i, c, order, values):
        for s in range(4):
            zero = window_slice(w, True, band, c, i, s)
            term = jnp.sum(zero * values[s], axis=0, keepdims=True)
            res[band, i - 2, c, pl.ds(order * 4 + s, 1), :] = term

    def sweep(order, first, last):
        source, before, target = {
            1: (w, None, t1),
            2: (t1, w, t2),
            3: (t2, t1, t1),
            4: (t1, t2, None),
        }[order]

        def body(j, carry):
            i = first + j
            for band in range(2):
                if order < 4:
                    emit = store_row(target, band, i)
                else:
                    emit = lambda c, values, band=band: moments(band, i, c, 4, values)
                window_step(chunks, order, w, source, before, band, i, emit)
            return carry

        lax.fori_loop(0, last - first + 1, body, 0)

    def collect(order, ref):
        def body(j, carry):
            i = 2 + j
            for band in range(2):
                for c in range(chunks):
                    values = [window_slice(ref, ref is w, band, c, i, s) for s in range(4)]
                    moments(band, i, c, order, values)
            return carry

        lax.fori_loop(0, 3, body, 0)

    collect(0, w)
    sweep(1, 0, 6)
    collect(1, t1)
    sweep(2, 1, 5)
    collect(2, t2)
    sweep(3, 1, 5)
    collect(3, t1)
    sweep(4, 2, 4)
    away = pltpu.make_async_copy(res, out, sems.at[6])
    away.start()
    away.wait()


def edges(idx, records, after):
    chunks = records[0].shape[0]
    any_ = pl.BlockSpec(memory_space=pl.ANY)
    smem = pl.BlockSpec(memory_space=pltpu.SMEM)
    return pl.pallas_call(
        functools.partial(edges_kernel, chunks),
        out_shape=jax.ShapeDtypeStruct((2, 3, chunks, 24, LANES), F32),
        in_specs=[smem, any_, any_, any_, any_, any_, any_],
        out_specs=any_,
        scratch_shapes=[
            pltpu.VMEM((2, chunks, (WIN + 2) * REC, LANES), F32),
            pltpu.VMEM((2, chunks, (WIN + 2) * 32, LANES), F32),
            pltpu.VMEM((2, chunks, (WIN + 2) * 32, LANES), F32),
            pltpu.VMEM((2, 3, chunks, 24, LANES), F32),
            pltpu.SemaphoreType.DMA((7,)),
        ],
        compiler_params=pltpu.CompilerParams(vmem_limit_bytes=VMEM_LIMIT),
        cost_estimate=pl.CostEstimate(
            flops=20_000_000, bytes_accessed=4_000_000, transcendentals=0
        ),
        name="edges",
    )(idx, *records, after)


ACOS = (
    1.5707963050,
    -0.2145988016,
    0.0889789874,
    -0.0501743046,
    0.0308918810,
    -0.0170881256,
    0.0066700901,
    -0.0012624911,
)


def arccos(e):
    size = jnp.abs(e)
    poly = jnp.full_like(size, ACOS[-1])
    for value in ACOS[-2::-1]:
        poly = poly * size + value
    angle = jnp.sqrt(1.0 - size) * poly
    return jnp.where(e < 0.0, math.pi - angle, angle)


def weights_of(e):
    gain = jackson(CHEB + 1)
    sine = jnp.sqrt((1.0 - e) * (1.0 + e))
    square = e * e
    sines = [sine, 2.0 * e * sine, (4.0 * square - 1.0) * sine, 4.0 * e * (2.0 * square - 1.0) * sine]
    out = [gain[0] * (1.0 - arccos(e) / math.pi)]
    for m in range(1, CHEB + 1):
        out.append(sines[m - 1] * (-2.0 * gain[m] / (math.pi * m)))
    return out


def density_kernel(chunks, half, scale, sites, idx, filling, sums, mine, other, edge, out):
    core = idx[1]
    added = jnp.sum(sums[...], axis=0, keepdims=True) * scale
    lane = lax.broadcasted_iota(jnp.int32, (1, LANES), 1)
    totals = [jnp.sum(jnp.where(lane == m, added, 0.0)) for m in range(CHEB + 1)]
    totals[3] = 2.0 * totals[3] - totals[1]
    totals[4] = 2.0 * totals[4] - totals[0]
    target = filling[0] * sites

    point = (
        lax.broadcasted_iota(jnp.int32, (SUB, LANES), 0) * LANES
        + lax.broadcasted_iota(jnp.int32, (SUB, LANES), 1)
        + 1
    )
    ways = 2 ** (BISECT // 2)
    valid = point < ways
    low = jnp.float32(-1.0)
    step = 2.0
    for _ in range(2):
        step = step / ways
        mids = jnp.where(valid, low + point.astype(F32) * step, 0.0)
        count = None
        for value, total in zip(weights_of(mids), totals):
            term = value * total
            count = term if count is None else count + term
        below = jnp.sum(jnp.where(valid & (count < target), 1.0, 0.0))
        low = low + below * step
    chem = jnp.full((SUB, LANES), low + 0.5 * step, F32)
    weights = [value * scale for value in weights_of(chem)]
    tall = 4 * half + SUB

    for c in range(chunks):
        for s in range(4):
            for g in range(half // SUB):
                at = pl.ds(g * SUB, SUB)
                acc = None
                for m in range(CHEB + 1):
                    term = weights[m] * (mine[m, s, c, at, :] + other[m, s, c, at, :])
                    acc = term if acc is None else acc + term
                out[pl.ds(c * tall + s * half + g * SUB, SUB), :] = acc
        bands = []
        for band in range(2):
            rows = []
            for r in range(3):
                acc = None
                for m in range(CHEB + 1):
                    term = weights[m][0:4] * edge[band, r, c, pl.ds(4 * m, 4), :]
                    acc = term if acc is None else acc + term
                rows.append(acc)
            bands.append(rows)
            halo = rows[0] if band == 0 else rows[2]
            out[pl.ds(chunks * tall + band * SUB + c, 1), :] = jnp.sum(halo, axis=0, keepdims=True)
        upper, lower = bands[0][1:], bands[1][:2]

        @pl.when(core == 0)
        def _():
            for r in range(2):
                for s in range(4):
                    out[pl.ds(c * tall + s * half + r, 1), :] = upper[r][s : s + 1]
                out[pl.ds(c * tall + 4 * half + 4 * r, 4), :] = lower[r]

        @pl.when(core != 0)
        def _():
            for r in range(2):
                for s in range(4):
                    out[pl.ds(c * tall + s * half + half - 2 + r, 1), :] = lower[r][s : s + 1]
                out[pl.ds(c * tall + 4 * half + 4 * r, 4), :] = upper[r]


def density(idx, filling, sums, mine, other, edge, vectors, sites):
    _, _, chunks, half, _ = mine.shape
    smem = pl.BlockSpec(memory_space=pltpu.SMEM)
    vmem = pl.BlockSpec(memory_space=pltpu.VMEM)
    return pl.pallas_call(
        functools.partial(density_kernel, chunks, half, 1.0 / vectors, float(sites)),
        out_shape=jax.ShapeDtypeStruct((chunks * (4 * half + SUB) + 2 * SUB, LANES), F32),
        in_specs=[smem, smem, vmem, vmem, vmem, vmem],
        out_specs=vmem,
        compiler_params=pltpu.CompilerParams(vmem_limit_bytes=VMEM_LIMIT),
        cost_estimate=pl.CostEstimate(flops=2_000_000, bytes_accessed=4_000_000, transcendentals=0),
        name="density",
    )(idx, filling, sums, mine, other, edge)


def potential_kernel(chunks, half, idx, mine, other, out, dens, charge):
    first = idx[1] == 0
    tall = 4 * half + SUB
    guard = SUB

    for c in range(chunks):
        for s in range(4):
            at = pl.ds(c * tall + s * half, half)
            m, o = mine[at, :], other[at, :]
            dens[s, c, pl.ds(0, half), :] = jnp.where(first, m, o)
            dens[s, c, pl.ds(half, half), :] = jnp.where(first, o, m)
        at = pl.ds(c * tall + 4 * half, SUB)
        m, o = mine[at, :], other[at, :]
        upper, lower = jnp.where(first, o, m), jnp.where(first, m, o)
        for r in range(2):
            for s in range(4):
                k = 4 * r + s
                for row, more in ((r, upper), (2 * half - 2 + r, lower)):
                    dens[s, c, pl.ds(row, 1), :] = dens[s, c, pl.ds(row, 1), :] + more[k : k + 1]
        for g in range(2 * half // SUB):
            at = pl.ds(g * SUB, SUB)
            total = (dens[0, c, at, :] + dens[1, c, at, :]) + (dens[2, c, at, :] + dens[3, c, at, :])
            charge[c, pl.ds(guard + g * SUB, SUB), :] = total - 2.0
        for band, row in ((0, guard - 1), (1, guard + 2 * half)):
            at = pl.ds(chunks * tall + band * SUB + c, 1)
            charge[c, pl.ds(row, 1), :] = mine[at, :] + other[at, :] - 2.0
    for g in range(2 * half // SUB):
        at = pl.ds(guard + g * SUB, SUB)
        for c in range(chunks):
            here = charge[c, at, :]
            left = from_left(roll_right(here), roll_right(charge[(c - 1) % chunks, at, :]))
            right = from_right(roll_left(here), roll_left(charge[(c + 1) % chunks, at, :]))
            near = (
                charge[c, pl.ds(guard + g * SUB - 1, SUB), :]
                + charge[c, pl.ds(guard + g * SUB + 1, SUB), :]
                + left
                + right
            )
            base = 0.5 * here + 0.25 * near
            for s in range(4):
                value = dens[s, c, pl.ds(g * SUB, SUB), :]
                out[s, pl.ds(g * SUB, SUB), pl.ds(c * LANES, LANES)] = 3.0 * (value - 0.5) + base


def new_potential(idx, mine, other, chunks):
    half = ((mine.shape[0] - 2 * SUB) // chunks - SUB) // 4
    smem = pl.BlockSpec(memory_space=pltpu.SMEM)
    vmem = pl.BlockSpec(memory_space=pltpu.VMEM)
    return pl.pallas_call(
        functools.partial(potential_kernel, chunks, half),
        out_shape=jax.ShapeDtypeStruct((4, 2 * half, chunks * LANES), F32),
        in_specs=[smem, vmem, vmem],
        out_specs=vmem,
        scratch_shapes=[
            pltpu.VMEM((4, chunks, 2 * half, LANES), F32),
            pltpu.VMEM((chunks, 2 * half + 2 * SUB, LANES), F32),
        ],
        compiler_params=pltpu.CompilerParams(vmem_limit_bytes=VMEM_LIMIT),
        cost_estimate=pl.CostEstimate(flops=1_000_000, bytes_accessed=2_000_000, transcendentals=0),
        name="new_potential",
    )(idx, mine, other)


def per_device(vectors, hoppings, potential, stacking, interlayer, filling):
    strips, ranks = lax.axis_size("dom"), lax.axis_size("vec")
    _, nvec, rows, width = vectors.shape
    dom, vec = lax.axis_index("dom"), lax.axis_index("vec")
    idx = jnp.stack([dom % 2, vec % 2]).astype(jnp.int32)
    long_way = [(i, (i - 1 if i % 2 == 0 else i + 1) % strips) for i in range(strips)]
    short_way = [(i, i ^ 1) for i in range(strips)]
    sibling = [(i, i ^ 1) for i in range(ranks)]
    across = [(i, i ^ 2) for i in range(ranks)]

    own_long, own_short, extra = pack(
        idx,
        interlayer,
        vectors.reshape(4 * nvec, rows, width),
        hoppings.reshape(6, rows, width),
        potential,
        stacking,
    )
    got_long = lax.ppermute(own_long, "dom", long_way)
    got_short = lax.ppermute(own_short, "dom", short_way)
    mine, yours, part = interior(
        idx, interlayer, vectors, hoppings, potential, stacking, own_short
    )
    records = (own_long, own_short, got_long, got_short, extra)
    totals = totals_of(idx, records, part, strips * ranks)
    edge = edges(idx, records, totals)
    yours, ready = lax.optimization_barrier((yours, totals))
    other = lax.ppermute(yours, "vec", sibling)
    sums = lax.all_to_all(ready, ("dom", "vec"), 0, 0, tiled=True)
    sites = 4 * rows * width * strips
    chip = density(idx, filling, sums, mine, other, edge, nvec * ranks, sites)
    whole = chip + lax.ppermute(chip, "vec", across)
    return new_potential(idx, whole, lax.ppermute(whole, "vec", sibling), width // LANES)


def solution(mesh):
    placed = (
        P(None, "vec", "dom", None),
        P(None, None, "dom", None),
        P(None, "dom", None),
        P("dom", None),
        P(),
        P(),
    )
    return jax.shard_map(
        per_device, mesh=mesh, in_specs=placed, out_specs=P(None, "dom", None), check_vma=False
    )
```

```python
import functools
import math

import jax
import jax.numpy as jnp
from jax import lax
from jax.experimental import pallas as pl
from jax.experimental.pallas import tpu as pltpu
from jax.sharding import PartitionSpec as P

CHEB = 4
BISECT = 16
LANES = 128
SUB = 8
REC = 48
COEF = 32
F32 = jnp.float32
VMEM_LIMIT = 44 * 1024 * 1024
VMEM_WIDE = 64 * 1024 * 1024 - 256 * 1024


def jackson(count):
    angle = math.pi / (count + 1)
    return [
        ((count - m + 1) * math.cos(angle * m) + math.sin(angle * m) / math.tan(angle))
        / (count + 1)
        for m in range(count)
    ]


def lane_is(where, shape=(SUB, LANES)):
    return lax.broadcasted_iota(jnp.int32, shape, 1) == where


def from_left(here, left):
    return jnp.where(lane_is(0, here.shape), left, here)


def from_right(here, right):
    return jnp.where(lane_is(LANES - 1, here.shape), right, here)


def roll_left(x):
    return pltpu.roll(x, LANES - 1, 1)


def roll_right(x):
    return pltpu.roll(x, 1, 1)


def pick(classes, table):
    values = list(table)
    bit = 1
    while len(values) > 1:
        hit = (classes & bit) != 0
        values = [jnp.where(hit, values[i + 1], values[i]) for i in range(0, len(values), 2)]
        bit *= 2
    return values[0]


def hop_apply(a, b, a_right, b_left, a_down, b_up, coef, t2_down):
    pot = coef[8:12]
    aa, ab = coef[12:14]
    out = []
    for layer in range(2):
        t0, t1, t2, t1r = coef[4 * layer : 4 * layer + 4]
        h_a = t0 * b[layer] + t1 * b_left[layer] + t2 * b_up[layer] + pot[2 * layer] * a[layer]
        h_b = (
            t0 * a[layer]
            + t1r * a_right[layer]
            + t2_down[layer] * a_down[layer]
            + pot[2 * layer + 1] * b[layer]
        )
        out.append([h_a, h_b])
    out[0][0] = out[0][0] + aa * a[1] + ab * b[1]
    out[1][0] = out[1][0] + aa * a[0]
    out[1][1] = out[1][1] + ab * a[0]
    return [out[0][0], out[0][1], out[1][0], out[1][1]]


def place():
    return lax.rem(lax.axis_index("dom"), 2), lax.rem(lax.axis_index("vec"), 2)


def pack_kernel(rows, chunks, table, vec, hop, pot, stk, long_out, short_out, extra, inter, v8, h8,
                p8, s8, rec, sems):
    copies = [pltpu.make_async_copy(table, inter, sems.at[0])]
    n = 1
    for band in range(2):
        at = pl.ds(band * (rows - SUB), SUB)
        for c in range(chunks):
            lanes = pl.ds(c * LANES, LANES)
            for src, dst in (
                (hop.at[:, at, lanes], h8.at[band, c]),
                (pot.at[:, at, lanes], p8.at[band, c]),
                (stk.at[at, lanes], s8.at[band, c]),
                (vec.at[:, at, lanes], v8.at[band, c]),
            ):
                copies.append(pltpu.make_async_copy(src, dst, sems.at[n]))
                n += 1
    for copy in copies:
        copy.start()
    nf = vec.shape[0]
    flat = v8.reshape(2, chunks, nf * SUB, LANES)
    odd = place()[0]
    outs = []
    copies[0].wait()
    waited = set()

    def wait_tile(band, c):
        if (band, c) not in waited:
            waited.add((band, c))
            for copy in copies[1 + 4 * (chunks * band + c) :][:4]:
                copy.wait()

    for band in range(2):
        for c in range(chunks):
            wait_tile(band, c)
            first = 0 if band == 0 else SUB - 4
            for r in range(4):
                for s in range(nf // SUB):
                    rec[band, c, pl.ds(r * REC + s * SUB, SUB), :] = flat[
                        band, c, pl.ds(s * SUB * SUB + first + r, SUB, stride=SUB), :
                    ]
            after = (c + 1) % chunks
            wait_tile(band, after)
            coef = []
            for layer in range(2):
                for k in range(3):
                    coef.append(h8[band, c, 3 * layer + k] * -0.25)
                    if k == 1:
                        here = h8[band, c, 3 * layer + 1]
                        there = h8[band, after, 3 * layer + 1]
                        shifted = from_right(roll_left(here), roll_left(there)) * -0.25
                coef.append(shifted)
            for s in range(4):
                coef.append(p8[band, c, s] * 0.25)
            classes = s8[band, c]
            for w in range(2):
                table = [inter[w, k] * 0.25 for k in range(inter.shape[1])]
                coef.append(pick(classes, table))
            for k, value in enumerate(coef):
                rec[band, c, pl.ds(COEF + k, 4, stride=REC), :] = value[first : first + 4]
            zero = jnp.zeros((4, LANES), F32)
            for k in range(len(coef), REC - COEF):
                rec[band, c, pl.ds(COEF + k, 4, stride=REC), :] = zero
            message = rec.at[band, c, pl.ds(band * REC, 3 * REC)]
            spare = rec.at[band, c, pl.ds((1 - band) * 3 * REC, REC)]
            away = pltpu.make_async_copy(spare, extra.at[band, c], sems.at[n])
            away.start()
            outs.append(away)
            n += 1

            @pl.when(odd == band)
            def _():
                pltpu.make_async_copy(message, long_out.at[c], sems.at[n]).start()

            @pl.when(odd != band)
            def _():
                pltpu.make_async_copy(message, short_out.at[c], sems.at[n]).start()

            outs.append(pltpu.make_async_copy(message, long_out.at[c], sems.at[n]))
            n += 1
    for copy in outs:
        copy.wait()


def pack(inter, vec, hop, pot, stk):
    fields, rows, width = vec.shape
    chunks = width // LANES
    any_ = pl.BlockSpec(memory_space=pl.ANY)
    message = jax.ShapeDtypeStruct((chunks, 3 * REC, LANES), F32)
    n_in = 2 * chunks * 4 + 1
    return pl.pallas_call(
        functools.partial(pack_kernel, rows, chunks),
        out_shape=[message, message, jax.ShapeDtypeStruct((2, chunks, REC, LANES), F32)],
        in_specs=[any_, any_, any_, any_, any_],
        out_specs=[any_, any_, any_],
        scratch_shapes=[
            pltpu.SMEM(inter.shape, F32),
            pltpu.VMEM((2, chunks, fields, SUB, LANES), F32),
            pltpu.VMEM((2, chunks, 6, SUB, LANES), F32),
            pltpu.VMEM((2, chunks, 4, SUB, LANES), F32),
            pltpu.VMEM((2, chunks, SUB, LANES), jnp.int32),
            pltpu.VMEM((2, chunks, 4 * REC, LANES), F32),
            pltpu.SemaphoreType.DMA((n_in + 4 * chunks,)),
        ],
        compiler_params=pltpu.CompilerParams(vmem_limit_bytes=VMEM_WIDE),
        cost_estimate=pl.CostEstimate(flops=1_000_000, bytes_accessed=4_000_000, transcendentals=0),
        name="pack",
    )(inter, vec, hop, pot, stk)


PAD = 8


def interior_kernel(rows, chunks, nvec, group, table, vec, hop, pot, stk, after, keep, send, tot,
                    inter, x, t1, t2, hp, pt, st, ww, mom, dots, sems):
    del after
    halves = nvec // group
    copies = [pltpu.make_async_copy(table, inter, sems.at[0])]
    n = 1
    for c in range(chunks):
        lanes = pl.ds(c * LANES, LANES)
        for src, dst in (
            (hop.at[:, :, :, lanes], hp.at[:, 0:3, c, pl.ds(0, rows)]),
            (pot.at[:, :, lanes], pt.at[:, c]),
            (stk.at[:, lanes], st.at[c]),
        ):
            copies.append(pltpu.make_async_copy(src, dst, sems.at[n]))
            n += 1
    late = []
    for q in range(halves):
        part = []
        for c in range(chunks):
            lanes = pl.ds(c * LANES, LANES)
            part.append(
                pltpu.make_async_copy(
                    vec.at[:, pl.ds(q * group, group), :, lanes],
                    x.at[:, pl.ds(q * group, group), c, pl.ds(PAD, rows)],
                    sems.at[n],
                )
            )
            n += 1
        late.append(part)
    for copy in copies + [copy for part in late for copy in part]:
        copy.start()
    for copy in copies:
        copy.wait()

    groups = rows // SUB

    def prepare(g, carry):
        at = pl.ds(pl.multiple_of(g * SUB, SUB), SUB)
        for layer in range(2):
            rolled = {}
            for c in range(chunks):
                rolled[c] = roll_left(hp[layer, 1, c, at, :])
            for c in range(chunks):
                hp[layer, 3, c, at, :] = (
                    from_right(rolled[c], rolled[(c + 1) % chunks]) * -0.25
                )
            for k in range(3):
                for c in range(chunks):
                    hp[layer, k, c, at, :] = hp[layer, k, c, at, :] * -0.25
        for c in range(chunks):
            for s in range(4):
                pt[s, c, at, :] = pt[s, c, at, :] * 0.25
            classes = st[c, at, :]
            for w in range(2):
                table = [inter[w, k] * 0.25 for k in range(inter.shape[1])]
                ww[w, c, at, :] = pick(classes, table)
        return carry

    lax.fori_loop(0, groups, prepare, 0)

    def sweep(order, q, source, before, target):
        def load(ref, s, v, c, at):
            return ref[s, v, c, at, :]

        def body(g, carry):
            base = pl.multiple_of(g * SUB, SUB)
            mid = pl.ds(base + PAD, SUB)
            up = pl.ds(base + PAD - 1, SUB)
            down = pl.ds(base + PAD + 1, SUB)
            plain = pl.ds(base, SUB)
            plain_down = pl.ds(base + 1, SUB)
            vs = range(group)
            src, off = source

            def rolled(site, c, fn):
                return [fn(load(src, site, v + off, c, mid)) for v in vs]

            products = [None] * 2
            b_prev = [rolled(2 * l + 1, chunks - 1, roll_right) for l in range(2)]
            a_here = [rolled(2 * l, 0, roll_left) for l in range(2)]
            for c in range(chunks):
                nxt = (c + 1) % chunks
                a_next = [rolled(2 * l, nxt, roll_left) for l in range(2)]
                b_here = [rolled(2 * l + 1, c, roll_right) for l in range(2)]
                coef = []
                for layer in range(2):
                    for k in range(4):
                        coef.append(hp[layer, k, c, plain, :])
                for s in range(4):
                    coef.append(pt[s, c, plain, :])
                for w in range(2):
                    coef.append(ww[w, c, plain, :])
                t2_down = [hp[layer, 2, c, plain_down, :] for layer in range(2)]
                sums = [None] * 4
                squares = [None] * 4
                for v in vs:
                    a = [load(src, 2 * l, v + off, c, mid) for l in range(2)]
                    b = [load(src, 2 * l + 1, v + off, c, mid) for l in range(2)]
                    a_down = [load(src, 2 * l, v + off, c, down) for l in range(2)]
                    b_up = [load(src, 2 * l + 1, v + off, c, up) for l in range(2)]
                    a_right = [from_right(a_here[l][v], a_next[l][v]) for l in range(2)]
                    b_left = [from_left(b_here[l][v], b_prev[l][v]) for l in range(2)]
                    new = hop_apply(a, b, a_right, b_left, a_down, b_up, coef, t2_down)
                    for s in range(4):
                        if order == 1:
                            value = new[s] * 0.5
                        else:
                            ref, shift = before
                            value = new[s] - load(ref, s, v + shift, c, mid)
                        if target is not None:
                            target[s, v, c, mid, :] = value
                        first = load(x, s, v + q * group, c, mid)
                        term = first * value
                        sums[s] = term if sums[s] is None else sums[s] + term
                        if order == 2:
                            prior = load(src, s, v + off, c, mid)
                            for k, pair in enumerate((prior * value, value * value)):
                                products[k] = pair if products[k] is None else products[k] + pair
                        if order == 1:
                            sq = first * first
                            squares[s] = sq if squares[s] is None else squares[s] + sq
                for s in range(4):
                    if q > 0:
                        sums[s] = sums[s] + mom[order, s, c, plain, :]
                    mom[order, s, c, plain, :] = sums[s]
                    if order == 1:
                        if q > 0:
                            squares[s] = squares[s] + mom[0, s, c, plain, :]
                        mom[0, s, c, plain, :] = squares[s]
                a_here = a_next
                b_prev = b_here
            if order == 2:
                row = lax.broadcasted_iota(jnp.int32, (SUB, LANES), 0) + base
                inside = (row >= 2) & (row < rows - 2)
                for k in range(2):
                    dots[k] = dots[k] + jnp.where(inside, products[k], 0.0)
            return carry

        lax.fori_loop(0, groups, body, 0, unroll=4)

    half = rows // 2
    core = place()[1]
    keep_at = pl.ds(pl.multiple_of(core * half, SUB), half)
    send_at = pl.ds(pl.multiple_of((1 - core) * half, SUB), half)
    outs = []

    def write_out(order):
        for rows_at, dst, k in ((keep_at, keep, 0), (send_at, send, 1)):
            copy = pltpu.make_async_copy(
                mom.at[order, :, :, rows_at], dst.at[order], sems.at[n + 2 * order + k]
            )
            copy.start()
            outs.append(copy)

    dots[...] = jnp.zeros_like(dots)
    for q in range(halves):
        for copy in late[q]:
            copy.wait()
        start = (x, q * group)
        steps = ((start, None, t1), ((t1, 0), start, t2), ((t2, 0), (t1, 0), t1), ((t1, 0), (t2, 0), None))
        for order, (source, before, target) in enumerate(steps, 1):
            sweep(order, q, source, before, target)
            if q == halves - 1:
                if order == 1:
                    write_out(0)
                write_out(order)

    def add_up(g, carry):
        base = pl.multiple_of(g * SUB, SUB)
        row = lax.broadcasted_iota(jnp.int32, (SUB, LANES), 0) + base
        inside = (row >= 2) & (row < rows - 2)
        result = []
        for m in range(3):
            acc = None
            for s in range(4):
                for c in range(chunks):
                    value = mom[m, s, c, pl.ds(base, SUB), :]
                    acc = value if acc is None else acc + value
            result.append(carry[m] + jnp.where(inside, acc, 0.0))
        return tuple(result)

    sums = lax.fori_loop(0, groups, add_up, tuple(jnp.zeros((SUB, LANES), F32) for _ in range(3)))
    for m in range(3):
        tot[m] = sums[m]
    for k in range(2):
        tot[3 + k] = dots[k]
    for copy in outs:
        copy.wait()


def interior(inter, vec, hop, pot, stk, after):
    _, nvec, rows, width = vec.shape
    chunks = width // LANES
    group = 2
    any_ = pl.BlockSpec(memory_space=pl.ANY)
    half = jax.ShapeDtypeStruct((CHEB + 1, 4, chunks, rows // 2, LANES), F32)
    n = 1 + chunks * (3 + nvec // group) + 2 * (CHEB + 1)
    return pl.pallas_call(
        functools.partial(interior_kernel, rows, chunks, nvec, group),
        out_shape=[half, half, jax.ShapeDtypeStruct((CHEB + 1, SUB, LANES), F32)],
        in_specs=[any_] * 6,
        out_specs=[any_, any_, pl.BlockSpec(memory_space=pltpu.VMEM)],
        scratch_shapes=[
            pltpu.SMEM(inter.shape, F32),
            pltpu.VMEM((4, nvec, chunks, rows + 2 * PAD, LANES), F32),
            pltpu.VMEM((4, group, chunks, rows + 2 * PAD, LANES), F32),
            pltpu.VMEM((4, group, chunks, rows + 2 * PAD, LANES), F32),
            pltpu.VMEM((2, 4, chunks, rows + SUB, LANES), F32),
            pltpu.VMEM((4, chunks, rows, LANES), F32),
            pltpu.VMEM((chunks, rows, LANES), jnp.int32),
            pltpu.VMEM((2, chunks, rows, LANES), F32),
            pltpu.VMEM((CHEB + 1, 4, chunks, rows, LANES), F32),
            pltpu.VMEM((2, SUB, LANES), F32),
            pltpu.SemaphoreType.DMA((n,)),
        ],
        compiler_params=pltpu.CompilerParams(vmem_limit_bytes=VMEM_WIDE),
        cost_estimate=pl.CostEstimate(
            flops=60_000_000, bytes_accessed=9_000_000, transcendentals=0
        ),
        name="interior",
    )(inter, vec, hop, pot, stk, after)


WIN = 7
GUARD = REC


def gather_window(refs, w, sems, part=None, dots=None, beside=()):
    own_long, own_short, got_long, got_short, extra = refs
    odd = place()[0]
    even = odd == 0
    copies = []

    def both(first, second, take, band, place_at, count):
        src_at, dst_at = pl.ds(take * REC, count * REC), pl.ds(GUARD + place_at * REC, count * REC)
        dst, sem = w.at[band, :, dst_at], sems.at[len(copies)]

        @pl.when(even)
        def _():
            pltpu.make_async_copy(first.at[:, src_at], dst, sem).start()

        @pl.when(jnp.logical_not(even))
        def _():
            pltpu.make_async_copy(second.at[:, src_at], dst, sem).start()

        copies.append(pltpu.make_async_copy(first.at[:, src_at], dst, sem))

    few = part is not None
    if few:
        both(got_long, got_short, 2, 0, 2, 1)
        both(got_short, got_long, 0, 1, 4, 1)
    else:
        both(got_long, got_short, 0, 0, 0, 3)
        both(got_short, got_long, 0, 1, 4, 3)
    both(own_long, own_short, 0, 0, 3, 3)
    both(own_short, own_long, 0, 1, 1, 3)
    if few:
        copy = pltpu.make_async_copy(part, dots, sems.at[len(copies)])
        copy.start()
        copies.append(copy)
    else:
        for band, place_at in ((0, 6), (1, 0)):
            copy = pltpu.make_async_copy(
                extra.at[band], w.at[band, :, pl.ds(GUARD + place_at * REC, REC)],
                sems.at[len(copies)],
            )
            copy.start()
            copies.append(copy)
    for copy in beside:
        copy.start()
    for copy in copies:
        copy.wait()


def window_slice(ref, is_w, band, c, i, site):
    start = GUARD + i * REC + site * SUB if is_w else (i + 1) * 32 + site * SUB
    return ref[band, c, pl.ds(pl.multiple_of(start, SUB), SUB), :]


def window_step(chunks, order, w, source, before, band, i, emit):
    from_w = order == 1

    def here(site, c, shift=0):
        return window_slice(source, from_w, band, c, i + shift, site)

    def coef_at(k, c, shift=0):
        at = GUARD + (i + shift) * REC + COEF + k
        return jnp.broadcast_to(w[band, c, pl.ds(at, 1), :], (SUB, LANES))

    b_prev = [roll_right(here(2 * l + 1, chunks - 1)) for l in range(2)]
    a_here = [roll_left(here(2 * l, 0)) for l in range(2)]
    for c in range(chunks):
        nxt = (c + 1) % chunks
        a_next = [roll_left(here(2 * l, nxt)) for l in range(2)]
        b_here = [roll_right(here(2 * l + 1, c)) for l in range(2)]
        coef = [coef_at(k, c) for k in range(14)]
        t2_down = [coef_at(4 * l + 2, c, 1) for l in range(2)]
        a = [here(2 * l, c) for l in range(2)]
        b = [here(2 * l + 1, c) for l in range(2)]
        a_down = [here(2 * l, c, 1) for l in range(2)]
        b_up = [here(2 * l + 1, c, -1) for l in range(2)]
        a_right = [from_right(a_here[l], a_next[l]) for l in range(2)]
        b_left = [from_left(b_here[l], b_prev[l]) for l in range(2)]
        new = hop_apply(a, b, a_right, b_left, a_down, b_up, coef, t2_down)
        for s in range(4):
            if order == 1:
                new[s] = new[s] * 0.5
            else:
                new[s] = new[s] - window_slice(before, order == 2, band, c, i, s)
        emit(c, new)
        a_here = a_next
        b_prev = b_here


def store_row(target, band, i):
    def emit(c, values):
        for s in range(4):
            at = pl.multiple_of((i + 1) * 32 + s * SUB, SUB)
            target[band, c, pl.ds(at, SUB), :] = values[s]

    return emit


def totals_kernel(chunks, parts, own_long, own_short, got_long, got_short, part, tot, w, t1, dots,
                  sems):
    gather_window((own_long, own_short, got_long, got_short, None), w, sems, part, dots)

    def first(j, carry):
        for band in range(2):
            i = 2 - band + j
            window_step(chunks, 1, w, w, None, band, i, store_row(t1, band, i))
        return carry

    lax.fori_loop(0, 4, first, 0, unroll=2)

    def second(j, carry):
        for band in range(2):
            i = 3 - band + j
            sums = [None] * 5

            def emit(c, values):
                for s in range(4):
                    zero = window_slice(w, True, band, c, i, s)
                    one = window_slice(t1, False, band, c, i, s)
                    two = values[s]
                    terms = (zero * zero, zero * one, zero * two, one * two, two * two)
                    for k, term in enumerate(terms):
                        sums[k] = term if sums[k] is None else sums[k] + term

            window_step(chunks, 2, w, t1, w, band, i, emit)
            for k in range(5):
                dots[k] = dots[k] + sums[k]
        return carry

    lax.fori_loop(0, 2, second, 0, unroll=2)
    lane = lax.broadcasted_iota(jnp.int32, (SUB, LANES), 1)
    row = jnp.zeros((SUB, LANES), F32)
    for m in range(5):
        row = jnp.where(lane == m, jnp.sum(dots[m]), row)
    for k in range(parts // SUB):
        tot[pl.ds(k * SUB, SUB), :] = row


def totals_of(records, part, parts):
    chunks = records[0].shape[0]
    any_ = pl.BlockSpec(memory_space=pl.ANY)
    vmem = pl.BlockSpec(memory_space=pltpu.VMEM)
    return pl.pallas_call(
        functools.partial(totals_kernel, chunks, parts),
        out_shape=jax.ShapeDtypeStruct((parts, LANES), F32),
        in_specs=[any_] * 5,
        out_specs=vmem,
        scratch_shapes=[
            pltpu.VMEM((2, chunks, (WIN + 2) * REC, LANES), F32),
            pltpu.VMEM((2, chunks, (WIN + 2) * 32, LANES), F32),
            pltpu.VMEM((5, SUB, LANES), F32),
            pltpu.SemaphoreType.DMA((5,)),
        ],
        compiler_params=pltpu.CompilerParams(vmem_limit_bytes=VMEM_WIDE),
        cost_estimate=pl.CostEstimate(flops=8_000_000, bytes_accessed=4_000_000, transcendentals=0),
        name="totals",
    )(*records[:4], part)


def edges_kernel(chunks, half, own_long, own_short, got_long, got_short, extra, mine_in, other_in,
                 after, out, w, t1, t2, res, mine, other, slab, sems):
    del after
    inner = [
        pltpu.make_async_copy(src, dst, sems.at[7 + k])
        for k, (src, dst) in enumerate(((mine_in, mine), (other_in, other)))
    ]
    gather_window((own_long, own_short, got_long, got_short, extra), w, sems, beside=inner)
    row = lax.broadcasted_iota(jnp.int32, (SUB, LANES), 0)
    single, double = (row & 1) != 0, (row & 2) != 0

    def merged(hit, a, b, shift):
        return jnp.where(hit, b, a) + pltpu.roll(jnp.where(hit, a, b), shift, 0)

    def moments(band, i, c, order, values):
        p = [window_slice(w, True, band, c, i, s) * values[s] for s in range(4)]
        pairs = [merged(single, p[2 * k], p[2 * k + 1], 1) for k in range(2)]
        both = merged(double, pairs[0], pairs[1], 2)
        both = both + pltpu.roll(both, 4, 0)
        res[band, i - 2, c, pl.ds(order * 4, 4), :] = both[0:4]

    def sweep(order, first, last):
        source, before, target = {
            1: (w, None, t1),
            2: (t1, w, t2),
            3: (t2, t1, t1),
            4: (t1, t2, None),
        }[order]

        def body(j, carry):
            i = first + j
            for band in range(2):
                if order < 4:
                    emit = store_row(target, band, i)
                else:
                    emit = lambda c, values, band=band: moments(band, i, c, 4, values)
                window_step(chunks, order, w, source, before, band, i, emit)
            return carry

        lax.fori_loop(0, last - first + 1, body, 0, unroll=1 if order == 4 else 2)

    def collect(order, ref):
        def body(j, carry):
            i = 2 + j
            for band in range(2):
                for c in range(chunks):
                    values = [window_slice(ref, ref is w, band, c, i, s) for s in range(4)]
                    moments(band, i, c, order, values)
            return carry

        lax.fori_loop(0, 3, body, 0)

    collect(0, w)
    sweep(1, 0, 6)
    collect(1, t1)
    sweep(2, 1, 5)
    collect(2, t2)
    sweep(3, 1, 5)
    collect(3, t1)
    sweep(4, 2, 4)
    for copy in inner:
        copy.wait()
    tall = 4 * half + SUB
    core = place()[1]

    def assemble(m, carry):
        for c in range(chunks):
            for s in range(4):
                for g in range(half // SUB):
                    at = pl.ds(g * SUB, SUB)
                    slab[m, pl.ds(c * tall + s * half + g * SUB, SUB), :] = (
                        mine[m, s, c, at, :] + other[m, s, c, at, :]
                    )
            for band, r in ((0, 0), (1, 2)):
                halo = res[band, r, c, pl.ds(4 * m, 4), :]
                slab[m, pl.ds(chunks * tall + band * SUB + c, 1), :] = jnp.sum(
                    halo, axis=0, keepdims=True
                )
            for r in range(2):
                upper = res[0, r + 1, c, pl.ds(4 * m, 4), :]
                lower = res[1, r, c, pl.ds(4 * m, 4), :]
                here = jnp.where(core == 0, upper, lower)
                place_at = jnp.where(core == 0, r, half - 2 + r)
                for s in range(4):
                    slab[m, pl.ds(c * tall + s * half + place_at, 1), :] = here[s : s + 1]
                slab[m, pl.ds(c * tall + 4 * half + 4 * r, 4), :] = jnp.where(
                    core == 0, lower, upper
                )
        return carry

    lax.fori_loop(0, CHEB + 1, assemble, 0)
    away = pltpu.make_async_copy(slab, out, sems.at[6])
    away.start()
    away.wait()


def edges(records, mine, other, after):
    _, _, chunks, half, _ = mine.shape
    slabs = (CHEB + 1, chunks * (4 * half + SUB) + 2 * SUB, LANES)
    any_ = pl.BlockSpec(memory_space=pl.ANY)
    return pl.pallas_call(
        functools.partial(edges_kernel, chunks, half),
        out_shape=jax.ShapeDtypeStruct(slabs, F32),
        in_specs=[any_] * 8,
        out_specs=any_,
        scratch_shapes=[
            pltpu.VMEM((2, chunks, (WIN + 2) * REC, LANES), F32),
            pltpu.VMEM((2, chunks, (WIN + 2) * 32, LANES), F32),
            pltpu.VMEM((2, chunks, (WIN + 2) * 32, LANES), F32),
            pltpu.VMEM((2, 3, chunks, 24, LANES), F32),
            pltpu.VMEM(mine.shape, F32),
            pltpu.VMEM(mine.shape, F32),
            pltpu.VMEM(slabs, F32),
            pltpu.SemaphoreType.DMA((9,)),
        ],
        compiler_params=pltpu.CompilerParams(vmem_limit_bytes=VMEM_WIDE),
        cost_estimate=pl.CostEstimate(
            flops=20_000_000, bytes_accessed=4_000_000, transcendentals=0
        ),
        name="edges",
    )(*records, mine, other, after)


ACOS = (
    1.5707963050,
    -0.2145988016,
    0.0889789874,
    -0.0501743046,
    0.0308918810,
    -0.0170881256,
    0.0066700901,
    -0.0012624911,
)


def arccos(e):
    size = jnp.abs(e)
    poly = jnp.full_like(size, ACOS[-1])
    for value in ACOS[-2::-1]:
        poly = poly * size + value
    angle = jnp.sqrt(1.0 - size) * poly
    return jnp.where(e < 0.0, math.pi - angle, angle)


def weights_of(e):
    gain = jackson(CHEB + 1)
    sine = jnp.sqrt((1.0 - e) * (1.0 + e))
    square = e * e
    sines = [sine, 2.0 * e * sine, (4.0 * square - 1.0) * sine, 4.0 * e * (2.0 * square - 1.0) * sine]
    out = [gain[0] * (1.0 - arccos(e) / math.pi)]
    for m in range(1, CHEB + 1):
        out.append(sines[m - 1] * (-2.0 * gain[m] / (math.pi * m)))
    return out


def density_kernel(scale, sites, filling, sums, slabs, out):
    added = jnp.sum(sums[...], axis=0, keepdims=True) * scale
    lane = lax.broadcasted_iota(jnp.int32, (1, LANES), 1)
    totals = [jnp.sum(jnp.where(lane == m, added, 0.0)) for m in range(CHEB + 1)]
    totals[3] = 2.0 * totals[3] - totals[1]
    totals[4] = 2.0 * totals[4] - totals[0]
    target = filling[0] * sites

    point = (
        lax.broadcasted_iota(jnp.int32, (SUB, LANES), 0) * LANES
        + lax.broadcasted_iota(jnp.int32, (SUB, LANES), 1)
        + 1
    )
    ways = 2 ** (BISECT // 2)
    valid = point < ways
    low = jnp.float32(-1.0)
    step = 2.0
    for _ in range(2):
        step = step / ways
        mids = jnp.where(valid, low + point.astype(F32) * step, 0.0)
        count = None
        for value, total in zip(weights_of(mids), totals):
            term = value * total
            count = term if count is None else count + term
        below = jnp.sum(jnp.where(valid & (count < target), 1.0, 0.0))
        low = low + below * step
    chem = jnp.full((SUB, LANES), low + 0.5 * step, F32)
    weights = [value * scale for value in weights_of(chem)]
    for k in range(out.shape[0] // SUB):
        at = pl.ds(k * SUB, SUB)
        acc = None
        for m in range(CHEB + 1):
            term = weights[m] * slabs[m, at, :]
            acc = term if acc is None else acc + term
        out[at, :] = acc


def density(filling, sums, slabs, vectors, sites):
    smem = pl.BlockSpec(memory_space=pltpu.SMEM)
    vmem = pl.BlockSpec(memory_space=pltpu.VMEM)
    return pl.pallas_call(
        functools.partial(density_kernel, 1.0 / vectors, float(sites)),
        out_shape=jax.ShapeDtypeStruct(slabs.shape[1:], F32),
        in_specs=[smem, vmem, vmem],
        out_specs=vmem,
        compiler_params=pltpu.CompilerParams(vmem_limit_bytes=VMEM_LIMIT),
        cost_estimate=pl.CostEstimate(flops=2_000_000, bytes_accessed=4_000_000, transcendentals=0),
        name="density",
    )(filling, sums, slabs)


def potential_kernel(chunks, half, mine, other, out, dens, charge):
    first = place()[1] == 0
    tall = 4 * half + SUB
    guard = SUB

    for c in range(chunks):
        for s in range(4):
            at = pl.ds(c * tall + s * half, half)
            m, o = mine[at, :], other[at, :]
            dens[s, c, pl.ds(0, half), :] = jnp.where(first, m, o)
            dens[s, c, pl.ds(half, half), :] = jnp.where(first, o, m)
        at = pl.ds(c * tall + 4 * half, SUB)
        m, o = mine[at, :], other[at, :]
        upper, lower = jnp.where(first, o, m), jnp.where(first, m, o)
        for r in range(2):
            for s in range(4):
                k = 4 * r + s
                for row, more in ((r, upper), (2 * half - 2 + r, lower)):
                    dens[s, c, pl.ds(row, 1), :] = dens[s, c, pl.ds(row, 1), :] + more[k : k + 1]
        for g in range(2 * half // SUB):
            at = pl.ds(g * SUB, SUB)
            total = (dens[0, c, at, :] + dens[1, c, at, :]) + (dens[2, c, at, :] + dens[3, c, at, :])
            charge[c, pl.ds(guard + g * SUB, SUB), :] = total - 2.0
        for band, row in ((0, guard - 1), (1, guard + 2 * half)):
            at = pl.ds(chunks * tall + band * SUB + c, 1)
            charge[c, pl.ds(row, 1), :] = mine[at, :] + other[at, :] - 2.0
    for g in range(2 * half // SUB):
        at = pl.ds(guard + g * SUB, SUB)
        for c in range(chunks):
            here = charge[c, at, :]
            left = from_left(roll_right(here), roll_right(charge[(c - 1) % chunks, at, :]))
            right = from_right(roll_left(here), roll_left(charge[(c + 1) % chunks, at, :]))
            near = (
                charge[c, pl.ds(guard + g * SUB - 1, SUB), :]
                + charge[c, pl.ds(guard + g * SUB + 1, SUB), :]
                + left
                + right
            )
            base = 0.5 * here + 0.25 * near
            for s in range(4):
                value = dens[s, c, pl.ds(g * SUB, SUB), :]
                out[s, pl.ds(g * SUB, SUB), pl.ds(c * LANES, LANES)] = 3.0 * (value - 0.5) + base


def new_potential(mine, other, chunks):
    half = ((mine.shape[0] - 2 * SUB) // chunks - SUB) // 4
    vmem = pl.BlockSpec(memory_space=pltpu.VMEM)
    return pl.pallas_call(
        functools.partial(potential_kernel, chunks, half),
        out_shape=jax.ShapeDtypeStruct((4, 2 * half, chunks * LANES), F32),
        in_specs=[vmem, vmem],
        out_specs=vmem,
        scratch_shapes=[
            pltpu.VMEM((4, chunks, 2 * half, LANES), F32),
            pltpu.VMEM((chunks, 2 * half + 2 * SUB, LANES), F32),
        ],
        compiler_params=pltpu.CompilerParams(vmem_limit_bytes=VMEM_LIMIT),
        cost_estimate=pl.CostEstimate(flops=1_000_000, bytes_accessed=2_000_000, transcendentals=0),
        name="new_potential",
    )(mine, other)


def per_device(vectors, hoppings, potential, stacking, interlayer, filling):
    strips, ranks = lax.axis_size("dom"), lax.axis_size("vec")
    _, nvec, rows, width = vectors.shape
    long_way = [(i, (i - 1 if i % 2 == 0 else i + 1) % strips) for i in range(strips)]
    short_way = [(i, i ^ 1) for i in range(strips)]
    sibling = [(i, i ^ 1) for i in range(ranks)]
    across = [(i, i ^ 2) for i in range(ranks)]

    own_long, own_short, extra = pack(
        interlayer,
        vectors.reshape(4 * nvec, rows, width),
        hoppings.reshape(6, rows, width),
        potential,
        stacking,
    )
    got_long = lax.ppermute(own_long, "dom", long_way)
    got_short = lax.ppermute(own_short, "dom", short_way)
    mine, yours, part = interior(interlayer, vectors, hoppings, potential, stacking, own_short)
    records = (own_long, own_short, got_long, got_short, extra)
    totals = totals_of(records, part, strips * ranks)
    yours, ready = lax.optimization_barrier((yours, totals))
    other = lax.ppermute(yours, "vec", sibling)
    slabs = edges(records, mine, other, totals)
    sums = lax.all_to_all(ready, ("dom", "vec"), 0, 0, tiled=True)
    sites = 4 * rows * width * strips
    chip = density(filling, sums, slabs, nvec * ranks, sites)
    whole = chip + lax.ppermute(chip, "vec", across)
    return new_potential(whole, lax.ppermute(whole, "vec", sibling), width // LANES)


def solution(mesh):
    placed = (
        P(None, "vec", "dom", None),
        P(None, None, "dom", None),
        P(None, "dom", None),
        P("dom", None),
        P(),
        P(),
    )
    return jax.shard_map(
        per_device, mesh=mesh, in_specs=placed, out_specs=P(None, "dom", None), check_vma=False
    )
```

```python
import functools
import math

import jax
import jax.numpy as jnp
from jax import lax
from jax.experimental import pallas as pl
from jax.experimental.pallas import tpu as pltpu
from jax.sharding import PartitionSpec as P

CHEB = 4
BISECT = 16
LANES = 128
SUB = 8
REC = 48
COEF = 32
F32 = jnp.float32
VMEM_LIMIT = 44 * 1024 * 1024
VMEM_WIDE = 64 * 1024 * 1024 - 256 * 1024
SLOT = (0, 3, 5, 8, 1, 4, 6, 9, 10, 12, 11, 13, 7, 2)
FAR = COEF + 8
NEAR = 2 * REC
MESSAGE = NEAR + FAR
EXTRA = REC + 8


def jackson(count):
    angle = math.pi / (count + 1)
    return [
        ((count - m + 1) * math.cos(angle * m) + math.sin(angle * m) / math.tan(angle))
        / (count + 1)
        for m in range(count)
    ]


def lane_is(where, shape=(SUB, LANES)):
    return lax.broadcasted_iota(jnp.int32, shape, 1) == where


def from_left(here, left):
    return jnp.where(lane_is(0, here.shape), left, here)


def from_right(here, right):
    return jnp.where(lane_is(LANES - 1, here.shape), right, here)


def roll_left(x):
    return pltpu.roll(x, LANES - 1, 1)


def roll_right(x):
    return pltpu.roll(x, 1, 1)


def pick(classes, table):
    values = list(table)
    bit = 1
    while len(values) > 1:
        hit = (classes & bit) != 0
        values = [jnp.where(hit, values[i + 1], values[i]) for i in range(0, len(values), 2)]
        bit *= 2
    return values[0]


def hop_apply(a, b, a_right, b_left, a_down, b_up, coef, t2_down):
    pot = coef[8:12]
    aa, ab = coef[12:14]
    out = []
    for layer in range(2):
        t0, t1, t2, t1r = coef[4 * layer : 4 * layer + 4]
        h_a = t0 * b[layer] + t1 * b_left[layer] + t2 * b_up[layer] + pot[2 * layer] * a[layer]
        h_b = (
            t0 * a[layer]
            + t1r * a_right[layer]
            + t2_down[layer] * a_down[layer]
            + pot[2 * layer + 1] * b[layer]
        )
        out.append([h_a, h_b])
    out[0][0] = out[0][0] + aa * a[1] + ab * b[1]
    out[1][0] = out[1][0] + aa * a[0]
    out[1][1] = out[1][1] + ab * a[0]
    return [out[0][0], out[0][1], out[1][0], out[1][1]]


def place():
    return lax.rem(lax.axis_index("dom"), 2), lax.rem(lax.axis_index("vec"), 2)


def pack_kernel(rows, chunks, table, vec, hop, pot, stk, long_out, short_out, extra, inter, v8, h8,
                p8, s8, rec, sems):
    copies = [pltpu.make_async_copy(table, inter, sems.at[0])]
    n = 1
    for band in range(2):
        at = pl.ds(band * (rows - SUB), SUB)
        for c in range(chunks):
            lanes = pl.ds(c * LANES, LANES)
            for src, dst in (
                (hop.at[:, at, lanes], h8.at[band, c]),
                (pot.at[:, at, lanes], p8.at[band, c]),
                (stk.at[at, lanes], s8.at[band, c]),
                (vec.at[:, at, lanes], v8.at[band, c]),
            ):
                copies.append(pltpu.make_async_copy(src, dst, sems.at[n]))
                n += 1
    for copy in copies:
        copy.start()
    nf = vec.shape[0]
    flat = v8.reshape(2, chunks, nf * SUB, LANES)
    odd = place()[0]
    outs = []
    copies[0].wait()
    waited = set()

    def wait_tile(band, c):
        if (band, c) not in waited:
            waited.add((band, c))
            for copy in copies[1 + 4 * (chunks * band + c) :][:4]:
                copy.wait()

    for band in range(2):
        for c in range(chunks):
            wait_tile(band, c)
            first = 0 if band == 0 else SUB - 4
            for r in range(4):
                for s in range(nf // SUB):
                    rec[band, c, pl.ds(r * REC + s * SUB, SUB), :] = flat[
                        band, c, pl.ds(s * SUB * SUB + first + r, SUB, stride=SUB), :
                    ]
            after = (c + 1) % chunks
            wait_tile(band, after)
            coef = []
            for layer in range(2):
                for k in range(3):
                    coef.append(h8[band, c, 3 * layer + k] * -0.25)
                    if k == 1:
                        here = h8[band, c, 3 * layer + 1]
                        there = h8[band, after, 3 * layer + 1]
                        shifted = from_right(roll_left(here), roll_left(there)) * -0.25
                coef.append(shifted)
            for s in range(4):
                coef.append(p8[band, c, s] * 0.25)
            classes = s8[band, c]
            for w in range(2):
                table = [inter[w, k] * 0.25 for k in range(inter.shape[1])]
                coef.append(pick(classes, table))
            for k, value in enumerate(coef):
                at = pl.ds(COEF + SLOT[k], 4, stride=REC)
                rec[band, c, at, :] = value[first : first + 4]
            zero = jnp.zeros((4, LANES), F32)
            for k in range(len(coef), REC - COEF):
                rec[band, c, pl.ds(COEF + k, 4, stride=REC), :] = zero
            third = (2, 5)[band]
            for r, slot, k in (
                ((0, 14, 8), (0, 15, 10)),
                ((2, 14, 3), (2, 15, 7), (3, 14, 9), (3, 15, 11)),
            )[band]:
                rec[band, c, pl.ds(r * REC + COEF + slot, 1), :] = coef[k][third : third + 1]
            third_at = (2, 1)[band] * REC
            parts = (
                (pl.ds((0, 2)[band] * REC, NEAR), pl.ds(0, NEAR)),
                (pl.ds(third_at, FAR), pl.ds(NEAR, FAR)),
            )
            for src_at, dst_at in (
                (pl.ds((1 - band) * 3 * REC, REC), pl.ds(0, REC)),
                (pl.ds(third_at + FAR, REC - FAR), pl.ds(REC, REC - FAR)),
            ):
                away = pltpu.make_async_copy(
                    rec.at[band, c, src_at], extra.at[band, c, dst_at], sems.at[n]
                )
                away.start()
                outs.append(away)
                n += 1
            for src_at, dst_at in parts:
                src, sem = rec.at[band, c, src_at], sems.at[n]

                @pl.when(odd == band)
                def _():
                    pltpu.make_async_copy(src, long_out.at[c, dst_at], sem).start()

                @pl.when(odd != band)
                def _():
                    pltpu.make_async_copy(src, short_out.at[c, dst_at], sem).start()

                outs.append(pltpu.make_async_copy(src, long_out.at[c, dst_at], sem))
                n += 1
    for copy in outs:
        copy.wait()


def pack(inter, vec, hop, pot, stk):
    fields, rows, width = vec.shape
    chunks = width // LANES
    any_ = pl.BlockSpec(memory_space=pl.ANY)
    message = jax.ShapeDtypeStruct((chunks, MESSAGE, LANES), F32)
    n_in = 2 * chunks * 4 + 1
    return pl.pallas_call(
        functools.partial(pack_kernel, rows, chunks),
        out_shape=[message, message, jax.ShapeDtypeStruct((2, chunks, EXTRA, LANES), F32)],
        in_specs=[any_, any_, any_, any_, any_],
        out_specs=[any_, any_, any_],
        scratch_shapes=[
            pltpu.SMEM(inter.shape, F32),
            pltpu.VMEM((2, chunks, fields, SUB, LANES), F32),
            pltpu.VMEM((2, chunks, 6, SUB, LANES), F32),
            pltpu.VMEM((2, chunks, 4, SUB, LANES), F32),
            pltpu.VMEM((2, chunks, SUB, LANES), jnp.int32),
            pltpu.VMEM((2, chunks, 4 * REC, LANES), F32),
            pltpu.SemaphoreType.DMA((n_in + 8 * chunks,)),
        ],
        compiler_params=pltpu.CompilerParams(vmem_limit_bytes=VMEM_WIDE),
        cost_estimate=pl.CostEstimate(flops=1_000_000, bytes_accessed=4_000_000, transcendentals=0),
        name="pack",
    )(inter, vec, hop, pot, stk)


PAD = 8


def interior_kernel(rows, chunks, nvec, group, table, vec, hop, pot, stk, after, keep, send, tot,
                    inter, x, t1, t2, hp, pt, st, ww, mom, dots, ends, sems):
    del after
    halves = nvec // group
    copies = [pltpu.make_async_copy(table, inter, sems.at[0])]
    n = 1
    for c in range(chunks):
        lanes = pl.ds(c * LANES, LANES)
        for src, dst in (
            (hop.at[:, :, :, lanes], hp.at[:, 0:3, c, pl.ds(0, rows)]),
            (pot.at[:, :, lanes], pt.at[:, c]),
            (stk.at[:, lanes], st.at[c]),
        ):
            copies.append(pltpu.make_async_copy(src, dst, sems.at[n]))
            n += 1
    late = []
    for q in range(halves):
        part = []
        for c in range(chunks):
            lanes = pl.ds(c * LANES, LANES)
            part.append(
                pltpu.make_async_copy(
                    vec.at[:, pl.ds(q * group, group), :, lanes],
                    x.at[:, pl.ds(q * group, group), c, pl.ds(PAD, rows)],
                    sems.at[n],
                )
            )
            n += 1
        late.append(part)
    for copy in copies + [copy for part in late for copy in part]:
        copy.start()
    for copy in copies:
        copy.wait()

    groups = rows // SUB

    def prepare(g, carry):
        at = pl.ds(pl.multiple_of(g * SUB, SUB), SUB)
        for layer in range(2):
            rolled = {}
            for c in range(chunks):
                rolled[c] = roll_left(hp[layer, 1, c, at, :])
            for c in range(chunks):
                hp[layer, 3, c, at, :] = (
                    from_right(rolled[c], rolled[(c + 1) % chunks]) * -0.25
                )
            for k in range(3):
                for c in range(chunks):
                    hp[layer, k, c, at, :] = hp[layer, k, c, at, :] * -0.25
        for c in range(chunks):
            for s in range(4):
                pt[s, c, at, :] = pt[s, c, at, :] * 0.25
            classes = st[c, at, :]
            for w in range(2):
                table = [inter[w, k] * 0.25 for k in range(inter.shape[1])]
                ww[w, c, at, :] = pick(classes, table)
        return carry

    lax.fori_loop(0, groups, prepare, 0)

    def sweep(order, q, source, before, target):
        def load(ref, s, v, c, at):
            return ref[s, v, c, at, :]

        def body(g, carry):
            base = pl.multiple_of(g * SUB, SUB)
            mid = pl.ds(base + PAD, SUB)
            up = pl.ds(base + PAD - 1, SUB)
            down = pl.ds(base + PAD + 1, SUB)
            plain = pl.ds(base, SUB)
            plain_down = pl.ds(base + 1, SUB)
            vs = range(group)
            src, off = source

            def rolled(site, c, fn):
                return [fn(load(src, site, v + off, c, mid)) for v in vs]

            products = [None] * 2
            b_prev = [rolled(2 * l + 1, chunks - 1, roll_right) for l in range(2)]
            a_here = [rolled(2 * l, 0, roll_left) for l in range(2)]
            for c in range(chunks):
                nxt = (c + 1) % chunks
                a_next = [rolled(2 * l, nxt, roll_left) for l in range(2)]
                b_here = [rolled(2 * l + 1, c, roll_right) for l in range(2)]
                coef = []
                for layer in range(2):
                    for k in range(4):
                        coef.append(hp[layer, k, c, plain, :])
                for s in range(4):
                    coef.append(pt[s, c, plain, :])
                for w in range(2):
                    coef.append(ww[w, c, plain, :])
                t2_down = [hp[layer, 2, c, plain_down, :] for layer in range(2)]
                sums = [None] * 4
                squares = [None] * 4
                for v in vs:
                    a = [load(src, 2 * l, v + off, c, mid) for l in range(2)]
                    b = [load(src, 2 * l + 1, v + off, c, mid) for l in range(2)]
                    a_down = [load(src, 2 * l, v + off, c, down) for l in range(2)]
                    b_up = [load(src, 2 * l + 1, v + off, c, up) for l in range(2)]
                    a_right = [from_right(a_here[l][v], a_next[l][v]) for l in range(2)]
                    b_left = [from_left(b_here[l][v], b_prev[l][v]) for l in range(2)]
                    new = hop_apply(a, b, a_right, b_left, a_down, b_up, coef, t2_down)
                    for s in range(4):
                        if order == 1:
                            value = new[s] * 0.5
                        elif order == CHEB:
                            value = new[s]
                        else:
                            ref, shift = before
                            value = new[s] - load(ref, s, v + shift, c, mid)
                        if target is not None:
                            target[s, v, c, mid, :] = value
                        first = load(x, s, v + q * group, c, mid)
                        term = first * value
                        sums[s] = term if sums[s] is None else sums[s] + term
                        if order == 2:
                            prior = load(src, s, v + off, c, mid)
                            for k, pair in enumerate((prior * value, value * value)):
                                products[k] = pair if products[k] is None else products[k] + pair
                        if order == 1:
                            sq = first * first
                            squares[s] = sq if squares[s] is None else squares[s] + sq
                for s in range(4):
                    if q > 0:
                        sums[s] = sums[s] + mom[order, s, c, plain, :]
                    if order == CHEB and q == halves - 1:
                        sums[s] = sums[s] - mom[order - 2, s, c, plain, :]
                    mom[order, s, c, plain, :] = sums[s]
                    if order == 1:
                        if q > 0:
                            squares[s] = squares[s] + mom[0, s, c, plain, :]
                        mom[0, s, c, plain, :] = squares[s]
                a_here = a_next
                b_prev = b_here
            if order == 2:
                row = lax.broadcasted_iota(jnp.int32, (SUB, LANES), 0) + base
                inside = (row >= 2) & (row < rows - 2)
                for k in range(2):
                    dots[k] = dots[k] + jnp.where(inside, products[k], 0.0)
            return carry

        lax.fori_loop(0, groups, body, 0, unroll=4)

    half = rows // 2
    core = place()[1]
    keep_at = pl.ds(pl.multiple_of(core * half, SUB), half)
    send_at = pl.ds(pl.multiple_of((1 - core) * half, SUB), half)
    outs = []

    def write_out(order):
        for rows_at, dst, k in ((keep_at, keep, 0), (send_at, send, 1)):
            copy = pltpu.make_async_copy(
                mom.at[order, :, :, rows_at], dst.at[order], sems.at[n + 2 * order + k]
            )
            copy.start()
            outs.append(copy)

    dots[...] = jnp.zeros_like(dots)
    for q in range(halves):
        for copy in late[q]:
            copy.wait()
        start = (x, q * group)
        steps = ((start, None, t1), ((t1, 0), start, t2), ((t2, 0), (t1, 0), t1), ((t1, 0), (t2, 0), None))
        for order, (source, before, target) in enumerate(steps, 1):
            sweep(order, q, source, before, target)
            if q == halves - 1:
                if order == 1:
                    write_out(0)
                write_out(order)

    def add_up(g, carry):
        base = pl.multiple_of(g * SUB, SUB)
        row = lax.broadcasted_iota(jnp.int32, (SUB, LANES), 0) + base
        inside = (row >= 2) & (row < rows - 2)
        result = []
        for m in range(3):
            acc = None
            for s in range(4):
                for c in range(chunks):
                    value = mom[m, s, c, pl.ds(base, SUB), :]
                    acc = value if acc is None else acc + value
            result.append(carry[m] + jnp.where(inside, acc, 0.0))
        return tuple(result)

    sums = lax.fori_loop(0, groups, add_up, tuple(jnp.zeros((SUB, LANES), F32) for _ in range(3)))
    for m in range(3):
        ends[m] = sums[m]
    for k in range(2):
        ends[3 + k] = dots[k]
    last = pltpu.make_async_copy(ends, tot, sems.at[n + 2 * (CHEB + 1)])
    last.start()
    outs.append(last)
    for copy in outs:
        copy.wait()


def interior(inter, vec, hop, pot, stk, after):
    _, nvec, rows, width = vec.shape
    chunks = width // LANES
    group = 2
    any_ = pl.BlockSpec(memory_space=pl.ANY)
    half = jax.ShapeDtypeStruct((CHEB + 1, 4, chunks, rows // 2, LANES), F32)
    n = 2 + chunks * (3 + nvec // group) + 2 * (CHEB + 1)
    return pl.pallas_call(
        functools.partial(interior_kernel, rows, chunks, nvec, group),
        out_shape=[half, half, jax.ShapeDtypeStruct((CHEB + 1, SUB, LANES), F32)],
        in_specs=[any_] * 6,
        out_specs=[any_, any_, any_],
        scratch_shapes=[
            pltpu.SMEM(inter.shape, F32),
            pltpu.VMEM((4, nvec, chunks, rows + 2 * PAD, LANES), F32),
            pltpu.VMEM((4, group, chunks, rows + 2 * PAD, LANES), F32),
            pltpu.VMEM((4, group, chunks, rows + 2 * PAD, LANES), F32),
            pltpu.VMEM((2, 4, chunks, rows + SUB, LANES), F32),
            pltpu.VMEM((4, chunks, rows, LANES), F32),
            pltpu.VMEM((chunks, rows, LANES), jnp.int32),
            pltpu.VMEM((2, chunks, rows, LANES), F32),
            pltpu.VMEM((CHEB + 1, 4, chunks, rows, LANES), F32),
            pltpu.VMEM((2, SUB, LANES), F32),
            pltpu.VMEM((CHEB + 1, SUB, LANES), F32),
            pltpu.SemaphoreType.DMA((n,)),
        ],
        compiler_params=pltpu.CompilerParams(vmem_limit_bytes=VMEM_WIDE),
        cost_estimate=pl.CostEstimate(
            flops=60_000_000, bytes_accessed=9_000_000, transcendentals=0
        ),
        name="interior",
    )(inter, vec, hop, pot, stk, after)


WIN = 7
GUARD = REC


def gather_window(refs, w, sems, part=None, dots=None, share=None, filling=None, beside=()):
    own_long, own_short, got_long, got_short, extra = refs
    odd = place()[0]
    even = odd == 0
    copies = []

    def both(first, second, band, src_at, dst_at):
        dst, sem = w.at[band, :, dst_at], sems.at[len(copies)]

        @pl.when(even)
        def _():
            pltpu.make_async_copy(first.at[:, src_at], dst, sem).start()

        @pl.when(jnp.logical_not(even))
        def _():
            pltpu.make_async_copy(second.at[:, src_at], dst, sem).start()

        copies.append(pltpu.make_async_copy(first.at[:, src_at], dst, sem))

    def at(record, size):
        return pl.ds(GUARD + record * REC, size)

    few = part is not None
    if few:
        both(got_long, got_short, 0, pl.ds(REC, REC), at(2, REC))
        both(got_short, got_long, 1, pl.ds(0, REC), at(4, REC))
    else:
        both(got_long, got_short, 0, pl.ds(0, NEAR), at(1, NEAR))
        both(got_short, got_long, 1, pl.ds(0, NEAR), at(4, NEAR))
        both(got_long, got_short, 0, pl.ds(NEAR, FAR), at(0, FAR))
        both(got_short, got_long, 1, pl.ds(NEAR, FAR), at(6, FAR))
    both(own_long, own_short, 0, pl.ds(0, NEAR), at(3, NEAR))
    both(own_short, own_long, 1, pl.ds(0, NEAR), at(2, NEAR))
    both(own_long, own_short, 0, pl.ds(NEAR, FAR), at(5, FAR))
    both(own_short, own_long, 1, pl.ds(NEAR, FAR), at(1, FAR))
    plain = [
        (extra.at[0, :, pl.ds(REC, REC - FAR)], w.at[0, :, pl.ds(GUARD + 5 * REC + FAR, REC - FAR)]),
        (extra.at[1, :, pl.ds(REC, REC - FAR)], w.at[1, :, pl.ds(GUARD + REC + FAR, REC - FAR)]),
    ]
    if few:
        plain.extend(((part, dots), (share, filling)))
    else:
        plain.append((extra.at[0, :, pl.ds(0, REC)], w.at[0, :, at(6, REC)]))
        plain.append((extra.at[1, :, pl.ds(0, REC)], w.at[1, :, at(0, REC)]))
    for src, dst in plain:
        copy = pltpu.make_async_copy(src, dst, sems.at[len(copies)])
        copy.start()
        copies.append(copy)
    for copy in copies:
        copy.wait()
    for copy in beside:
        copy.start()
    if not few:
        for band, r, slot, to, to_slot in ((0, 1, 14, 0, 8), (0, 2, 14, 0, 12), (1, 4, 14, 6, 10)):
            for c in range(w.shape[1]):
                w[band, c, pl.ds(GUARD + to * REC + COEF + to_slot, 2), :] = w[
                    band, c, pl.ds(GUARD + r * REC + COEF + slot, 2), :
                ]


def window_slice(ref, is_w, band, c, i, site):
    start = GUARD + i * REC + site * SUB if is_w else (i + 1) * 32 + site * SUB
    return ref[band, c, pl.ds(pl.multiple_of(start, SUB), SUB), :]


def window_step(chunks, order, w, source, before, band, i, emit):
    from_w = order == 1

    def here(site, c, shift=0):
        return window_slice(source, from_w, band, c, i + shift, site)

    def coef_at(k, c, shift=0):
        at = GUARD + (i + shift) * REC + COEF + SLOT[k]
        return jnp.broadcast_to(w[band, c, pl.ds(at, 1), :], (SUB, LANES))

    b_prev = [roll_right(here(2 * l + 1, chunks - 1)) for l in range(2)]
    a_here = [roll_left(here(2 * l, 0)) for l in range(2)]
    for c in range(chunks):
        nxt = (c + 1) % chunks
        a_next = [roll_left(here(2 * l, nxt)) for l in range(2)]
        b_here = [roll_right(here(2 * l + 1, c)) for l in range(2)]
        coef = [coef_at(k, c) for k in range(14)]
        t2_down = [coef_at(4 * l + 2, c, 1) for l in range(2)]
        a = [here(2 * l, c) for l in range(2)]
        b = [here(2 * l + 1, c) for l in range(2)]
        a_down = [here(2 * l, c, 1) for l in range(2)]
        b_up = [here(2 * l + 1, c, -1) for l in range(2)]
        a_right = [from_right(a_here[l], a_next[l]) for l in range(2)]
        b_left = [from_left(b_here[l], b_prev[l]) for l in range(2)]
        new = hop_apply(a, b, a_right, b_left, a_down, b_up, coef, t2_down)
        for s in range(4):
            if order == 1:
                new[s] = new[s] * 0.5
            else:
                new[s] = new[s] - window_slice(before, order == 2, band, c, i, s)
        emit(c, new)
        a_here = a_next
        b_prev = b_here


def store_row(target, band, i):
    def emit(c, values):
        for s in range(4):
            at = pl.multiple_of((i + 1) * 32 + s * SUB, SUB)
            target[band, c, pl.ds(at, SUB), :] = values[s]

    return emit


def totals_kernel(chunks, parts, own_long, own_short, got_long, got_short, extra, part, share, tot,
                  w, t1, dots, filling, sems):
    records = (own_long, own_short, got_long, got_short, extra)
    gather_window(records, w, sems, part, dots, share, filling)

    def first(j, carry):
        for band in range(2):
            i = 2 - band + j
            window_step(chunks, 1, w, w, None, band, i, store_row(t1, band, i))
        return carry

    lax.fori_loop(0, 4, first, 0, unroll=2)

    def second(j, carry):
        for band in range(2):
            i = 3 - band + j
            sums = [None] * 5

            def emit(c, values):
                for s in range(4):
                    zero = window_slice(w, True, band, c, i, s)
                    one = window_slice(t1, False, band, c, i, s)
                    two = values[s]
                    terms = (zero * zero, zero * one, zero * two, one * two, two * two)
                    for k, term in enumerate(terms):
                        sums[k] = term if sums[k] is None else sums[k] + term

            window_step(chunks, 2, w, t1, w, band, i, emit)
            for k in range(5):
                dots[k] = dots[k] + sums[k]
        return carry

    lax.fori_loop(0, 2, second, 0, unroll=2)
    lane = lax.broadcasted_iota(jnp.int32, (SUB, LANES), 1)
    row = jnp.zeros((SUB, LANES), F32)
    for m in range(5):
        row = jnp.where(lane == m, jnp.sum(dots[m]), row)
    row = jnp.where(lane == 5, filling[0], row)
    for k in range(parts // SUB):
        tot[pl.ds(k * SUB, SUB), :] = row


def totals_of(records, part, filling, parts):
    chunks = records[0].shape[0]
    any_ = pl.BlockSpec(memory_space=pl.ANY)
    vmem = pl.BlockSpec(memory_space=pltpu.VMEM)
    return pl.pallas_call(
        functools.partial(totals_kernel, chunks, parts),
        out_shape=jax.ShapeDtypeStruct((parts, LANES), F32),
        in_specs=[any_] * 7,
        out_specs=vmem,
        scratch_shapes=[
            pltpu.VMEM((2, chunks, (WIN + 2) * REC, LANES), F32),
            pltpu.VMEM((2, chunks, (WIN + 2) * 32, LANES), F32),
            pltpu.VMEM((5, SUB, LANES), F32),
            pltpu.SMEM((1,), F32),
            pltpu.SemaphoreType.DMA((10,)),
        ],
        compiler_params=pltpu.CompilerParams(vmem_limit_bytes=VMEM_WIDE),
        cost_estimate=pl.CostEstimate(flops=8_000_000, bytes_accessed=4_000_000, transcendentals=0),
        name="totals",
    )(*records, part, filling)


def edges_kernel(chunks, half, own_long, own_short, got_long, got_short, extra, mine_in, other_in,
                 after, out, w, t1, t2, res, mine, other, slab, sems):
    del after
    inner = [
        pltpu.make_async_copy(src, dst, sems.at[12 + k])
        for k, (src, dst) in enumerate(((mine_in, mine), (other_in, other)))
    ]
    gather_window((own_long, own_short, got_long, got_short, extra), w, sems, beside=inner)
    row = lax.broadcasted_iota(jnp.int32, (SUB, LANES), 0)
    single, double = (row & 1) != 0, (row & 2) != 0

    def merged(hit, a, b, shift):
        return jnp.where(hit, b, a) + pltpu.roll(jnp.where(hit, a, b), shift, 0)

    def moments(band, i, c, order, values):
        p = [window_slice(w, True, band, c, i, s) * values[s] for s in range(4)]
        pairs = [merged(single, p[2 * k], p[2 * k + 1], 1) for k in range(2)]
        both = merged(double, pairs[0], pairs[1], 2)
        both = both + pltpu.roll(both, 4, 0)
        res[band, i - 2, c, pl.ds(order * 4, 4), :] = both[0:4]

    def sweep(order, first, last):
        source, before, target = {
            1: (w, None, t1),
            2: (t1, w, t2),
            3: (t2, t1, t1),
            4: (t1, t2, None),
        }[order]

        def body(j, carry):
            i = first + j
            for band in range(2):
                if order < 4:
                    emit = store_row(target, band, i)
                else:
                    emit = lambda c, values, band=band: moments(band, i, c, 4, values)
                window_step(chunks, order, w, source, before, band, i, emit)
            return carry

        lax.fori_loop(0, last - first + 1, body, 0, unroll=1 if order == 4 else 2)

    def collect(order, ref):
        def body(j, carry):
            i = 2 + j
            for band in range(2):
                for c in range(chunks):
                    values = [window_slice(ref, ref is w, band, c, i, s) for s in range(4)]
                    moments(band, i, c, order, values)
            return carry

        lax.fori_loop(0, 3, body, 0)

    collect(0, w)
    sweep(1, 0, 6)
    collect(1, t1)
    sweep(2, 1, 5)
    collect(2, t2)
    sweep(3, 1, 5)
    collect(3, t1)
    sweep(4, 2, 4)
    for copy in inner:
        copy.wait()
    tall = 4 * half + SUB
    core = place()[1]

    outs = []
    for m in range(CHEB + 1):
        for c in range(chunks):
            upper = [res[0, r + 1, c, pl.ds(4 * m, 4), :] for r in range(2)]
            lower = [res[1, r, c, pl.ds(4 * m, 4), :] for r in range(2)]
            own = [jnp.where(core == 0, upper[r], lower[r]) for r in range(2)]
            rest = [jnp.where(core == 0, lower[r], upper[r]) for r in range(2)]
            places = [jnp.where(core == 0, r, half - 2 + r) for r in range(2)]
            for s in range(4):
                for g in range(half // SUB):
                    at = pl.ds(g * SUB, SUB)
                    value = mine[m, s, c, at, :] + other[m, s, c, at, :]
                    for r in range(2):
                        hit = row + g * SUB == places[r]
                        value = jnp.where(hit, own[r][s : s + 1], value)
                    slab[m, pl.ds(c * tall + s * half + g * SUB, SUB), :] = value
            for r in range(2):
                slab[m, pl.ds(c * tall + 4 * half + 4 * r, 4), :] = rest[r]
            for band, r in ((0, 0), (1, 2)):
                halo = res[band, r, c, pl.ds(4 * m, 4), :]
                slab[m, pl.ds(chunks * tall + band * SUB + c, 1), :] = jnp.sum(
                    halo, axis=0, keepdims=True
                )
        away = pltpu.make_async_copy(slab.at[m], out.at[m], sems.at[m])
        away.start()
        outs.append(away)
    for copy in outs:
        copy.wait()


def edges(records, mine, other, after):
    _, _, chunks, half, _ = mine.shape
    slabs = (CHEB + 1, chunks * (4 * half + SUB) + 2 * SUB, LANES)
    any_ = pl.BlockSpec(memory_space=pl.ANY)
    return pl.pallas_call(
        functools.partial(edges_kernel, chunks, half),
        out_shape=jax.ShapeDtypeStruct(slabs, F32),
        in_specs=[any_] * 8,
        out_specs=any_,
        scratch_shapes=[
            pltpu.VMEM((2, chunks, (WIN + 2) * REC, LANES), F32),
            pltpu.VMEM((2, chunks, (WIN + 2) * 32, LANES), F32),
            pltpu.VMEM((2, chunks, (WIN + 2) * 32, LANES), F32),
            pltpu.VMEM((2, 3, chunks, 24, LANES), F32),
            pltpu.VMEM(mine.shape, F32),
            pltpu.VMEM(mine.shape, F32),
            pltpu.VMEM(slabs, F32),
            pltpu.SemaphoreType.DMA((14,)),
        ],
        compiler_params=pltpu.CompilerParams(vmem_limit_bytes=VMEM_WIDE),
        cost_estimate=pl.CostEstimate(
            flops=20_000_000, bytes_accessed=4_000_000, transcendentals=0
        ),
        name="edges",
    )(*records, mine, other, after)


ACOS = (
    1.5707963050,
    -0.2145988016,
    0.0889789874,
    -0.0501743046,
    0.0308918810,
    -0.0170881256,
    0.0066700901,
    -0.0012624911,
)


def arccos(e):
    size = jnp.abs(e)
    poly = jnp.full_like(size, ACOS[-1])
    for value in ACOS[-2::-1]:
        poly = poly * size + value
    angle = jnp.sqrt(1.0 - size) * poly
    return jnp.where(e < 0.0, math.pi - angle, angle)


def weights_of(e):
    gain = jackson(CHEB + 1)
    sine = jnp.sqrt((1.0 - e) * (1.0 + e))
    square = e * e
    sines = [sine, 2.0 * e * sine, (4.0 * square - 1.0) * sine, 4.0 * e * (2.0 * square - 1.0) * sine]
    out = [gain[0] * (1.0 - arccos(e) / math.pi)]
    for m in range(1, CHEB + 1):
        out.append(sines[m - 1] * (-2.0 * gain[m] / (math.pi * m)))
    return out


def density_kernel(scale, sites, sums, slabs, out):
    added = jnp.sum(sums[...], axis=0, keepdims=True) * scale
    lane = lax.broadcasted_iota(jnp.int32, (1, LANES), 1)
    totals = [jnp.sum(jnp.where(lane == m, added, 0.0)) for m in range(CHEB + 1)]
    totals[3] = 2.0 * totals[3] - totals[1]
    totals[4] = 2.0 * totals[4] - totals[0]
    target = jnp.sum(jnp.where(lane == 5, sums[0:1, :], 0.0)) * sites

    point = (
        lax.broadcasted_iota(jnp.int32, (SUB, LANES), 0) * LANES
        + lax.broadcasted_iota(jnp.int32, (SUB, LANES), 1)
        + 1
    )
    ways = 2 ** (BISECT // 2)
    valid = point < ways
    low = jnp.float32(-1.0)
    step = 2.0
    for _ in range(2):
        step = step / ways
        mids = jnp.where(valid, low + point.astype(F32) * step, 0.0)
        count = None
        for value, total in zip(weights_of(mids), totals):
            term = value * total
            count = term if count is None else count + term
        below = jnp.sum(jnp.where(valid & (count < target), 1.0, 0.0))
        low = low + below * step
    chem = jnp.full((SUB, LANES), low + 0.5 * step, F32)
    weights = weights_of(chem)
    for k in range(out.shape[0] // SUB):
        at = pl.ds(k * SUB, SUB)
        acc = None
        for m in range(CHEB + 1):
            term = weights[m] * slabs[m, at, :]
            acc = term if acc is None else acc + term
        out[at, :] = acc


def density(sums, slabs, vectors, sites):
    vmem = pl.BlockSpec(memory_space=pltpu.VMEM)
    return pl.pallas_call(
        functools.partial(density_kernel, 1.0 / vectors, float(sites)),
        out_shape=jax.ShapeDtypeStruct(slabs.shape[1:], F32),
        in_specs=[vmem, vmem],
        out_specs=vmem,
        compiler_params=pltpu.CompilerParams(vmem_limit_bytes=VMEM_LIMIT),
        cost_estimate=pl.CostEstimate(flops=2_000_000, bytes_accessed=4_000_000, transcendentals=0),
        name="density",
    )(sums, slabs)


def potential_kernel(chunks, half, mine, other, out, dens, charge):
    first = place()[1] == 0
    tall = 4 * half + SUB
    guard = SUB

    for c in range(chunks):
        for s in range(4):
            at = pl.ds(c * tall + s * half, half)
            m, o = mine[at, :], other[at, :]
            dens[s, c, pl.ds(0, half), :] = jnp.where(first, m, o)
            dens[s, c, pl.ds(half, half), :] = jnp.where(first, o, m)
        at = pl.ds(c * tall + 4 * half, SUB)
        m, o = mine[at, :], other[at, :]
        upper, lower = jnp.where(first, o, m), jnp.where(first, m, o)
        for r in range(2):
            for s in range(4):
                k = 4 * r + s
                for row, more in ((r, upper), (2 * half - 2 + r, lower)):
                    dens[s, c, pl.ds(row, 1), :] = dens[s, c, pl.ds(row, 1), :] + more[k : k + 1]
        for g in range(2 * half // SUB):
            at = pl.ds(g * SUB, SUB)
            total = (dens[0, c, at, :] + dens[1, c, at, :]) + (dens[2, c, at, :] + dens[3, c, at, :])
            charge[c, pl.ds(guard + g * SUB, SUB), :] = total - 2.0
        for band, row in ((0, guard - 1), (1, guard + 2 * half)):
            at = pl.ds(chunks * tall + band * SUB + c, 1)
            charge[c, pl.ds(row, 1), :] = mine[at, :] + other[at, :] - 2.0
    for g in range(2 * half // SUB):
        at = pl.ds(guard + g * SUB, SUB)
        for c in range(chunks):
            here = charge[c, at, :]
            left = from_left(roll_right(here), roll_right(charge[(c - 1) % chunks, at, :]))
            right = from_right(roll_left(here), roll_left(charge[(c + 1) % chunks, at, :]))
            near = (
                charge[c, pl.ds(guard + g * SUB - 1, SUB), :]
                + charge[c, pl.ds(guard + g * SUB + 1, SUB), :]
                + left
                + right
            )
            base = 0.5 * here + 0.25 * near
            for s in range(4):
                value = dens[s, c, pl.ds(g * SUB, SUB), :]
                out[s, pl.ds(g * SUB, SUB), pl.ds(c * LANES, LANES)] = 3.0 * (value - 0.5) + base


def new_potential(mine, other, chunks):
    half = ((mine.shape[0] - 2 * SUB) // chunks - SUB) // 4
    vmem = pl.BlockSpec(memory_space=pltpu.VMEM)
    return pl.pallas_call(
        functools.partial(potential_kernel, chunks, half),
        out_shape=jax.ShapeDtypeStruct((4, 2 * half, chunks * LANES), F32),
        in_specs=[vmem, vmem],
        out_specs=vmem,
        scratch_shapes=[
            pltpu.VMEM((4, chunks, 2 * half, LANES), F32),
            pltpu.VMEM((chunks, 2 * half + 2 * SUB, LANES), F32),
        ],
        compiler_params=pltpu.CompilerParams(vmem_limit_bytes=VMEM_LIMIT),
        cost_estimate=pl.CostEstimate(flops=1_000_000, bytes_accessed=2_000_000, transcendentals=0),
        name="new_potential",
    )(mine, other)


def per_device(vectors, hoppings, potential, stacking, interlayer, filling):
    strips, ranks = lax.axis_size("dom"), lax.axis_size("vec")
    _, nvec, rows, width = vectors.shape
    long_way = [(i, (i - 1 if i % 2 == 0 else i + 1) % strips) for i in range(strips)]
    short_way = [(i, i ^ 1) for i in range(strips)]
    sibling = [(i, i ^ 1) for i in range(ranks)]
    across = [(i, i ^ 2) for i in range(ranks)]

    own_long, own_short, extra = pack(
        interlayer,
        vectors.reshape(4 * nvec, rows, width),
        hoppings.reshape(6, rows, width),
        potential,
        stacking,
    )
    got_long = lax.ppermute(own_long, "dom", long_way)
    got_short = lax.ppermute(own_short, "dom", short_way)
    mine, yours, part = interior(interlayer, vectors, hoppings, potential, stacking, own_long)
    records = (own_long, own_short, got_long, got_short, extra)
    totals = totals_of(records, part, filling, strips * ranks)
    yours, ready = lax.optimization_barrier((yours, totals))
    other = lax.ppermute(yours, "vec", sibling)
    slabs = edges(records, mine, other, totals) * (1.0 / (nvec * ranks))
    sums = lax.all_to_all(ready, ("dom", "vec"), 0, 0, tiled=True)
    sites = 4 * rows * width * strips
    chip = density(sums, slabs, nvec * ranks, sites)
    whole = chip + lax.ppermute(chip, "vec", across)
    return new_potential(whole, lax.ppermute(whole, "vec", sibling), width // LANES)


def solution(mesh):
    placed = (
        P(None, "vec", "dom", None),
        P(None, None, "dom", None),
        P(None, "dom", None),
        P("dom", None),
        P(),
        P(),
    )
    return jax.shard_map(
        per_device, mesh=mesh, in_specs=placed, out_specs=P(None, "dom", None), check_vma=False
    )
```

```python
import functools
import math

import jax
import jax.numpy as jnp
from jax import lax
from jax.experimental import pallas as pl
from jax.experimental.pallas import tpu as pltpu
from jax.sharding import PartitionSpec as P

CHEB = 4
BISECT = 16
LANES = 128
SUB = 8
REC = 48
COEF = 32
F32 = jnp.float32
VMEM_LIMIT = 44 * 1024 * 1024
VMEM_WIDE = 64 * 1024 * 1024 - 256 * 1024
SLOT = (0, 3, 5, 8, 1, 4, 6, 9, 10, 12, 11, 13, 7, 2)
FAR = COEF + 8
NEAR = 2 * REC
MESSAGE = NEAR + FAR
EXTRA = REC + 8


def jackson(count):
    angle = math.pi / (count + 1)
    return [
        ((count - m + 1) * math.cos(angle * m) + math.sin(angle * m) / math.tan(angle))
        / (count + 1)
        for m in range(count)
    ]


def lane_is(where, shape=(SUB, LANES)):
    return lax.broadcasted_iota(jnp.int32, shape, 1) == where


def from_left(here, left):
    return jnp.where(lane_is(0, here.shape), left, here)


def from_right(here, right):
    return jnp.where(lane_is(LANES - 1, here.shape), right, here)


def roll_left(x):
    return pltpu.roll(x, LANES - 1, 1)


def roll_right(x):
    return pltpu.roll(x, 1, 1)


def pick(classes, table):
    values = list(table)
    bit = 1
    while len(values) > 1:
        hit = (classes & bit) != 0
        values = [jnp.where(hit, values[i + 1], values[i]) for i in range(0, len(values), 2)]
        bit *= 2
    return values[0]


def hop_apply(a, b, a_right, b_left, a_down, b_up, coef, t2_down):
    pot = coef[8:12]
    aa, ab = coef[12:14]
    out = []
    for layer in range(2):
        t0, t1, t2, t1r = coef[4 * layer : 4 * layer + 4]
        h_a = t0 * b[layer] + t1 * b_left[layer] + t2 * b_up[layer] + pot[2 * layer] * a[layer]
        h_b = (
            t0 * a[layer]
            + t1r * a_right[layer]
            + t2_down[layer] * a_down[layer]
            + pot[2 * layer + 1] * b[layer]
        )
        out.append([h_a, h_b])
    out[0][0] = out[0][0] + aa * a[1] + ab * b[1]
    out[1][0] = out[1][0] + aa * a[0]
    out[1][1] = out[1][1] + ab * a[0]
    return [out[0][0], out[0][1], out[1][0], out[1][1]]


def place():
    return lax.rem(lax.axis_index("dom"), 2), lax.rem(lax.axis_index("vec"), 2)


def pack_kernel(rows, chunks, table, vec, hop, pot, stk, long_out, short_out, extra, inter, v8, h8,
                p8, s8, rec, sems):
    copies = [pltpu.make_async_copy(table, inter, sems.at[0])]
    n = 1
    for band in range(2):
        at = pl.ds(band * (rows - SUB), SUB)
        for src, dst in (
            (hop.at[:, at], h8.at[band]),
            (pot.at[:, at], p8.at[band]),
            (stk.at[at], s8.at[band]),
        ):
            copies.append(pltpu.make_async_copy(src, dst, sems.at[n]))
            n += 1
        for c in range(chunks):
            src = vec.at[:, at, pl.ds(c * LANES, LANES)]
            copies.append(pltpu.make_async_copy(src, v8.at[band, c], sems.at[n]))
            n += 1
    for copy in copies:
        copy.start()
    nf = vec.shape[0]
    flat = v8.reshape(2, chunks, nf * SUB, LANES)
    odd = place()[0]
    outs = []
    copies[0].wait()

    for band in range(2):
        for copy in copies[1 + band * (3 + chunks) :][: 3 + chunks]:
            copy.wait()
        for c in range(chunks):
            lanes = pl.ds(c * LANES, LANES)
            first = 0 if band == 0 else SUB - 4
            for r in range(4):
                for s in range(nf // SUB):
                    rec[band, c, pl.ds(r * REC + s * SUB, SUB), :] = flat[
                        band, c, pl.ds(s * SUB * SUB + first + r, SUB, stride=SUB), :
                    ]
            after = pl.ds((c + 1) % chunks * LANES, LANES)
            coef = []
            for layer in range(2):
                for k in range(3):
                    coef.append(h8[band, 3 * layer + k, :, lanes] * -0.25)
                    if k == 1:
                        here = h8[band, 3 * layer + 1, :, lanes]
                        there = h8[band, 3 * layer + 1, :, after]
                        shifted = from_right(roll_left(here), roll_left(there)) * -0.25
                coef.append(shifted)
            for s in range(4):
                coef.append(p8[band, s, :, lanes] * 0.25)
            classes = s8[band, :, lanes]
            for w in range(2):
                table = [inter[w, k] * 0.25 for k in range(inter.shape[1])]
                coef.append(pick(classes, table))
            for k, value in enumerate(coef):
                at = pl.ds(COEF + SLOT[k], 4, stride=REC)
                rec[band, c, at, :] = value[first : first + 4]
            zero = jnp.zeros((4, LANES), F32)
            for k in range(len(coef), REC - COEF):
                rec[band, c, pl.ds(COEF + k, 4, stride=REC), :] = zero
            third = (2, 5)[band]
            for r, slot, k in (
                ((0, 14, 8), (0, 15, 10)),
                ((2, 14, 3), (2, 15, 7), (3, 14, 9), (3, 15, 11)),
            )[band]:
                rec[band, c, pl.ds(r * REC + COEF + slot, 1), :] = coef[k][third : third + 1]
        third_at = (2, 1)[band] * REC
        parts = (
            (pl.ds((0, 2)[band] * REC, NEAR), pl.ds(0, NEAR)),
            (pl.ds(third_at, FAR), pl.ds(NEAR, FAR)),
        )
        for src_at, dst_at in (
            (pl.ds((1 - band) * 3 * REC, REC), pl.ds(0, REC)),
            (pl.ds(third_at + FAR, REC - FAR), pl.ds(REC, REC - FAR)),
        ):
            away = pltpu.make_async_copy(
                rec.at[band, :, src_at], extra.at[band, :, dst_at], sems.at[n]
            )
            away.start()
            outs.append(away)
            n += 1
        for src_at, dst_at in parts:
            src, sem = rec.at[band, :, src_at], sems.at[n]

            @pl.when(odd == band)
            def _():
                pltpu.make_async_copy(src, long_out.at[:, dst_at], sem).start()

            @pl.when(odd != band)
            def _():
                pltpu.make_async_copy(src, short_out.at[:, dst_at], sem).start()

            outs.append(pltpu.make_async_copy(src, long_out.at[:, dst_at], sem))
            n += 1
    for copy in outs:
        copy.wait()


def pack(inter, vec, hop, pot, stk):
    fields, rows, width = vec.shape
    chunks = width // LANES
    any_ = pl.BlockSpec(memory_space=pl.ANY)
    message = jax.ShapeDtypeStruct((chunks, MESSAGE, LANES), F32)
    n_in = 2 * (chunks + 3) + 1
    return pl.pallas_call(
        functools.partial(pack_kernel, rows, chunks),
        out_shape=[message, message, jax.ShapeDtypeStruct((2, chunks, EXTRA, LANES), F32)],
        in_specs=[any_, any_, any_, any_, any_],
        out_specs=[any_, any_, any_],
        scratch_shapes=[
            pltpu.SMEM(inter.shape, F32),
            pltpu.VMEM((2, chunks, fields, SUB, LANES), F32),
            pltpu.VMEM((2, 6, SUB, width), F32),
            pltpu.VMEM((2, 4, SUB, width), F32),
            pltpu.VMEM((2, SUB, width), jnp.int32),
            pltpu.VMEM((2, chunks, 4 * REC, LANES), F32),
            pltpu.SemaphoreType.DMA((n_in + 8,)),
        ],
        compiler_params=pltpu.CompilerParams(vmem_limit_bytes=VMEM_WIDE),
        cost_estimate=pl.CostEstimate(flops=1_000_000, bytes_accessed=4_000_000, transcendentals=0),
        name="pack",
    )(inter, vec, hop, pot, stk)


PAD = 8


def interior_kernel(rows, chunks, nvec, group, table, vec, hop, pot, stk, after, keep, send, tot,
                    inter, hop_raw, pot_raw, x, t1, t2, hp, pt, st, ww, mom, dots, ends,
                    sems):
    del after
    halves = nvec // group
    copies = [pltpu.make_async_copy(table, inter, sems.at[0])]
    n = 1
    for src, dst in ((hop, hop_raw), (pot, pot_raw), (stk, st)):
        copies.append(pltpu.make_async_copy(src, dst, sems.at[n]))
        n += 1
    late = []
    for q in range(halves):
        part = []
        for c in range(chunks):
            lanes = pl.ds(c * LANES, LANES)
            part.append(
                pltpu.make_async_copy(
                    vec.at[:, pl.ds(q * group, group), :, lanes],
                    x.at[:, pl.ds(q * group, group), c, pl.ds(PAD, rows)],
                    sems.at[n],
                )
            )
            n += 1
        late.append(part)
    for copy in copies + [copy for part in late for copy in part]:
        copy.start()
    for copy in copies:
        copy.wait()

    groups = rows // SUB

    def prepare(g, carry):
        at = pl.ds(pl.multiple_of(g * SUB, SUB), SUB)
        lanes = [pl.ds(c * LANES, LANES) for c in range(chunks)]
        for layer in range(2):
            rolled = [roll_left(hop_raw[layer, 1, at, lanes[c]]) for c in range(chunks)]
            for c in range(chunks):
                hp[layer, 3, c, at, :] = (
                    from_right(rolled[c], rolled[(c + 1) % chunks]) * -0.25
                )
            for k in range(3):
                for c in range(chunks):
                    hp[layer, k, c, at, :] = hop_raw[layer, k, at, lanes[c]] * -0.25
        for c in range(chunks):
            for s in range(4):
                pt[s, c, at, :] = pot_raw[s, at, lanes[c]] * 0.25
            classes = st[at, lanes[c]]
            for w in range(2):
                table = [inter[w, k] * 0.25 for k in range(inter.shape[1])]
                ww[w, c, at, :] = pick(classes, table)
        return carry

    lax.fori_loop(0, groups, prepare, 0)

    def sweep(order, q, source, before, target):
        def load(ref, s, v, c, at):
            return ref[s, v, c, at, :]

        def body(g, carry):
            base = pl.multiple_of(g * SUB, SUB)
            mid = pl.ds(base + PAD, SUB)
            up = pl.ds(base + PAD - 1, SUB)
            down = pl.ds(base + PAD + 1, SUB)
            plain = pl.ds(base, SUB)
            plain_down = pl.ds(base + 1, SUB)
            vs = range(group)
            src, off = source

            def rolled(site, c, fn):
                return [fn(load(src, site, v + off, c, mid)) for v in vs]

            products = [None] * 2
            b_prev = [rolled(2 * l + 1, chunks - 1, roll_right) for l in range(2)]
            a_here = [rolled(2 * l, 0, roll_left) for l in range(2)]
            for c in range(chunks):
                nxt = (c + 1) % chunks
                a_next = [rolled(2 * l, nxt, roll_left) for l in range(2)]
                b_here = [rolled(2 * l + 1, c, roll_right) for l in range(2)]
                coef = []
                for layer in range(2):
                    for k in range(4):
                        coef.append(hp[layer, k, c, plain, :])
                for s in range(4):
                    coef.append(pt[s, c, plain, :])
                for w in range(2):
                    coef.append(ww[w, c, plain, :])
                t2_down = [hp[layer, 2, c, plain_down, :] for layer in range(2)]
                sums = [None] * 4
                squares = [None] * 4
                for v in vs:
                    a = [load(src, 2 * l, v + off, c, mid) for l in range(2)]
                    b = [load(src, 2 * l + 1, v + off, c, mid) for l in range(2)]
                    a_down = [load(src, 2 * l, v + off, c, down) for l in range(2)]
                    b_up = [load(src, 2 * l + 1, v + off, c, up) for l in range(2)]
                    a_right = [from_right(a_here[l][v], a_next[l][v]) for l in range(2)]
                    b_left = [from_left(b_here[l][v], b_prev[l][v]) for l in range(2)]
                    new = hop_apply(a, b, a_right, b_left, a_down, b_up, coef, t2_down)
                    for s in range(4):
                        if order == 1:
                            value = new[s] * 0.5
                        elif order == CHEB:
                            value = new[s]
                        else:
                            ref, shift = before
                            value = new[s] - load(ref, s, v + shift, c, mid)
                        if target is not None:
                            target[s, v, c, mid, :] = value
                        first = load(x, s, v + q * group, c, mid)
                        term = first * value
                        sums[s] = term if sums[s] is None else sums[s] + term
                        if order == 2:
                            prior = load(src, s, v + off, c, mid)
                            for k, pair in enumerate((prior * value, value * value)):
                                products[k] = pair if products[k] is None else products[k] + pair
                        if order == 1:
                            sq = first * first
                            squares[s] = sq if squares[s] is None else squares[s] + sq
                for s in range(4):
                    if q > 0:
                        sums[s] = sums[s] + mom[order, s, c, plain, :]
                    if order == CHEB and q == halves - 1:
                        sums[s] = sums[s] - mom[order - 2, s, c, plain, :]
                    mom[order, s, c, plain, :] = sums[s]
                    if order == 1:
                        if q > 0:
                            squares[s] = squares[s] + mom[0, s, c, plain, :]
                        mom[0, s, c, plain, :] = squares[s]
                a_here = a_next
                b_prev = b_here
            if order == 2:
                row = lax.broadcasted_iota(jnp.int32, (SUB, LANES), 0) + base
                inside = (row >= 2) & (row < rows - 2)
                for k in range(2):
                    dots[k] = dots[k] + jnp.where(inside, products[k], 0.0)
            return carry

        lax.fori_loop(0, groups, body, 0, unroll=4)

    half = rows // 2
    core = place()[1]
    keep_at = pl.ds(pl.multiple_of(core * half, SUB), half)
    send_at = pl.ds(pl.multiple_of((1 - core) * half, SUB), half)
    outs = []

    def write_out(order):
        for rows_at, dst, k in ((keep_at, keep, 0), (send_at, send, 1)):
            copy = pltpu.make_async_copy(
                mom.at[order, :, :, rows_at], dst.at[order], sems.at[n + 2 * order + k]
            )
            copy.start()
            outs.append(copy)

    dots[...] = jnp.zeros_like(dots)
    for q in range(halves):
        for copy in late[q]:
            copy.wait()
        start = (x, q * group)
        steps = ((start, None, t1), ((t1, 0), start, t2), ((t2, 0), (t1, 0), t1), ((t1, 0), (t2, 0), None))
        for order, (source, before, target) in enumerate(steps, 1):
            sweep(order, q, source, before, target)
            if q == halves - 1:
                if order == 1:
                    write_out(0)
                write_out(order)

    def add_up(g, carry):
        base = pl.multiple_of(g * SUB, SUB)
        row = lax.broadcasted_iota(jnp.int32, (SUB, LANES), 0) + base
        inside = (row >= 2) & (row < rows - 2)
        result = []
        for m in range(3):
            acc = None
            for s in range(4):
                for c in range(chunks):
                    value = mom[m, s, c, pl.ds(base, SUB), :]
                    acc = value if acc is None else acc + value
            result.append(carry[m] + jnp.where(inside, acc, 0.0))
        return tuple(result)

    sums = lax.fori_loop(0, groups, add_up, tuple(jnp.zeros((SUB, LANES), F32) for _ in range(3)))
    for m in range(3):
        ends[m] = sums[m]
    for k in range(2):
        ends[3 + k] = dots[k]
    last = pltpu.make_async_copy(ends, tot, sems.at[n + 2 * (CHEB + 1)])
    last.start()
    outs.append(last)
    for copy in outs:
        copy.wait()


def interior(inter, vec, hop, pot, stk, after):
    _, nvec, rows, width = vec.shape
    chunks = width // LANES
    group = 2
    any_ = pl.BlockSpec(memory_space=pl.ANY)
    half = jax.ShapeDtypeStruct((CHEB + 1, 4, chunks, rows // 2, LANES), F32)
    n = 5 + chunks * (nvec // group) + 2 * (CHEB + 1)
    return pl.pallas_call(
        functools.partial(interior_kernel, rows, chunks, nvec, group),
        out_shape=[half, half, jax.ShapeDtypeStruct((CHEB + 1, SUB, LANES), F32)],
        in_specs=[any_] * 6,
        out_specs=[any_, any_, any_],
        scratch_shapes=[
            pltpu.SMEM(inter.shape, F32),
            pltpu.VMEM(hop.shape, F32),
            pltpu.VMEM(pot.shape, F32),
            pltpu.VMEM((4, nvec, chunks, rows + 2 * PAD, LANES), F32),
            pltpu.VMEM((4, group, chunks, rows + 2 * PAD, LANES), F32),
            pltpu.VMEM((4, group, chunks, rows + 2 * PAD, LANES), F32),
            pltpu.VMEM((2, 4, chunks, rows + SUB, LANES), F32),
            pltpu.VMEM((4, chunks, rows, LANES), F32),
            pltpu.VMEM((rows, width), jnp.int32),
            pltpu.VMEM((2, chunks, rows, LANES), F32),
            pltpu.VMEM((CHEB + 1, 4, chunks, rows, LANES), F32),
            pltpu.VMEM((2, SUB, LANES), F32),
            pltpu.VMEM((CHEB + 1, SUB, LANES), F32),
            pltpu.SemaphoreType.DMA((n,)),
        ],
        compiler_params=pltpu.CompilerParams(vmem_limit_bytes=VMEM_WIDE),
        cost_estimate=pl.CostEstimate(
            flops=60_000_000, bytes_accessed=9_000_000, transcendentals=0
        ),
        name="interior",
    )(inter, vec, hop, pot, stk, after)


WIN = 7
GUARD = REC


def gather_window(refs, w, sems, part=None, dots=None, share=None, filling=None, beside=()):
    own_long, own_short, got_long, got_short, extra = refs
    odd = place()[0]
    even = odd == 0
    copies = []

    def both(first, second, band, src_at, dst_at):
        dst, sem = w.at[band, :, dst_at], sems.at[len(copies)]

        @pl.when(even)
        def _():
            pltpu.make_async_copy(first.at[:, src_at], dst, sem).start()

        @pl.when(jnp.logical_not(even))
        def _():
            pltpu.make_async_copy(second.at[:, src_at], dst, sem).start()

        copies.append(pltpu.make_async_copy(first.at[:, src_at], dst, sem))

    def at(record, size):
        return pl.ds(GUARD + record * REC, size)

    few = part is not None
    if few:
        both(got_long, got_short, 0, pl.ds(REC, REC), at(2, REC))
        both(got_short, got_long, 1, pl.ds(0, REC), at(4, REC))
    else:
        both(got_long, got_short, 0, pl.ds(0, NEAR), at(1, NEAR))
        both(got_short, got_long, 1, pl.ds(0, NEAR), at(4, NEAR))
        both(got_long, got_short, 0, pl.ds(NEAR, FAR), at(0, FAR))
        both(got_short, got_long, 1, pl.ds(NEAR, FAR), at(6, FAR))
    both(own_long, own_short, 0, pl.ds(0, NEAR), at(3, NEAR))
    both(own_short, own_long, 1, pl.ds(0, NEAR), at(2, NEAR))
    both(own_long, own_short, 0, pl.ds(NEAR, FAR), at(5, FAR))
    both(own_short, own_long, 1, pl.ds(NEAR, FAR), at(1, FAR))
    plain = [
        (extra.at[0, :, pl.ds(REC, REC - FAR)], w.at[0, :, pl.ds(GUARD + 5 * REC + FAR, REC - FAR)]),
        (extra.at[1, :, pl.ds(REC, REC - FAR)], w.at[1, :, pl.ds(GUARD + REC + FAR, REC - FAR)]),
    ]
    if few:
        plain.extend(((part, dots), (share, filling)))
    else:
        plain.append((extra.at[0, :, pl.ds(0, REC)], w.at[0, :, at(6, REC)]))
        plain.append((extra.at[1, :, pl.ds(0, REC)], w.at[1, :, at(0, REC)]))
    for src, dst in plain:
        copy = pltpu.make_async_copy(src, dst, sems.at[len(copies)])
        copy.start()
        copies.append(copy)
    for copy in copies:
        copy.wait()
    for copy in beside:
        copy.start()
    if not few:
        for band, r, slot, to, to_slot in ((0, 1, 14, 0, 8), (0, 2, 14, 0, 12), (1, 4, 14, 6, 10)):
            for c in range(w.shape[1]):
                w[band, c, pl.ds(GUARD + to * REC + COEF + to_slot, 2), :] = w[
                    band, c, pl.ds(GUARD + r * REC + COEF + slot, 2), :
                ]


def window_slice(ref, is_w, band, c, i, site):
    start = GUARD + i * REC + site * SUB if is_w else (i + 1) * 32 + site * SUB
    return ref[band, c, pl.ds(pl.multiple_of(start, SUB), SUB), :]


def window_step(chunks, order, w, source, before, band, i, emit):
    from_w = order == 1

    def here(site, c, shift=0):
        return window_slice(source, from_w, band, c, i + shift, site)

    def coef_at(k, c, shift=0):
        at = GUARD + (i + shift) * REC + COEF + SLOT[k]
        return jnp.broadcast_to(w[band, c, pl.ds(at, 1), :], (SUB, LANES))

    b_prev = [roll_right(here(2 * l + 1, chunks - 1)) for l in range(2)]
    a_here = [roll_left(here(2 * l, 0)) for l in range(2)]
    for c in range(chunks):
        nxt = (c + 1) % chunks
        a_next = [roll_left(here(2 * l, nxt)) for l in range(2)]
        b_here = [roll_right(here(2 * l + 1, c)) for l in range(2)]
        coef = [coef_at(k, c) for k in range(14)]
        t2_down = [coef_at(4 * l + 2, c, 1) for l in range(2)]
        a = [here(2 * l, c) for l in range(2)]
        b = [here(2 * l + 1, c) for l in range(2)]
        a_down = [here(2 * l, c, 1) for l in range(2)]
        b_up = [here(2 * l + 1, c, -1) for l in range(2)]
        a_right = [from_right(a_here[l], a_next[l]) for l in range(2)]
        b_left = [from_left(b_here[l], b_prev[l]) for l in range(2)]
        new = hop_apply(a, b, a_right, b_left, a_down, b_up, coef, t2_down)
        for s in range(4):
            if order == 1:
                new[s] = new[s] * 0.5
            else:
                new[s] = new[s] - window_slice(before, order == 2, band, c, i, s)
        emit(c, new)
        a_here = a_next
        b_prev = b_here


def store_row(target, band, i):
    def emit(c, values):
        for s in range(4):
            at = pl.multiple_of((i + 1) * 32 + s * SUB, SUB)
            target[band, c, pl.ds(at, SUB), :] = values[s]

    return emit


def totals_kernel(chunks, parts, own_long, own_short, got_long, got_short, extra, part, share, tot,
                  w, t1, dots, filling, sems):
    records = (own_long, own_short, got_long, got_short, extra)
    gather_window(records, w, sems, part, dots, share, filling)

    def first(j, carry):
        for band in range(2):
            i = 2 - band + j
            window_step(chunks, 1, w, w, None, band, i, store_row(t1, band, i))
        return carry

    lax.fori_loop(0, 4, first, 0, unroll=2)

    def second(j, carry):
        for band in range(2):
            i = 3 - band + j
            sums = [None] * 5

            def emit(c, values):
                for s in range(4):
                    zero = window_slice(w, True, band, c, i, s)
                    one = window_slice(t1, False, band, c, i, s)
                    two = values[s]
                    terms = (zero * zero, zero * one, zero * two, one * two, two * two)
                    for k, term in enumerate(terms):
                        sums[k] = term if sums[k] is None else sums[k] + term

            window_step(chunks, 2, w, t1, w, band, i, emit)
            for k in range(5):
                dots[k] = dots[k] + sums[k]
        return carry

    lax.fori_loop(0, 2, second, 0, unroll=2)
    lane = lax.broadcasted_iota(jnp.int32, (SUB, LANES), 1)
    row = jnp.zeros((SUB, LANES), F32)
    for m in range(5):
        row = jnp.where(lane == m, jnp.sum(dots[m]), row)
    row = jnp.where(lane == 5, filling[0], row)
    for k in range(parts // SUB):
        tot[pl.ds(k * SUB, SUB), :] = row


def totals_of(records, part, filling, parts):
    chunks = records[0].shape[0]
    any_ = pl.BlockSpec(memory_space=pl.ANY)
    vmem = pl.BlockSpec(memory_space=pltpu.VMEM)
    return pl.pallas_call(
        functools.partial(totals_kernel, chunks, parts),
        out_shape=jax.ShapeDtypeStruct((parts, LANES), F32),
        in_specs=[any_] * 7,
        out_specs=vmem,
        scratch_shapes=[
            pltpu.VMEM((2, chunks, (WIN + 2) * REC, LANES), F32),
            pltpu.VMEM((2, chunks, (WIN + 2) * 32, LANES), F32),
            pltpu.VMEM((5, SUB, LANES), F32),
            pltpu.SMEM((1,), F32),
            pltpu.SemaphoreType.DMA((10,)),
        ],
        compiler_params=pltpu.CompilerParams(vmem_limit_bytes=VMEM_WIDE),
        cost_estimate=pl.CostEstimate(flops=8_000_000, bytes_accessed=4_000_000, transcendentals=0),
        name="totals",
    )(*records, part, filling)


def edges_kernel(chunks, half, own_long, own_short, got_long, got_short, extra, mine_in, other_in,
                 after, out, w, t1, t2, res, mine, other, slab, sems):
    del after
    inner = [
        pltpu.make_async_copy(src, dst, sems.at[12 + k])
        for k, (src, dst) in enumerate(((mine_in, mine), (other_in, other)))
    ]
    gather_window((own_long, own_short, got_long, got_short, extra), w, sems, beside=inner)
    row = lax.broadcasted_iota(jnp.int32, (SUB, LANES), 0)
    single, double = (row & 1) != 0, (row & 2) != 0

    def merged(hit, a, b, shift):
        return jnp.where(hit, b, a) + pltpu.roll(jnp.where(hit, a, b), shift, 0)

    def moments(band, i, c, order, values):
        p = [window_slice(w, True, band, c, i, s) * values[s] for s in range(4)]
        pairs = [merged(single, p[2 * k], p[2 * k + 1], 1) for k in range(2)]
        both = merged(double, pairs[0], pairs[1], 2)
        both = both + pltpu.roll(both, 4, 0)
        res[band, i - 2, c, pl.ds(order * 4, 4), :] = both[0:4]

    def sweep(order, first, last):
        source, before, target = {
            1: (w, None, t1),
            2: (t1, w, t2),
            3: (t2, t1, t1),
            4: (t1, t2, None),
        }[order]

        def body(j, carry):
            i = first + j
            for band in range(2):
                if order < 4:
                    emit = store_row(target, band, i)
                else:
                    emit = lambda c, values, band=band: moments(band, i, c, 4, values)
                window_step(chunks, order, w, source, before, band, i, emit)
            return carry

        lax.fori_loop(0, last - first + 1, body, 0, unroll=1 if order == 4 else 2)

    def collect(order, ref):
        def body(j, carry):
            i = 2 + j
            for band in range(2):
                for c in range(chunks):
                    values = [window_slice(ref, ref is w, band, c, i, s) for s in range(4)]
                    moments(band, i, c, order, values)
            return carry

        lax.fori_loop(0, 3, body, 0)

    collect(0, w)
    sweep(1, 0, 6)
    collect(1, t1)
    sweep(2, 1, 5)
    collect(2, t2)
    sweep(3, 1, 5)
    collect(3, t1)
    sweep(4, 2, 4)
    for copy in inner:
        copy.wait()
    tall = 4 * half + SUB
    core = place()[1]

    outs = []
    for m in range(CHEB + 1):
        for c in range(chunks):
            upper = [res[0, r + 1, c, pl.ds(4 * m, 4), :] for r in range(2)]
            lower = [res[1, r, c, pl.ds(4 * m, 4), :] for r in range(2)]
            own = [jnp.where(core == 0, upper[r], lower[r]) for r in range(2)]
            rest = [jnp.where(core == 0, lower[r], upper[r]) for r in range(2)]
            places = [jnp.where(core == 0, r, half - 2 + r) for r in range(2)]
            for s in range(4):
                for g in range(half // SUB):
                    at = pl.ds(g * SUB, SUB)
                    value = mine[m, s, c, at, :] + other[m, s, c, at, :]
                    for r in range(2):
                        hit = row + g * SUB == places[r]
                        value = jnp.where(hit, own[r][s : s + 1], value)
                    slab[m, pl.ds(c * tall + s * half + g * SUB, SUB), :] = value
            for r in range(2):
                slab[m, pl.ds(c * tall + 4 * half + 4 * r, 4), :] = rest[r]
            for band, r in ((0, 0), (1, 2)):
                halo = res[band, r, c, pl.ds(4 * m, 4), :]
                slab[m, pl.ds(chunks * tall + band * SUB + c, 1), :] = jnp.sum(
                    halo, axis=0, keepdims=True
                )
        away = pltpu.make_async_copy(slab.at[m], out.at[m], sems.at[m])
        away.start()
        outs.append(away)
    for copy in outs:
        copy.wait()


def edges(records, mine, other, after):
    _, _, chunks, half, _ = mine.shape
    slabs = (CHEB + 1, chunks * (4 * half + SUB) + 2 * SUB, LANES)
    any_ = pl.BlockSpec(memory_space=pl.ANY)
    return pl.pallas_call(
        functools.partial(edges_kernel, chunks, half),
        out_shape=jax.ShapeDtypeStruct(slabs, F32),
        in_specs=[any_] * 8,
        out_specs=any_,
        scratch_shapes=[
            pltpu.VMEM((2, chunks, (WIN + 2) * REC, LANES), F32),
            pltpu.VMEM((2, chunks, (WIN + 2) * 32, LANES), F32),
            pltpu.VMEM((2, chunks, (WIN + 2) * 32, LANES), F32),
            pltpu.VMEM((2, 3, chunks, 24, LANES), F32),
            pltpu.VMEM(mine.shape, F32),
            pltpu.VMEM(mine.shape, F32),
            pltpu.VMEM(slabs, F32),
            pltpu.SemaphoreType.DMA((14,)),
        ],
        compiler_params=pltpu.CompilerParams(vmem_limit_bytes=VMEM_WIDE),
        cost_estimate=pl.CostEstimate(
            flops=20_000_000, bytes_accessed=4_000_000, transcendentals=0
        ),
        name="edges",
    )(*records, mine, other, after)


ACOS = (
    1.5707963050,
    -0.2145988016,
    0.0889789874,
    -0.0501743046,
    0.0308918810,
    -0.0170881256,
    0.0066700901,
    -0.0012624911,
)


def arccos(e):
    size = jnp.abs(e)
    poly = jnp.full_like(size, ACOS[-1])
    for value in ACOS[-2::-1]:
        poly = poly * size + value
    angle = jnp.sqrt(1.0 - size) * poly
    return jnp.where(e < 0.0, math.pi - angle, angle)


def weights_of(e):
    gain = jackson(CHEB + 1)
    sine = jnp.sqrt((1.0 - e) * (1.0 + e))
    square = e * e
    sines = [sine, 2.0 * e * sine, (4.0 * square - 1.0) * sine, 4.0 * e * (2.0 * square - 1.0) * sine]
    out = [gain[0] * (1.0 - arccos(e) / math.pi)]
    for m in range(1, CHEB + 1):
        out.append(sines[m - 1] * (-2.0 * gain[m] / (math.pi * m)))
    return out


def density_kernel(scale, sites, sums, slabs, out):
    added = jnp.sum(sums[...], axis=0, keepdims=True) * scale
    lane = lax.broadcasted_iota(jnp.int32, (1, LANES), 1)
    totals = [jnp.sum(jnp.where(lane == m, added, 0.0)) for m in range(CHEB + 1)]
    totals[3] = 2.0 * totals[3] - totals[1]
    totals[4] = 2.0 * totals[4] - totals[0]
    target = jnp.sum(jnp.where(lane == 5, sums[0:1, :], 0.0)) * sites

    point = (
        lax.broadcasted_iota(jnp.int32, (SUB, LANES), 0) * LANES
        + lax.broadcasted_iota(jnp.int32, (SUB, LANES), 1)
        + 1
    )
    ways = 2 ** (BISECT // 2)
    valid = point < ways
    low = jnp.float32(-1.0)
    step = 2.0
    for _ in range(2):
        step = step / ways
        mids = jnp.where(valid, low + point.astype(F32) * step, 0.0)
        count = None
        for value, total in zip(weights_of(mids), totals):
            term = value * total
            count = term if count is None else count + term
        below = jnp.sum(jnp.where(valid & (count < target), 1.0, 0.0))
        low = low + below * step
    chem = jnp.full((SUB, LANES), low + 0.5 * step, F32)
    weights = weights_of(chem)
    for k in range(out.shape[0] // SUB):
        at = pl.ds(k * SUB, SUB)
        acc = None
        for m in range(CHEB + 1):
            term = weights[m] * slabs[m, at, :]
            acc = term if acc is None else acc + term
        out[at, :] = acc


def density(sums, slabs, vectors, sites):
    vmem = pl.BlockSpec(memory_space=pltpu.VMEM)
    return pl.pallas_call(
        functools.partial(density_kernel, 1.0 / vectors, float(sites)),
        out_shape=jax.ShapeDtypeStruct(slabs.shape[1:], F32),
        in_specs=[vmem, vmem],
        out_specs=vmem,
        compiler_params=pltpu.CompilerParams(vmem_limit_bytes=VMEM_LIMIT),
        cost_estimate=pl.CostEstimate(flops=2_000_000, bytes_accessed=4_000_000, transcendentals=0),
        name="density",
    )(sums, slabs)


def potential_kernel(chunks, half, mine, other, out, dens, charge):
    first = place()[1] == 0
    tall = 4 * half + SUB
    guard = SUB

    for c in range(chunks):
        for s in range(4):
            at = pl.ds(c * tall + s * half, half)
            m, o = mine[at, :], other[at, :]
            dens[s, c, pl.ds(0, half), :] = jnp.where(first, m, o)
            dens[s, c, pl.ds(half, half), :] = jnp.where(first, o, m)
        at = pl.ds(c * tall + 4 * half, SUB)
        m, o = mine[at, :], other[at, :]
        upper, lower = jnp.where(first, o, m), jnp.where(first, m, o)
        for r in range(2):
            for s in range(4):
                k = 4 * r + s
                for row, more in ((r, upper), (2 * half - 2 + r, lower)):
                    dens[s, c, pl.ds(row, 1), :] = dens[s, c, pl.ds(row, 1), :] + more[k : k + 1]
        for g in range(2 * half // SUB):
            at = pl.ds(g * SUB, SUB)
            total = (dens[0, c, at, :] + dens[1, c, at, :]) + (dens[2, c, at, :] + dens[3, c, at, :])
            charge[c, pl.ds(guard + g * SUB, SUB), :] = total - 2.0
        for band, row in ((0, guard - 1), (1, guard + 2 * half)):
            at = pl.ds(chunks * tall + band * SUB + c, 1)
            charge[c, pl.ds(row, 1), :] = mine[at, :] + other[at, :] - 2.0
    for g in range(2 * half // SUB):
        at = pl.ds(guard + g * SUB, SUB)
        for c in range(chunks):
            here = charge[c, at, :]
            left = from_left(roll_right(here), roll_right(charge[(c - 1) % chunks, at, :]))
            right = from_right(roll_left(here), roll_left(charge[(c + 1) % chunks, at, :]))
            near = (
                charge[c, pl.ds(guard + g * SUB - 1, SUB), :]
                + charge[c, pl.ds(guard + g * SUB + 1, SUB), :]
                + left
                + right
            )
            base = 0.5 * here + 0.25 * near
            for s in range(4):
                value = dens[s, c, pl.ds(g * SUB, SUB), :]
                out[s, pl.ds(g * SUB, SUB), pl.ds(c * LANES, LANES)] = 3.0 * (value - 0.5) + base


def new_potential(mine, other, chunks):
    half = ((mine.shape[0] - 2 * SUB) // chunks - SUB) // 4
    vmem = pl.BlockSpec(memory_space=pltpu.VMEM)
    return pl.pallas_call(
        functools.partial(potential_kernel, chunks, half),
        out_shape=jax.ShapeDtypeStruct((4, 2 * half, chunks * LANES), F32),
        in_specs=[vmem, vmem],
        out_specs=vmem,
        scratch_shapes=[
            pltpu.VMEM((4, chunks, 2 * half, LANES), F32),
            pltpu.VMEM((chunks, 2 * half + 2 * SUB, LANES), F32),
        ],
        compiler_params=pltpu.CompilerParams(vmem_limit_bytes=VMEM_LIMIT),
        cost_estimate=pl.CostEstimate(flops=1_000_000, bytes_accessed=2_000_000, transcendentals=0),
        name="new_potential",
    )(mine, other)


def per_device(vectors, hoppings, potential, stacking, interlayer, filling):
    strips, ranks = lax.axis_size("dom"), lax.axis_size("vec")
    _, nvec, rows, width = vectors.shape
    long_way = [(i, (i - 1 if i % 2 == 0 else i + 1) % strips) for i in range(strips)]
    short_way = [(i, i ^ 1) for i in range(strips)]
    sibling = [(i, i ^ 1) for i in range(ranks)]
    across = [(i, i ^ 2) for i in range(ranks)]

    own_long, own_short, extra = pack(
        interlayer,
        vectors.reshape(4 * nvec, rows, width),
        hoppings.reshape(6, rows, width),
        potential,
        stacking,
    )
    got_long = lax.ppermute(own_long, "dom", long_way)
    got_short = lax.ppermute(own_short, "dom", short_way)
    mine, yours, part = interior(interlayer, vectors, hoppings, potential, stacking, own_long)
    records = (own_long, own_short, got_long, got_short, extra)
    totals = totals_of(records, part, filling, strips * ranks)
    yours, ready = lax.optimization_barrier((yours, totals))
    other = lax.ppermute(yours, "vec", sibling)
    slabs = edges(records, mine, other, totals) * (1.0 / (nvec * ranks))
    sums = lax.all_to_all(ready, ("dom", "vec"), 0, 0, tiled=True)
    sites = 4 * rows * width * strips
    chip = density(sums, slabs, nvec * ranks, sites)
    whole = chip + lax.ppermute(chip, "vec", across)
    return new_potential(whole, lax.ppermute(whole, "vec", sibling), width // LANES)


def solution(mesh):
    placed = (
        P(None, "vec", "dom", None),
        P(None, None, "dom", None),
        P(None, "dom", None),
        P("dom", None),
        P(),
        P(),
    )
    return jax.shard_map(
        per_device, mesh=mesh, in_specs=placed, out_specs=P(None, "dom", None), check_vma=False
    )
```

```python
import functools
import math

import jax
import jax.numpy as jnp
from jax import lax
from jax.experimental import pallas as pl
from jax.experimental.pallas import tpu as pltpu
from jax.sharding import PartitionSpec as P

CHEB = 4
BISECT = 16
LANES = 128
SUB = 8
REC = 48
COEF = 32
F32 = jnp.float32
VMEM_LIMIT = 44 * 1024 * 1024
VMEM_WIDE = 64 * 1024 * 1024 - 256 * 1024
SLOT = (0, 3, 5, 8, 1, 4, 6, 9, 10, 12, 11, 13, 7, 2)
FAR = COEF + 8
NEAR = 2 * REC
MESSAGE = NEAR + FAR
EXTRA = REC + 8


def jackson(count):
    angle = math.pi / (count + 1)
    return [
        ((count - m + 1) * math.cos(angle * m) + math.sin(angle * m) / math.tan(angle))
        / (count + 1)
        for m in range(count)
    ]


def lane_is(where, shape=(SUB, LANES)):
    return lax.broadcasted_iota(jnp.int32, shape, 1) == where


def from_left(here, left):
    return jnp.where(lane_is(0, here.shape), left, here)


def from_right(here, right):
    return jnp.where(lane_is(LANES - 1, here.shape), right, here)


def roll_left(x):
    return pltpu.roll(x, LANES - 1, 1)


def roll_right(x):
    return pltpu.roll(x, 1, 1)


def pick(classes, table):
    values = list(table)
    bit = 1
    while len(values) > 1:
        hit = (classes & bit) != 0
        values = [jnp.where(hit, values[i + 1], values[i]) for i in range(0, len(values), 2)]
        bit *= 2
    return values[0]


def hop_apply(a, b, a_right, b_left, a_down, b_up, coef, t2_down, sites="AB"):
    pot = coef[8:12]
    aa, ab = coef[12:14]
    out = []
    for layer in range(2):
        t0, t1, t2, t1r = coef[4 * layer : 4 * layer + 4]
        h_a = h_b = None
        if "A" in sites:
            h_a = t0 * b[layer] + t1 * b_left[layer] + t2 * b_up[layer] + pot[2 * layer] * a[layer]
        if "B" in sites:
            h_b = (
                t0 * a[layer]
                + t1r * a_right[layer]
                + t2_down[layer] * a_down[layer]
                + pot[2 * layer + 1] * b[layer]
            )
        out.append([h_a, h_b])
    if "A" in sites:
        out[0][0] = out[0][0] + aa * a[1] + ab * b[1]
        out[1][0] = out[1][0] + aa * a[0]
    if "B" in sites:
        out[1][1] = out[1][1] + ab * a[0]
    return [out[0][0], out[0][1], out[1][0], out[1][1]]


def place():
    return lax.rem(lax.axis_index("dom"), 2), lax.rem(lax.axis_index("vec"), 2)


def pack_kernel(rows, chunks, table, vec, hop, pot, stk, long_out, short_out, extra, inter, v8, h8,
                p8, s8, rec, sems):
    copies = [pltpu.make_async_copy(table, inter, sems.at[0])]
    n = 1
    for band in range(2):
        at = pl.ds(band * (rows - SUB), SUB)
        for src, dst in (
            (hop.at[:, at], h8.at[band]),
            (pot.at[:, at], p8.at[band]),
            (stk.at[at], s8.at[band]),
        ):
            copies.append(pltpu.make_async_copy(src, dst, sems.at[n]))
            n += 1
        for c in range(chunks):
            src = vec.at[:, at, pl.ds(c * LANES, LANES)]
            copies.append(pltpu.make_async_copy(src, v8.at[band, c], sems.at[n]))
            n += 1
    for copy in copies:
        copy.start()
    nf = vec.shape[0]
    flat = v8.reshape(2, chunks, nf * SUB, LANES)
    odd = place()[0]
    outs = []
    copies[0].wait()

    for band in range(2):
        for copy in copies[1 + band * (3 + chunks) :][: 3 + chunks]:
            copy.wait()
        for c in range(chunks):
            lanes = pl.ds(c * LANES, LANES)
            first = 0 if band == 0 else SUB - 4
            for r in range(4):
                for s in range(nf // SUB):
                    rec[band, c, pl.ds(r * REC + s * SUB, SUB), :] = flat[
                        band, c, pl.ds(s * SUB * SUB + first + r, SUB, stride=SUB), :
                    ]
            after = pl.ds((c + 1) % chunks * LANES, LANES)
            coef = []
            for layer in range(2):
                for k in range(3):
                    coef.append(h8[band, 3 * layer + k, :, lanes] * -0.25)
                    if k == 1:
                        here = h8[band, 3 * layer + 1, :, lanes]
                        there = h8[band, 3 * layer + 1, :, after]
                        shifted = from_right(roll_left(here), roll_left(there)) * -0.25
                coef.append(shifted)
            for s in range(4):
                coef.append(p8[band, s, :, lanes] * 0.25)
            classes = s8[band, :, lanes]
            for w in range(2):
                table = [inter[w, k] * 0.25 for k in range(inter.shape[1])]
                coef.append(pick(classes, table))
            for k, value in enumerate(coef):
                at = pl.ds(COEF + SLOT[k], 4, stride=REC)
                rec[band, c, at, :] = value[first : first + 4]
            zero = jnp.zeros((4, LANES), F32)
            for k in range(len(coef), REC - COEF):
                rec[band, c, pl.ds(COEF + k, 4, stride=REC), :] = zero
            third = (2, 5)[band]
            for r, slot, k in (
                ((0, 14, 8), (0, 15, 10)),
                ((2, 14, 3), (2, 15, 7), (3, 14, 9), (3, 15, 11)),
            )[band]:
                rec[band, c, pl.ds(r * REC + COEF + slot, 1), :] = coef[k][third : third + 1]
        third_at = (2, 1)[band] * REC
        parts = (
            (pl.ds((0, 2)[band] * REC, NEAR), pl.ds(0, NEAR)),
            (pl.ds(third_at, FAR), pl.ds(NEAR, FAR)),
        )
        for src_at, dst_at in parts:
            src, sem = rec.at[band, :, src_at], sems.at[n]

            @pl.when(odd == band)
            def _():
                pltpu.make_async_copy(src, long_out.at[:, dst_at], sem).start()

            @pl.when(odd != band)
            def _():
                pltpu.make_async_copy(src, short_out.at[:, dst_at], sem).start()

            outs.append(pltpu.make_async_copy(src, long_out.at[:, dst_at], sem))
            n += 1
        for src_at, dst_at in (
            (pl.ds((1 - band) * 3 * REC, REC), pl.ds(0, REC)),
            (pl.ds(third_at + FAR, REC - FAR), pl.ds(REC, REC - FAR)),
        ):
            away = pltpu.make_async_copy(
                rec.at[band, :, src_at], extra.at[band, :, dst_at], sems.at[n]
            )
            away.start()
            outs.append(away)
            n += 1
    for copy in outs:
        copy.wait()


def pack(inter, vec, hop, pot, stk):
    fields, rows, width = vec.shape
    chunks = width // LANES
    any_ = pl.BlockSpec(memory_space=pl.ANY)
    message = jax.ShapeDtypeStruct((chunks, MESSAGE, LANES), F32)
    n_in = 2 * (chunks + 3) + 1
    return pl.pallas_call(
        functools.partial(pack_kernel, rows, chunks),
        out_shape=[message, message, jax.ShapeDtypeStruct((2, chunks, EXTRA, LANES), F32)],
        in_specs=[any_, any_, any_, any_, any_],
        out_specs=[any_, any_, any_],
        scratch_shapes=[
            pltpu.SMEM(inter.shape, F32),
            pltpu.VMEM((2, chunks, fields, SUB, LANES), F32),
            pltpu.VMEM((2, 6, SUB, width), F32),
            pltpu.VMEM((2, 4, SUB, width), F32),
            pltpu.VMEM((2, SUB, width), jnp.int32),
            pltpu.VMEM((2, chunks, 4 * REC, LANES), F32),
            pltpu.SemaphoreType.DMA((n_in + 8,)),
        ],
        compiler_params=pltpu.CompilerParams(vmem_limit_bytes=VMEM_WIDE),
        cost_estimate=pl.CostEstimate(flops=1_000_000, bytes_accessed=4_000_000, transcendentals=0),
        name="pack",
    )(inter, vec, hop, pot, stk)


PAD = 8


def interior_kernel(rows, chunks, nvec, group, table, vec, hop, pot, stk, after, keep, send, tot,
                    inter, hop_raw, pot_raw, x, t1, t2, hp, pt, st, ww, mom, dots, ends,
                    sems):
    del after
    halves = nvec // group
    copies = [pltpu.make_async_copy(table, inter, sems.at[0])]
    n = 1
    for src, dst in ((hop, hop_raw), (pot, pot_raw), (stk, st)):
        copies.append(pltpu.make_async_copy(src, dst, sems.at[n]))
        n += 1
    late = []
    for q in range(halves):
        part = []
        for c in range(chunks):
            lanes = pl.ds(c * LANES, LANES)
            part.append(
                pltpu.make_async_copy(
                    vec.at[:, pl.ds(q * group, group), :, lanes],
                    x.at[:, pl.ds(q * group, group), c, pl.ds(PAD, rows)],
                    sems.at[n],
                )
            )
            n += 1
        late.append(part)
    for copy in copies + [copy for part in late for copy in part]:
        copy.start()
    for copy in copies:
        copy.wait()

    groups = rows // SUB

    def prepare(g, carry):
        at = pl.ds(pl.multiple_of(g * SUB, SUB), SUB)
        lanes = [pl.ds(c * LANES, LANES) for c in range(chunks)]
        for layer in range(2):
            rolled = [roll_left(hop_raw[layer, 1, at, lanes[c]]) for c in range(chunks)]
            for c in range(chunks):
                hp[layer, 3, c, at, :] = (
                    from_right(rolled[c], rolled[(c + 1) % chunks]) * -0.25
                )
            for k in range(3):
                for c in range(chunks):
                    hp[layer, k, c, at, :] = hop_raw[layer, k, at, lanes[c]] * -0.25
        for c in range(chunks):
            for s in range(4):
                pt[s, c, at, :] = pot_raw[s, at, lanes[c]] * 0.25
            classes = st[at, lanes[c]]
            for w in range(2):
                table = [inter[w, k] * 0.25 for k in range(inter.shape[1])]
                ww[w, c, at, :] = pick(classes, table)
        return carry

    lax.fori_loop(0, groups, prepare, 0)

    def sweep(order, q, source, before, target):
        def load(ref, s, v, c, at):
            return ref[s, v, c, at, :]

        def body(g, carry):
            base = pl.multiple_of(g * SUB, SUB)
            mid = pl.ds(base + PAD, SUB)
            up = pl.ds(base + PAD - 1, SUB)
            down = pl.ds(base + PAD + 1, SUB)
            plain = pl.ds(base, SUB)
            plain_down = pl.ds(base + 1, SUB)
            vs = range(group)
            src, off = source

            def rolled(site, c, fn):
                return [fn(load(src, site, v + off, c, mid)) for v in vs]

            products = [None] * 2
            b_prev = [rolled(2 * l + 1, chunks - 1, roll_right) for l in range(2)]
            a_here = [rolled(2 * l, 0, roll_left) for l in range(2)]
            for c in range(chunks):
                nxt = (c + 1) % chunks
                a_next = [rolled(2 * l, nxt, roll_left) for l in range(2)]
                b_here = [rolled(2 * l + 1, c, roll_right) for l in range(2)]
                coef = []
                for layer in range(2):
                    for k in range(4):
                        coef.append(hp[layer, k, c, plain, :])
                for s in range(4):
                    coef.append(pt[s, c, plain, :])
                for w in range(2):
                    coef.append(ww[w, c, plain, :])
                t2_down = [hp[layer, 2, c, plain_down, :] for layer in range(2)]
                sums = [None] * 4
                squares = [None] * 4
                for v in vs:
                    a = [load(src, 2 * l, v + off, c, mid) for l in range(2)]
                    b = [load(src, 2 * l + 1, v + off, c, mid) for l in range(2)]
                    a_down = [load(src, 2 * l, v + off, c, down) for l in range(2)]
                    b_up = [load(src, 2 * l + 1, v + off, c, up) for l in range(2)]
                    a_right = [from_right(a_here[l][v], a_next[l][v]) for l in range(2)]
                    b_left = [from_left(b_here[l][v], b_prev[l][v]) for l in range(2)]
                    new = hop_apply(a, b, a_right, b_left, a_down, b_up, coef, t2_down)
                    for s in range(4):
                        if order == 1:
                            value = new[s] * 0.5
                        elif order == CHEB:
                            value = new[s]
                        else:
                            ref, shift = before
                            value = new[s] - load(ref, s, v + shift, c, mid)
                        if target is not None:
                            target[s, v, c, mid, :] = value
                        first = load(x, s, v + q * group, c, mid)
                        term = first * value
                        sums[s] = term if sums[s] is None else sums[s] + term
                        if order == 2:
                            prior = load(src, s, v + off, c, mid)
                            for k, pair in enumerate((prior * value, value * value)):
                                products[k] = pair if products[k] is None else products[k] + pair
                        if order == 1:
                            sq = first * first
                            squares[s] = sq if squares[s] is None else squares[s] + sq
                for s in range(4):
                    if q > 0:
                        sums[s] = sums[s] + mom[order, s, c, plain, :]
                    if order == CHEB and q == halves - 1:
                        sums[s] = sums[s] - mom[order - 2, s, c, plain, :]
                    mom[order, s, c, plain, :] = sums[s]
                    if order == 1:
                        if q > 0:
                            squares[s] = squares[s] + mom[0, s, c, plain, :]
                        mom[0, s, c, plain, :] = squares[s]
                a_here = a_next
                b_prev = b_here
            if order == 2:
                row = lax.broadcasted_iota(jnp.int32, (SUB, LANES), 0) + base
                inside = (row >= 2) & (row < rows - 2)
                for k in range(2):
                    dots[k] = dots[k] + jnp.where(inside, products[k], 0.0)
            return carry

        lax.fori_loop(0, groups, body, 0, unroll=4)

    half = rows // 2
    core = place()[1]
    keep_at = pl.ds(pl.multiple_of(core * half, SUB), half)
    send_at = pl.ds(pl.multiple_of((1 - core) * half, SUB), half)
    outs = []

    def write_out(order):
        for rows_at, dst, k in ((keep_at, keep, 0), (send_at, send, 1)):
            copy = pltpu.make_async_copy(
                mom.at[order, :, :, rows_at], dst.at[order], sems.at[n + 2 * order + k]
            )
            copy.start()
            outs.append(copy)

    dots[...] = jnp.zeros_like(dots)
    for q in range(halves):
        for copy in late[q]:
            copy.wait()
        start = (x, q * group)
        steps = ((start, None, t1), ((t1, 0), start, t2), ((t2, 0), (t1, 0), t1), ((t1, 0), (t2, 0), None))
        for order, (source, before, target) in enumerate(steps, 1):
            sweep(order, q, source, before, target)
            if q == halves - 1:
                if order == 1:
                    write_out(0)
                write_out(order)

    def add_up(g, carry):
        base = pl.multiple_of(g * SUB, SUB)
        row = lax.broadcasted_iota(jnp.int32, (SUB, LANES), 0) + base
        inside = (row >= 2) & (row < rows - 2)
        result = []
        for m in range(3):
            acc = None
            for s in range(4):
                for c in range(chunks):
                    value = mom[m, s, c, pl.ds(base, SUB), :]
                    acc = value if acc is None else acc + value
            result.append(carry[m] + jnp.where(inside, acc, 0.0))
        return tuple(result)

    sums = lax.fori_loop(0, groups, add_up, tuple(jnp.zeros((SUB, LANES), F32) for _ in range(3)))
    for m in range(3):
        ends[m] = sums[m]
    for k in range(2):
        ends[3 + k] = dots[k]
    last = pltpu.make_async_copy(ends, tot, sems.at[n + 2 * (CHEB + 1)])
    last.start()
    outs.append(last)
    for copy in outs:
        copy.wait()


def interior(inter, vec, hop, pot, stk, after):
    _, nvec, rows, width = vec.shape
    chunks = width // LANES
    group = 2
    any_ = pl.BlockSpec(memory_space=pl.ANY)
    half = jax.ShapeDtypeStruct((CHEB + 1, 4, chunks, rows // 2, LANES), F32)
    n = 5 + chunks * (nvec // group) + 2 * (CHEB + 1)
    return pl.pallas_call(
        functools.partial(interior_kernel, rows, chunks, nvec, group),
        out_shape=[half, half, jax.ShapeDtypeStruct((CHEB + 1, SUB, LANES), F32)],
        in_specs=[any_] * 6,
        out_specs=[any_, any_, any_],
        scratch_shapes=[
            pltpu.SMEM(inter.shape, F32),
            pltpu.VMEM(hop.shape, F32),
            pltpu.VMEM(pot.shape, F32),
            pltpu.VMEM((4, nvec, chunks, rows + 2 * PAD, LANES), F32),
            pltpu.VMEM((4, group, chunks, rows + 2 * PAD, LANES), F32),
            pltpu.VMEM((4, group, chunks, rows + 2 * PAD, LANES), F32),
            pltpu.VMEM((2, 4, chunks, rows + SUB, LANES), F32),
            pltpu.VMEM((4, chunks, rows, LANES), F32),
            pltpu.VMEM((rows, width), jnp.int32),
            pltpu.VMEM((2, chunks, rows, LANES), F32),
            pltpu.VMEM((CHEB + 1, 4, chunks, rows, LANES), F32),
            pltpu.VMEM((2, SUB, LANES), F32),
            pltpu.VMEM((CHEB + 1, SUB, LANES), F32),
            pltpu.SemaphoreType.DMA((n,)),
        ],
        compiler_params=pltpu.CompilerParams(vmem_limit_bytes=VMEM_WIDE),
        cost_estimate=pl.CostEstimate(
            flops=60_000_000, bytes_accessed=9_000_000, transcendentals=0
        ),
        name="interior",
    )(inter, vec, hop, pot, stk, after)


WIN = 7
GUARD = REC


def gather_window(refs, w, sems, part=None, dots=None, share=None, filling=None, beside=()):
    own_long, own_short, got_long, got_short, extra = refs
    odd = place()[0]
    even = odd == 0
    copies = []

    def both(first, second, band, src_at, dst_at):
        dst, sem = w.at[band, :, dst_at], sems.at[len(copies)]

        @pl.when(even)
        def _():
            pltpu.make_async_copy(first.at[:, src_at], dst, sem).start()

        @pl.when(jnp.logical_not(even))
        def _():
            pltpu.make_async_copy(second.at[:, src_at], dst, sem).start()

        copies.append(pltpu.make_async_copy(first.at[:, src_at], dst, sem))

    def at(record, size):
        return pl.ds(GUARD + record * REC, size)

    few = part is not None
    if few:
        both(got_long, got_short, 0, pl.ds(REC, REC), at(2, REC))
        both(got_short, got_long, 1, pl.ds(0, REC), at(4, REC))
    else:
        both(got_long, got_short, 0, pl.ds(0, NEAR), at(1, NEAR))
        both(got_short, got_long, 1, pl.ds(0, NEAR), at(4, NEAR))
        both(got_long, got_short, 0, pl.ds(NEAR, FAR), at(0, FAR))
        both(got_short, got_long, 1, pl.ds(NEAR, FAR), at(6, FAR))
    both(own_long, own_short, 0, pl.ds(0, NEAR), at(3, NEAR))
    both(own_short, own_long, 1, pl.ds(0, NEAR), at(2, NEAR))
    both(own_long, own_short, 0, pl.ds(NEAR, FAR), at(5, FAR))
    both(own_short, own_long, 1, pl.ds(NEAR, FAR), at(1, FAR))
    plain = [
        (extra.at[0, :, pl.ds(REC, REC - FAR)], w.at[0, :, pl.ds(GUARD + 5 * REC + FAR, REC - FAR)]),
        (extra.at[1, :, pl.ds(REC, REC - FAR)], w.at[1, :, pl.ds(GUARD + REC + FAR, REC - FAR)]),
    ]
    if few:
        plain.extend(((part, dots), (share, filling)))
    else:
        plain.append((extra.at[0, :, pl.ds(0, REC)], w.at[0, :, at(6, REC)]))
        plain.append((extra.at[1, :, pl.ds(0, REC)], w.at[1, :, at(0, REC)]))
    for src, dst in plain:
        copy = pltpu.make_async_copy(src, dst, sems.at[len(copies)])
        copy.start()
        copies.append(copy)
    for copy in copies:
        copy.wait()
    for copy in beside:
        copy.start()
    if not few:
        for band, r, slot, to, to_slot in ((0, 1, 14, 0, 8), (0, 2, 14, 0, 12), (1, 4, 14, 6, 10)):
            for c in range(w.shape[1]):
                w[band, c, pl.ds(GUARD + to * REC + COEF + to_slot, 2), :] = w[
                    band, c, pl.ds(GUARD + r * REC + COEF + slot, 2), :
                ]


def window_slice(ref, is_w, band, c, i, site):
    start = GUARD + i * REC + site * SUB if is_w else (i + 1) * 32 + site * SUB
    return ref[band, c, pl.ds(pl.multiple_of(start, SUB), SUB), :]


def window_step(chunks, order, w, source, before, band, i, emit, sites="AB"):
    from_w = order == 1

    def here(site, c, shift=0):
        return window_slice(source, from_w, band, c, i + shift, site)

    def coef_at(k, c, shift=0):
        at = GUARD + (i + shift) * REC + COEF + SLOT[k]
        return jnp.broadcast_to(w[band, c, pl.ds(at, 1), :], (SUB, LANES))

    b_prev = [roll_right(here(2 * l + 1, chunks - 1)) for l in range(2)]
    a_here = [roll_left(here(2 * l, 0)) for l in range(2)]
    for c in range(chunks):
        nxt = (c + 1) % chunks
        a_next = [roll_left(here(2 * l, nxt)) for l in range(2)]
        b_here = [roll_right(here(2 * l + 1, c)) for l in range(2)]
        coef = [coef_at(k, c) for k in range(14)]
        t2_down = [coef_at(4 * l + 2, c, 1) for l in range(2)]
        a = [here(2 * l, c) for l in range(2)]
        b = [here(2 * l + 1, c) for l in range(2)]
        a_down = [here(2 * l, c, 1) for l in range(2)]
        b_up = [here(2 * l + 1, c, -1) for l in range(2)]
        a_right = [from_right(a_here[l], a_next[l]) for l in range(2)]
        b_left = [from_left(b_here[l], b_prev[l]) for l in range(2)]
        new = hop_apply(a, b, a_right, b_left, a_down, b_up, coef, t2_down, sites)
        for s in range(4):
            if new[s] is None:
                continue
            if order == 1:
                new[s] = new[s] * 0.5
            else:
                new[s] = new[s] - window_slice(before, order == 2, band, c, i, s)
        emit(c, new)
        a_here = a_next
        b_prev = b_here


def store_row(target, band, i):
    def emit(c, values):
        for s in range(4):
            at = pl.multiple_of((i + 1) * 32 + s * SUB, SUB)
            if values[s] is not None:
                target[band, c, pl.ds(at, SUB), :] = values[s]

    return emit


def totals_kernel(chunks, parts, own_long, own_short, got_long, got_short, extra, part, share, tot,
                  w, t1, dots, filling, sems):
    records = (own_long, own_short, got_long, got_short, extra)
    gather_window(records, w, sems, part, dots, share, filling)

    def first(j, carry):
        for band in range(2):
            i = 2 - band + j
            window_step(chunks, 1, w, w, None, band, i, store_row(t1, band, i))
        return carry

    lax.fori_loop(0, 4, first, 0, unroll=2)

    def second(j, carry):
        for band in range(2):
            i = 3 - band + j
            sums = [None] * 5

            def emit(c, values):
                for s in range(4):
                    zero = window_slice(w, True, band, c, i, s)
                    one = window_slice(t1, False, band, c, i, s)
                    two = values[s]
                    terms = (zero * zero, zero * one, zero * two, one * two, two * two)
                    for k, term in enumerate(terms):
                        sums[k] = term if sums[k] is None else sums[k] + term

            window_step(chunks, 2, w, t1, w, band, i, emit)
            for k in range(5):
                dots[k] = dots[k] + sums[k]
        return carry

    lax.fori_loop(0, 2, second, 0, unroll=2)
    lane = lax.broadcasted_iota(jnp.int32, (SUB, LANES), 1)
    row = jnp.zeros((SUB, LANES), F32)
    for m in range(5):
        row = jnp.where(lane == m, jnp.sum(dots[m]), row)
    row = jnp.where(lane == 5, filling[0], row)
    for k in range(parts // SUB):
        tot[pl.ds(k * SUB, SUB), :] = row


def totals_of(records, part, filling, parts):
    chunks = records[0].shape[0]
    any_ = pl.BlockSpec(memory_space=pl.ANY)
    vmem = pl.BlockSpec(memory_space=pltpu.VMEM)
    return pl.pallas_call(
        functools.partial(totals_kernel, chunks, parts),
        out_shape=jax.ShapeDtypeStruct((parts, LANES), F32),
        in_specs=[any_] * 7,
        out_specs=vmem,
        scratch_shapes=[
            pltpu.VMEM((2, chunks, (WIN + 2) * REC, LANES), F32),
            pltpu.VMEM((2, chunks, (WIN + 2) * 32, LANES), F32),
            pltpu.VMEM((5, SUB, LANES), F32),
            pltpu.SMEM((1,), F32),
            pltpu.SemaphoreType.DMA((10,)),
        ],
        compiler_params=pltpu.CompilerParams(vmem_limit_bytes=VMEM_WIDE),
        cost_estimate=pl.CostEstimate(flops=8_000_000, bytes_accessed=4_000_000, transcendentals=0),
        name="totals",
    )(*records, part, filling)


def edges_kernel(chunks, half, own_long, own_short, got_long, got_short, extra, mine_in, other_in,
                 after, out, w, t1, t2, res, mine, other, slab, sems):
    del after
    inner = [
        pltpu.make_async_copy(src, dst, sems.at[12 + k])
        for k, (src, dst) in enumerate(((mine_in, mine), (other_in, other)))
    ]
    gather_window((own_long, own_short, got_long, got_short, extra), w, sems, beside=inner)
    row = lax.broadcasted_iota(jnp.int32, (SUB, LANES), 0)
    single, double = (row & 1) != 0, (row & 2) != 0

    def merged(hit, a, b, shift):
        return jnp.where(hit, b, a) + pltpu.roll(jnp.where(hit, a, b), shift, 0)

    def moments(band, i, c, order, values):
        p = [window_slice(w, True, band, c, i, s) * values[s] for s in range(4)]
        pairs = [merged(single, p[2 * k], p[2 * k + 1], 1) for k in range(2)]
        both = merged(double, pairs[0], pairs[1], 2)
        both = both + pltpu.roll(both, 4, 0)
        res[band, i - 2, c, pl.ds(order * 4, 4), :] = both[0:4]

    def sweep(order, first, last):
        source, before, target = {
            1: (w, None, t1),
            2: (t1, w, t2),
            3: (t2, t1, t1),
            4: (t1, t2, None),
        }[order]

        def step(i, sites):
            for band in range(2):
                if order < CHEB:
                    emit = store_row(target, band, i)
                else:
                    emit = lambda c, values, band=band: moments(band, i, c, CHEB, values)
                window_step(chunks, order, w, source, before, band, i, emit, sites)

        def body(j, carry):
            step(first + j, "AB")
            return carry

        if order in (1, 3):
            step(first - 1, "B")
            step(last + 1, "A")
        lax.fori_loop(0, last - first + 1, body, 0, unroll=1 if order == CHEB else 2)

    def collect(order, ref):
        def body(j, carry):
            i = 2 + j
            for band in range(2):
                for c in range(chunks):
                    values = [window_slice(ref, ref is w, band, c, i, s) for s in range(4)]
                    moments(band, i, c, order, values)
            return carry

        lax.fori_loop(0, 3, body, 0)

    collect(0, w)
    sweep(1, 1, 5)
    collect(1, t1)
    sweep(2, 1, 5)
    collect(2, t2)
    sweep(3, 2, 4)
    collect(3, t1)
    sweep(4, 2, 4)
    for copy in inner:
        copy.wait()
    tall = 4 * half + SUB
    core = place()[1]

    outs = []
    for m in range(CHEB + 1):
        for c in range(chunks):
            upper = [res[0, r + 1, c, pl.ds(4 * m, 4), :] for r in range(2)]
            lower = [res[1, r, c, pl.ds(4 * m, 4), :] for r in range(2)]
            own = [jnp.where(core == 0, upper[r], lower[r]) for r in range(2)]
            rest = [jnp.where(core == 0, lower[r], upper[r]) for r in range(2)]
            places = [jnp.where(core == 0, r, half - 2 + r) for r in range(2)]
            for s in range(4):
                for g in range(half // SUB):
                    at = pl.ds(g * SUB, SUB)
                    value = mine[m, s, c, at, :] + other[m, s, c, at, :]
                    for r in range(2):
                        hit = row + g * SUB == places[r]
                        value = jnp.where(hit, own[r][s : s + 1], value)
                    slab[m, pl.ds(c * tall + s * half + g * SUB, SUB), :] = value
            for r in range(2):
                slab[m, pl.ds(c * tall + 4 * half + 4 * r, 4), :] = rest[r]
            for band, r in ((0, 0), (1, 2)):
                halo = res[band, r, c, pl.ds(4 * m, 4), :]
                slab[m, pl.ds(chunks * tall + band * SUB + c, 1), :] = jnp.sum(
                    halo, axis=0, keepdims=True
                )
        away = pltpu.make_async_copy(slab.at[m], out.at[m], sems.at[m])
        away.start()
        outs.append(away)
    for copy in outs:
        copy.wait()


def edges(records, mine, other, after):
    _, _, chunks, half, _ = mine.shape
    slabs = (CHEB + 1, chunks * (4 * half + SUB) + 2 * SUB, LANES)
    any_ = pl.BlockSpec(memory_space=pl.ANY)
    return pl.pallas_call(
        functools.partial(edges_kernel, chunks, half),
        out_shape=jax.ShapeDtypeStruct(slabs, F32),
        in_specs=[any_] * 8,
        out_specs=any_,
        scratch_shapes=[
            pltpu.VMEM((2, chunks, (WIN + 2) * REC, LANES), F32),
            pltpu.VMEM((2, chunks, (WIN + 2) * 32, LANES), F32),
            pltpu.VMEM((2, chunks, (WIN + 2) * 32, LANES), F32),
            pltpu.VMEM((2, 3, chunks, 24, LANES), F32),
            pltpu.VMEM(mine.shape, F32),
            pltpu.VMEM(mine.shape, F32),
            pltpu.VMEM(slabs, F32),
            pltpu.SemaphoreType.DMA((14,)),
        ],
        compiler_params=pltpu.CompilerParams(vmem_limit_bytes=VMEM_WIDE),
        cost_estimate=pl.CostEstimate(
            flops=20_000_000, bytes_accessed=4_000_000, transcendentals=0
        ),
        name="edges",
    )(*records, mine, other, after)


ACOS = (
    1.5707963050,
    -0.2145988016,
    0.0889789874,
    -0.0501743046,
    0.0308918810,
    -0.0170881256,
    0.0066700901,
    -0.0012624911,
)


def arccos(e):
    size = jnp.abs(e)
    poly = jnp.full_like(size, ACOS[-1])
    for value in ACOS[-2::-1]:
        poly = poly * size + value
    angle = jnp.sqrt(1.0 - size) * poly
    return jnp.where(e < 0.0, math.pi - angle, angle)


def weights_of(e):
    gain = jackson(CHEB + 1)
    sine = jnp.sqrt((1.0 - e) * (1.0 + e))
    square = e * e
    sines = [sine, 2.0 * e * sine, (4.0 * square - 1.0) * sine, 4.0 * e * (2.0 * square - 1.0) * sine]
    out = [gain[0] * (1.0 - arccos(e) / math.pi)]
    for m in range(1, CHEB + 1):
        out.append(sines[m - 1] * (-2.0 * gain[m] / (math.pi * m)))
    return out


def density_kernel(scale, sites, sums, slabs, out):
    added = jnp.sum(sums[...], axis=0, keepdims=True) * scale
    lane = lax.broadcasted_iota(jnp.int32, (1, LANES), 1)
    totals = [jnp.sum(jnp.where(lane == m, added, 0.0)) for m in range(CHEB + 1)]
    totals[3] = 2.0 * totals[3] - totals[1]
    totals[4] = 2.0 * totals[4] - totals[0]
    target = jnp.sum(jnp.where(lane == 5, sums[0:1, :], 0.0)) * sites

    point = (
        lax.broadcasted_iota(jnp.int32, (SUB, LANES), 0) * LANES
        + lax.broadcasted_iota(jnp.int32, (SUB, LANES), 1)
        + 1
    )
    ways = 2 ** (BISECT // 2)
    valid = point < ways
    low = jnp.float32(-1.0)
    step = 2.0
    for _ in range(2):
        step = step / ways
        mids = jnp.where(valid, low + point.astype(F32) * step, 0.0)
        count = None
        for value, total in zip(weights_of(mids), totals):
            term = value * total
            count = term if count is None else count + term
        below = jnp.sum(jnp.where(valid & (count < target), 1.0, 0.0))
        low = low + below * step
    chem = jnp.full((SUB, LANES), low + 0.5 * step, F32)
    weights = weights_of(chem)
    for k in range(out.shape[0] // SUB):
        at = pl.ds(k * SUB, SUB)
        acc = None
        for m in range(CHEB + 1):
            term = weights[m] * slabs[m, at, :]
            acc = term if acc is None else acc + term
        out[at, :] = acc


def density(sums, slabs, vectors, sites):
    vmem = pl.BlockSpec(memory_space=pltpu.VMEM)
    return pl.pallas_call(
        functools.partial(density_kernel, 1.0 / vectors, float(sites)),
        out_shape=jax.ShapeDtypeStruct(slabs.shape[1:], F32),
        in_specs=[vmem, vmem],
        out_specs=vmem,
        compiler_params=pltpu.CompilerParams(vmem_limit_bytes=VMEM_LIMIT),
        cost_estimate=pl.CostEstimate(flops=2_000_000, bytes_accessed=4_000_000, transcendentals=0),
        name="density",
    )(sums, slabs)


def potential_kernel(chunks, half, mine, other, out, dens, charge):
    first = place()[1] == 0
    tall = 4 * half + SUB
    guard = SUB

    for c in range(chunks):
        for s in range(4):
            at = pl.ds(c * tall + s * half, half)
            m, o = mine[at, :], other[at, :]
            dens[s, c, pl.ds(0, half), :] = jnp.where(first, m, o)
            dens[s, c, pl.ds(half, half), :] = jnp.where(first, o, m)
        at = pl.ds(c * tall + 4 * half, SUB)
        m, o = mine[at, :], other[at, :]
        upper, lower = jnp.where(first, o, m), jnp.where(first, m, o)
        for r in range(2):
            for s in range(4):
                k = 4 * r + s
                for row, more in ((r, upper), (2 * half - 2 + r, lower)):
                    dens[s, c, pl.ds(row, 1), :] = dens[s, c, pl.ds(row, 1), :] + more[k : k + 1]
        for g in range(2 * half // SUB):
            at = pl.ds(g * SUB, SUB)
            total = (dens[0, c, at, :] + dens[1, c, at, :]) + (dens[2, c, at, :] + dens[3, c, at, :])
            charge[c, pl.ds(guard + g * SUB, SUB), :] = total - 2.0
        for band, row in ((0, guard - 1), (1, guard + 2 * half)):
            at = pl.ds(chunks * tall + band * SUB + c, 1)
            charge[c, pl.ds(row, 1), :] = mine[at, :] + other[at, :] - 2.0
    for g in range(2 * half // SUB):
        at = pl.ds(guard + g * SUB, SUB)
        for c in range(chunks):
            here = charge[c, at, :]
            left = from_left(roll_right(here), roll_right(charge[(c - 1) % chunks, at, :]))
            right = from_right(roll_left(here), roll_left(charge[(c + 1) % chunks, at, :]))
            near = (
                charge[c, pl.ds(guard + g * SUB - 1, SUB), :]
                + charge[c, pl.ds(guard + g * SUB + 1, SUB), :]
                + left
                + right
            )
            base = 0.5 * here + 0.25 * near
            for s in range(4):
                value = dens[s, c, pl.ds(g * SUB, SUB), :]
                out[s, pl.ds(g * SUB, SUB), pl.ds(c * LANES, LANES)] = 3.0 * (value - 0.5) + base


def new_potential(mine, other, chunks):
    half = ((mine.shape[0] - 2 * SUB) // chunks - SUB) // 4
    vmem = pl.BlockSpec(memory_space=pltpu.VMEM)
    return pl.pallas_call(
        functools.partial(potential_kernel, chunks, half),
        out_shape=jax.ShapeDtypeStruct((4, 2 * half, chunks * LANES), F32),
        in_specs=[vmem, vmem],
        out_specs=vmem,
        scratch_shapes=[
            pltpu.VMEM((4, chunks, 2 * half, LANES), F32),
            pltpu.VMEM((chunks, 2 * half + 2 * SUB, LANES), F32),
        ],
        compiler_params=pltpu.CompilerParams(vmem_limit_bytes=VMEM_LIMIT),
        cost_estimate=pl.CostEstimate(flops=1_000_000, bytes_accessed=2_000_000, transcendentals=0),
        name="new_potential",
    )(mine, other)


def per_device(vectors, hoppings, potential, stacking, interlayer, filling):
    strips, ranks = lax.axis_size("dom"), lax.axis_size("vec")
    _, nvec, rows, width = vectors.shape
    long_way = [(i, (i - 1 if i % 2 == 0 else i + 1) % strips) for i in range(strips)]
    short_way = [(i, i ^ 1) for i in range(strips)]
    sibling = [(i, i ^ 1) for i in range(ranks)]
    across = [(i, i ^ 2) for i in range(ranks)]

    own_long, own_short, extra = pack(
        interlayer,
        vectors.reshape(4 * nvec, rows, width),
        hoppings.reshape(6, rows, width),
        potential,
        stacking,
    )
    got_long = lax.ppermute(own_long, "dom", long_way)
    got_short = lax.ppermute(own_short, "dom", short_way)
    mine, yours, part = interior(interlayer, vectors, hoppings, potential, stacking, own_long)
    records = (own_long, own_short, got_long, got_short, extra)
    totals = totals_of(records, part, filling, strips * ranks)
    yours, ready = lax.optimization_barrier((yours, totals))
    other = lax.ppermute(yours, "vec", sibling)
    slabs = edges(records, mine, other, totals) * (1.0 / (nvec * ranks))
    sums = lax.all_to_all(ready, ("dom", "vec"), 0, 0, tiled=True)
    sites = 4 * rows * width * strips
    chip = density(sums, slabs, nvec * ranks, sites)
    whole = chip + lax.ppermute(chip, "vec", across)
    return new_potential(whole, lax.ppermute(whole, "vec", sibling), width // LANES)


def solution(mesh):
    placed = (
        P(None, "vec", "dom", None),
        P(None, None, "dom", None),
        P(None, "dom", None),
        P("dom", None),
        P(),
        P(),
    )
    return jax.shard_map(
        per_device, mesh=mesh, in_specs=placed, out_specs=P(None, "dom", None), check_vma=False
    )
```
